256 devices in a mesh: row: 32 (over x, z), head: 8 (over y, core).
Axes of the slice: x: 4, y: 4, z: 8, core: 2. Of those that a mesh axis runs over, the one named last changes fastest.
Arguments:
- q_nope: bfloat16 [4, 64, 128, 128], P(None, 'row', 'head'), may hold values from -9 to 9
- q_rope: bfloat16 [4, 64, 8192], P(None, 'row', 'head'), may hold values from -18 to 18
- new_latent: bfloat16 [4, 64, 512], P(None, 'row'), may hold values from -6 to 6
- new_rope: bfloat16 [4, 64, 64], P(None, 'row'), may hold values from -6 to 6
- latent_pages: bfloat16 [2560, 64, 512], P('row'), may hold values from -6 to 6
- rope_pages: bfloat16 [2560, 4096], P('row'), may hold values from -6 to 6
- dest_rows: int32 [2560], P('row'), may hold values from 0 to 63, as said below
- dest_slots: int32 [2560], P('row'), may hold values from 0 to 39
- page_table: int32 [64, 40], P('row'), may hold values from 0 to 39, each once within a row
- lengths: int32 [64], P('row'), may hold values from 1 to 2560, as said below
- w_uk: bfloat16 [128, 128, 512], P('head'), may hold values from -0.5 to 0.5
- w_uv: bfloat16 [128, 512, 128], P('head'), may hold values from -1 to 1
- w_o: bfloat16 [16384, 7168], P('head', 'row'), may hold values from -0.046875 to 0.046875
Outputs:
- mixed_out: bfloat16 [4, 64, 7168], P(None, 'row', 'head')
The draws below stay inside these ranges and needn't reach their ends.
Inputs may be any that keep to these rules, and one draw needn't show every extreme that they name: `dest_rows`: together with dest_slots, each page of a device is named a row and a page slot of that row; every slot of every row is named exactly once over all pages. From the pages of one index of row at most 5 go to the rows of any one index of row, exactly 5 for some pairs; every index of row receives 80 pages. `page_table`: each row of the table is a permutation of the slots. `lengths`: some row holds 2560 tokens.
All inputs are finite; a program needn't handle non-finite values.
Results may differ from the reference program's by a relative error of at most 0.008.
Values may be sent and summed in bfloat16 or wider, within the bound.
No kernel may reach another device: no remote copies, remote signals or barrier semaphores. Data moves between devices by JAX's collectives and lax.ppermute only.
A program may use at most 128 MiB of HBM per device.

```python
import jax
import jax.numpy as jnp
from jax import lax

D = 7168
H = 128
LAT = 512
ROPE = 64
NOPE = 128
V = 128
PAGE = 64
STEPS = 4
ROWS_DEV = 2
PAGES_ROW = 40
ROWS = 64
PAGES_DEV = 80
PAGES_ALL = 2560
CTX = 2560
N_ROW = 32


def placement_lists(key):
    key = jax.random.fold_in(key, 500)
    key_pairs, key_sigma, key_dest, key_src, key_shuffle = jax.random.split(key, 5)
    base_count = PAGES_DEV // N_ROW
    remain = PAGES_DEV % N_ROW
    lifts = jax.random.randint(key_pairs, (N_ROW // 2,), 0, base_count + 1).at[0].set(base_count)
    index_ids = jnp.arange(N_ROW, dtype=jnp.int32)
    signs = jnp.where(index_ids % 2 == 0, 1, -1).astype(jnp.int32)
    weights = base_count + jnp.repeat(lifts, 2) * signs + (index_ids < remain).astype(jnp.int32)
    weights = weights[jax.random.permutation(key_shuffle, N_ROW)]
    sigma = jax.random.permutation(key_sigma, N_ROW)
    offsets = (sigma[None, :] - sigma[:, None]) % N_ROW
    counts = weights[offsets]
    ends = jnp.cumsum(counts, axis=1)
    page_ids = jnp.arange(PAGES_DEV, dtype=jnp.int32)
    target_dev = jnp.sum((ends[:, None, :] <= page_ids[None, :, None]).astype(jnp.int32), axis=2)
    starts = ends - counts
    rank = page_ids[None, :] - jnp.take_along_axis(starts, target_dev, axis=1)
    arrive_base = jnp.cumsum(counts, axis=0) - counts
    source_ids = jnp.broadcast_to(jnp.arange(N_ROW, dtype=jnp.int32)[:, None], (N_ROW, PAGES_DEV))
    arrive = arrive_base[source_ids, target_dev] + rank
    dest_perm = jax.vmap(lambda k: jax.random.permutation(k, PAGES_DEV))(jax.random.split(key_dest, N_ROW))
    local_pos = dest_perm[target_dev, arrive]
    row_ids = target_dev * ROWS_DEV + local_pos // PAGES_ROW
    slot_ids = local_pos % PAGES_ROW
    src_perm = jax.vmap(lambda k: jax.random.permutation(k, PAGES_DEV))(jax.random.split(key_src, N_ROW))
    rows_out = jnp.zeros((N_ROW, PAGES_DEV), jnp.int32).at[source_ids, src_perm].set(row_ids)
    slots_out = jnp.zeros((N_ROW, PAGES_DEV), jnp.int32).at[source_ids, src_perm].set(slot_ids)
    return (rows_out.reshape(PAGES_ALL), slots_out.reshape(PAGES_ALL))


def draw_dest_rows(key, part):
    return placement_lists(key)[0].astype(jnp.int32)


def draw_dest_slots(key, part):
    return placement_lists(key)[1].astype(jnp.int32)


def draw_lengths(key, part):
    key = jax.random.fold_in(key, 21)
    key_len, key_full = jax.random.split(key)
    spans = jax.random.randint(key_len, (ROWS,), 1, CTX + 1)
    chosen = jax.random.randint(key_full, (), 0, ROWS)
    return spans.at[chosen].set(CTX).astype(jnp.int32)


def draw_q_rope(key, part):
    key = jax.random.fold_in(key, 11)
    key_base = jax.random.fold_in(key, 0)
    values = jnp.clip(1.5 * jax.random.normal(key_base, (STEPS, ROWS, H, ROPE), jnp.float32), -9.0, 9.0)
    return values.reshape(STEPS, ROWS, H * ROPE).astype(jnp.bfloat16)


def draw_rope_pages(key, part):
    key = jax.random.fold_in(key, 12)
    key_base = jax.random.fold_in(key, 0)
    values = jnp.clip(jax.random.normal(key_base, (PAGES_ALL, PAGE, ROPE), jnp.float32), -6.0, 6.0)
    return values.reshape(PAGES_ALL, PAGE * ROPE).astype(jnp.bfloat16)


def shard_levels(rng, extent, cuts, least, top_value):
    factor_of = 1.0
    for dim, shards_of in cuts:
        heights = jax.random.uniform(jax.random.fold_in(jax.random.fold_in(rng, 6), dim), (shards_of,), jnp.float32, least / len(cuts), top_value / len(cuts))
        factor_of = factor_of * jnp.repeat(jnp.exp(heights), extent[dim] // shards_of).reshape((-1,) + (1,) * (len(extent) - 1 - dim))
    return factor_of


def scatter_about(stream_key, shape, width, most, shards=(), kind=jnp.bfloat16):
    entries = width * jax.random.normal(stream_key, shape, jnp.float32)
    if shards:
        entries = entries * shard_levels(stream_key, shape, shards, -0.22, 0.18)
    return jnp.clip(entries, -most, most).astype(kind)


def setup_inputs(seed: int = 0) -> dict:
    keys = jax.random.split(jax.random.key(seed), 14)
    return {
        "q_nope": scatter_about(keys[0], (STEPS, ROWS, H, NOPE), 1.5, 9.0, ((1, 32), (2, 8))),
        "q_rope": draw_q_rope(jax.random.fold_in(keys[13], 71), 0),
        "new_latent": scatter_about(keys[2], (STEPS, ROWS, LAT), 1.0, 6.0, ((1, 32),)),
        "new_rope": scatter_about(keys[3], (STEPS, ROWS, ROPE), 1.0, 6.0, ((1, 32),)),
        "latent_pages": scatter_about(keys[4], (PAGES_ALL, PAGE, LAT), 1.0, 6.0, ((0, 32),)),
        "rope_pages": draw_rope_pages(jax.random.fold_in(keys[13], 71), 0),
        "dest_rows": draw_dest_rows(jax.random.fold_in(keys[13], 71), 0),
        "dest_slots": draw_dest_slots(jax.random.fold_in(keys[13], 71), 0),
        "page_table": jax.vmap(lambda own: jax.random.permutation(own, PAGES_ROW))(jax.random.split(keys[8], ROWS)).reshape((ROWS, PAGES_ROW)).astype(jnp.int32),
        "lengths": draw_lengths(jax.random.fold_in(keys[13], 71), 0),
        "w_uk": scatter_about(keys[10], (H, NOPE, LAT), NOPE ** -0.5, 0.5, ((0, 8),)),
        "w_uv": scatter_about(keys[11], (H, LAT, V), (LAT // 16) ** -0.5, 1.0, ((0, 8),)),
        "w_o": scatter_about(keys[12], (H * V, D), (H * V) ** -0.5, 0.046875, ((0, 8), (1, 32))),
    }


def token_positions(page_table, page_len):
    pages_row = page_table.shape[1]
    slot_ids = jnp.arange(pages_row, dtype=jnp.int32)
    holds = (page_table[:, :, None] == slot_ids[None, None, :]).astype(jnp.int32)
    logical = jnp.sum(holds * slot_ids[None, :, None], axis=1)
    within = jnp.arange(page_len, dtype=jnp.int32)
    return (logical[:, :, None] * page_len + within[None, None, :]).reshape(page_table.shape[0], pages_row * page_len)


def attend(q_nope, q_rope, new_latent, new_rope, cache_lat, cache_rope, usable, w_uk, w_uv):
    step_count, row_count, heads, _ = q_nope.shape
    rope_w = new_rope.shape[-1]
    score_scale = 1.0 / (q_nope.shape[-1] + rope_w) ** 0.5
    absorbed = jnp.einsum('srhn,hnl->srhl', q_nope.astype(jnp.float32), w_uk.astype(jnp.float32)).astype(jnp.bfloat16)
    absorbed_f = absorbed.astype(jnp.float32)
    rope_q = q_rope.reshape(step_count, row_count, heads, rope_w).astype(jnp.float32)
    lat_f = cache_lat.astype(jnp.float32)
    new_lat_f = new_latent.astype(jnp.float32)
    cache_scores = (jnp.einsum('srhl,rkl->srhk', absorbed_f, lat_f) + jnp.einsum('srhe,rke->srhk', rope_q, cache_rope.astype(jnp.float32))) * score_scale
    cache_scores = jnp.where(usable[None, :, None, :], cache_scores, -1e30)
    fresh_scores = (jnp.einsum('srhl,url->srhu', absorbed_f, new_lat_f) + jnp.einsum('srhe,ure->srhu', rope_q, new_rope.astype(jnp.float32))) * score_scale
    step_ids = jnp.arange(step_count, dtype=jnp.int32)
    allowed = step_ids[None, :] <= step_ids[:, None]
    fresh_scores = jnp.where(allowed[:, None, None, :], fresh_scores, -1e30)
    highest = jnp.maximum(jnp.max(cache_scores, axis=-1), jnp.max(fresh_scores, axis=-1))
    cache_exp = jnp.exp(cache_scores - highest[..., None])
    fresh_exp = jnp.exp(fresh_scores - highest[..., None])
    denominator = jnp.sum(cache_exp, axis=-1) + jnp.sum(fresh_exp, axis=-1)
    cache_weights = (cache_exp / denominator[..., None]).astype(jnp.bfloat16).astype(jnp.float32)
    fresh_weights = (fresh_exp / denominator[..., None]).astype(jnp.bfloat16).astype(jnp.float32)
    latent_out = (jnp.einsum('srhk,rkl->srhl', cache_weights, lat_f) + jnp.einsum('srhu,url->srhl', fresh_weights, new_lat_f)).astype(jnp.bfloat16)
    head_out = jnp.einsum('srhl,hlv->srhv', latent_out.astype(jnp.float32), w_uv.astype(jnp.float32)).astype(jnp.bfloat16)
    return head_out.reshape(step_count, row_count, heads * w_uv.shape[-1])


def reference(q_nope, q_rope, new_latent, new_rope, latent_pages, rope_pages, dest_rows, dest_slots, page_table, lengths, w_uk, w_uv, w_o):
    target = (dest_rows * PAGES_ROW + dest_slots).astype(jnp.int32)
    cache_lat = jnp.zeros((ROWS * PAGES_ROW, PAGE, LAT), jnp.bfloat16).at[target].set(latent_pages)
    cache_lat = cache_lat.reshape(ROWS, PAGES_ROW * PAGE, LAT)
    cache_rope = jnp.zeros((ROWS * PAGES_ROW, PAGE * ROPE), jnp.bfloat16).at[target].set(rope_pages)
    cache_rope = cache_rope.reshape(ROWS, PAGES_ROW * PAGE, ROPE)
    usable = token_positions(page_table, PAGE) < lengths[:, None]

    def one_row(items):
        q_n, q_r, n_lat, n_rope, c_lat, c_rope, row_usable = items
        return attend(q_n[:, None], q_r[:, None], n_lat[:, None], n_rope[:, None], c_lat[None], c_rope[None], row_usable[None], w_uk, w_uv)[:, 0]

    head_out = lax.map(one_row, (jnp.transpose(q_nope, (1, 0, 2, 3)), jnp.transpose(q_rope, (1, 0, 2)), jnp.transpose(new_latent, (1, 0, 2)), jnp.transpose(new_rope, (1, 0, 2)), cache_lat, cache_rope, usable))
    head_out = jnp.transpose(head_out, (1, 0, 2)).reshape(STEPS * ROWS, H * V)
    mixed_out = jnp.dot(head_out, w_o, preferred_element_type=jnp.float32).astype(jnp.bfloat16)
    return mixed_out.reshape(STEPS, ROWS, D)
```

```python
import functools

import jax
import jax.numpy as jnp
from jax import lax
from jax.experimental import pallas as pl
from jax.experimental.pallas import tpu as pltpu
from jax.sharding import PartitionSpec as P

NX = 4
NZ = 8
TAIL = 128
INFO = 16
NEG = -1e30
LOG2E = 1.4426950408889634
LN2 = 0.6931471805599453

VMEM = pl.BlockSpec(memory_space=pltpu.VMEM)
SMEM = pl.BlockSpec(memory_space=pltpu.SMEM)


def call(body, out_shape, ins, scratch=(), flops=0, nbytes=0, mem=48, out_spec=VMEM):
    return pl.pallas_call(
        body,
        out_shape=out_shape,
        in_specs=[SMEM if a.dtype == jnp.int32 and a.ndim == 1 else VMEM for a in ins],
        out_specs=jax.tree.map(lambda _: out_spec, out_shape),
        scratch_shapes=list(scratch),
        compiler_params=pltpu.CompilerParams(vmem_limit_bytes=mem * 2**20),
        cost_estimate=pl.CostEstimate(flops=flops, bytes_accessed=nbytes, transcendentals=0),
    )(*ins)


def dot(a, b):
    return lax.dot_general(a, b, (((1,), (0,)), ((), ())), preferred_element_type=jnp.float32)


def dot_t(a, b):
    return lax.dot_general(a, b, (((1,), (1,)), ((), ())), preferred_element_type=jnp.float32)


def iota(shape, dim):
    return lax.broadcasted_iota(jnp.int32, shape, dim)


def pack_kernel(piece, per_pair, lat_ref, tail_ref, lane_ref, col_ref, out_ref, buf_ref, sem_ref):
    tokens, lat_w = lat_ref.shape
    pages = col_ref.shape[0]
    chunks, chunk, _ = buf_ref.shape
    dest = lane_ref[...]
    page_of = iota((1, tokens), 1) // piece
    same = (col_ref[...] == dest) & (iota((pages, tokens), 0) < page_of)
    rank = jnp.sum(same.astype(jnp.int32), axis=0, keepdims=True)
    place = (dest * per_pair + rank) * piece + iota((1, tokens), 1) % piece
    lat = lat_ref[...]
    tail = tail_ref[...]
    copies = []
    for i in range(chunks):
        pick = jnp.where(iota((chunk, tokens), 0) + i * chunk == place, 1.0, 0.0)
        pick = pick.astype(jnp.bfloat16)
        buf_ref[i, :, :lat_w] = dot(pick, lat).astype(jnp.bfloat16)
        buf_ref[i, :, lat_w:] = dot(pick, tail).astype(jnp.bfloat16)
        copy = pltpu.make_async_copy(
            buf_ref.at[i], out_ref.at[pl.ds(i * chunk, chunk)], sem_ref.at[i]
        )
        copy.start()
        copies.append(copy)
    for copy in copies:
        copy.wait()


def split3(x):
    hi = x.astype(jnp.bfloat16)
    rest = x - hi.astype(jnp.float32)
    mid = rest.astype(jnp.bfloat16)
    low = (rest - mid.astype(jnp.float32)).astype(jnp.bfloat16)
    return hi.astype(jnp.float32), mid.astype(jnp.float32), low.astype(jnp.float32)


def query_kernel(
    scale, rows, qn_ref, qtail_ref, w_ref, fresh_ref, fresh_t_ref, q_ref, part_ref, lse_ref, acc_ref
):
    heads, width, _ = qn_ref.shape
    lat_w = w_ref.shape[2]
    for head in range(heads):
        acc_ref[head * width : (head + 1) * width, :] = dot(qn_ref[head], w_ref[head])
    q_ref[:lat_w, :] = acc_ref[...].T.astype(jnp.bfloat16)
    q_ref[lat_w:, :] = qtail_ref[...].astype(jnp.float32).T.astype(jnp.bfloat16)
    scores = dot(fresh_ref[...], q_ref[...]) * scale
    shape = scores.shape
    token = iota(shape, 0)
    query = iota(shape, 1) % width
    allowed = (query % rows == token % rows) & (token // rows <= query // rows)
    scores = jnp.where(allowed, scores, NEG)
    high = jnp.max(scores, axis=0, keepdims=True)
    weights = jnp.exp(scores - high)
    total = jnp.sum(weights, axis=0, keepdims=True)
    part_ref[...] = dot(fresh_t_ref[...], weights.astype(jnp.bfloat16)) * (1.0 / total)
    lse_ref[...] = jnp.broadcast_to(high + jnp.log(total), lse_ref.shape)


def attend_kernel(scale, piece, rope_w, pages_row, place_ref, key_ref, limit_ref, *refs):
    q_refs, out_ref = refs[:-1], refs[-1]
    count = len(q_refs)
    tokens = key_ref.shape[0]
    lat_w = key_ref.shape[1] - TAIL
    tail = key_ref[:, lat_w:].astype(jnp.float32)
    lane = iota((tokens, TAIL), 1)
    label = jnp.sum(jnp.where(lane == rope_w, tail, 0.0), axis=1, keepdims=True).astype(jnp.int32)
    limit = jnp.sum(jnp.where(label == lane + 1, limit_ref[...], 0), axis=1, keepdims=True)
    usable = iota((tokens, 1), 0) % piece < limit
    second = label > pages_row
    first_bias = jnp.where(usable & ~second, 0.0, NEG)
    second_bias = jnp.where(usable & second, 0.0, NEG)
    tail = jnp.where(lane == rope_w, first_bias, tail)
    tail = jnp.where(lane == rope_w + 1, second_bias, tail)
    lat = key_ref[:, :lat_w]
    key = jnp.concatenate([lat, tail.astype(jnp.bfloat16)], axis=1)
    lat_t = lat.T
    head = place_ref[1]
    queries = q_refs[0].shape[1]
    for k in range(0, count, 2):
        query = jnp.concatenate([q_refs[k][...], q_refs[k + 1][...]], axis=1)
        scores = dot(key, query)
        high = jnp.max(scores, axis=0, keepdims=True)
        weights = jnp.exp2((scores - high) * (scale * LOG2E))
        total = jnp.sum(weights, axis=0, keepdims=True)
        part = dot(lat_t, weights.astype(jnp.bfloat16)) * (1.0 / total)
        part = part.astype(jnp.bfloat16)
        hi, mid, low = split3(high * scale + jnp.log(total))
        mark = iota((INFO, 2 * queries), 0)
        info = jnp.where(mark == 0, hi, jnp.where(mark == 1, mid, jnp.where(mark == 2, low, 0.0)))
        info = info.astype(jnp.bfloat16)
        for half in range(2):
            owner = (head - (k + half) + count) % count
            lanes = slice(half * queries, (half + 1) * queries)
            out_ref[owner, :lat_w, :] = part[:, lanes]
            out_ref[owner, lat_w:, :] = info[:, lanes]


def merge_kernel(width, fresh_ref, fresh_lse_ref, w_ref, part_ref, out_ref, lat_ref):
    heads, lat_w, value_w = w_ref.shape
    count = part_ref.shape[0]
    lses = [fresh_lse_ref[:1, :]]
    for k in range(count):
        info = part_ref[k, lat_w:, :].astype(jnp.float32)
        lses.append(jnp.sum(info, axis=0, keepdims=True))
    high = functools.reduce(jnp.maximum, lses)
    shares = [jnp.exp(lse - high) for lse in lses]
    inverse = 1.0 / functools.reduce(jnp.add, shares)
    total = fresh_ref[...] * (shares[0] * inverse)
    for k in range(count):
        total = total + part_ref[k, :lat_w, :].astype(jnp.float32) * (shares[k + 1] * inverse)
    lat_ref[...] = total.T
    for head in range(heads):
        rows = lat_ref[head * width : (head + 1) * width, :].astype(jnp.bfloat16)
        value = dot(rows, w_ref[head]).astype(jnp.bfloat16)
        for copy in range(out_ref.shape[0]):
            out_ref[copy, :, head * value_w : (head + 1) * value_w] = value


def project_kernel(width, place_ref, x_ref, *refs):
    ws, out_ref = refs[:-1], refs[-1]
    per_core = out_ref.shape[1]
    cores = out_ref.shape[0] // NX
    x = x_ref[...]
    here = place_ref[0] // NZ
    for k in range(NX):
        block = dot_t(x, ws[k][...])
        owner = (here - k + NX) % NX
        for core in range(cores):
            for i in range(per_core):
                first = (core * per_core + i) * width
                out_ref[owner * cores + core, i] = block[first : first + width]


def sum_kernel(place_ref, in_ref, *outs):
    count = len(outs)
    for j in range(count):
        i = (place_ref[0] + j) % count
        parts = [in_ref[k, i] for k in range(in_ref.shape[0])]
        outs[j][...] = functools.reduce(jnp.add, parts).astype(outs[j].dtype)


def shift(x, axis, n, k):
    if k % n == 0:
        return x
    return lax.ppermute(x, axis, [(i, (i + k) % n) for i in range(n)])


def shift_x(x, k):
    if k % NX == 0:
        return x
    return lax.ppermute(
        x,
        "row",
        [(a * NZ + b, (a + k) % NX * NZ + b) for a in range(NX) for b in range(NZ)],
    )


def on_device(
    q_nope,
    q_rope,
    new_latent,
    new_rope,
    latent_pages,
    rope_pages,
    dest_rows,
    dest_slots,
    page_table,
    lengths,
    w_uk,
    w_uv,
    w_o,
):
    bf16, f32 = jnp.bfloat16, jnp.float32
    n_row = lax.axis_size("row")
    n_head = lax.axis_size("head")
    row, head = lax.axis_index("row"), lax.axis_index("head")
    rows_dev, pages_row = page_table.shape
    pages, page_len, lat_w = latent_pages.shape
    rope_w = new_rope.shape[-1]
    steps, _, heads, nope_w = q_nope.shape
    value_w = w_uv.shape[-1]
    piece = page_len // n_head
    per_pair = 2 * (pages // n_row) + min(pages % n_row, 1)
    scale = 1.0 / (nope_w + rope_w) ** 0.5
    width = steps * rows_dev
    queries = heads * width
    tokens = pages * piece
    slots = n_row * per_pair * piece

    lat = lax.dynamic_slice_in_dim(latent_pages, head * piece, piece, axis=1)
    lat, rope_pages = lax.optimization_barrier((lat, rope_pages))
    lat = lat.reshape(tokens, lat_w)
    rope = lax.dynamic_slice_in_dim(rope_pages, head * piece * rope_w, piece * rope_w, axis=1)
    label = dest_rows % rows_dev * pages_row + dest_slots + 1
    label = jnp.repeat(label, piece)[:, None].astype(bf16)
    tail = jnp.concatenate(
        [rope.reshape(tokens, rope_w), label, jnp.zeros((tokens, TAIL - rope_w - 1), bf16)], axis=1
    )
    dest = dest_rows // rows_dev
    dest_lane = jnp.repeat(dest, piece)[None, :]
    send = call(
        functools.partial(pack_kernel, piece, per_pair),
        jax.ShapeDtypeStruct((slots, lat_w + TAIL), bf16),
        [lat, tail, dest_lane, dest[:, None]],
        scratch=[
            pltpu.VMEM((4, slots // 4, lat_w + TAIL), bf16),
            pltpu.SemaphoreType.DMA((4,)),
        ],
        flops=2 * slots * tokens * (lat_w + TAIL),
        nbytes=2 * (slots + tokens) * (lat_w + TAIL),
        out_spec=pl.BlockSpec(memory_space=pltpu.HBM),
    )
    send = send.reshape(n_row, per_pair * piece, lat_w + TAIL)
    got = lax.all_to_all(send, "row", split_axis=0, concat_axis=0, tiled=True)
    got = got.reshape(slots, lat_w + TAIL)

    place = jnp.stack([row, head]).astype(jnp.int32)
    qn = jnp.transpose(q_nope.reshape(width, heads, nope_w), (1, 0, 2))
    qr = jnp.transpose(q_rope.reshape(width, heads, rope_w), (1, 0, 2)).reshape(queries, rope_w)
    row_lane = jnp.arange(TAIL - rope_w, dtype=jnp.int32)[None, :]
    row_mark = (jnp.arange(queries, dtype=jnp.int32)[:, None] % rows_dev == row_lane).astype(bf16)
    q_tail = jnp.concatenate([qr, row_mark], axis=1)
    fresh = jnp.concatenate(
        [
            new_latent.reshape(width, lat_w),
            new_rope.reshape(width, rope_w),
            jnp.zeros((width, TAIL - rope_w), bf16),
        ],
        axis=1,
    )
    fresh = jnp.concatenate([fresh, jnp.zeros((-width % 16, lat_w + TAIL), bf16)], axis=0)
    query, fresh_part, fresh_lse = call(
        functools.partial(query_kernel, scale, rows_dev),
        (
            jax.ShapeDtypeStruct((lat_w + TAIL, queries), bf16),
            jax.ShapeDtypeStruct((lat_w, queries), f32),
            jax.ShapeDtypeStruct((8, queries), f32),
        ),
        [qn, q_tail, w_uk, fresh, fresh[:, :lat_w].T],
        scratch=[pltpu.VMEM((queries, lat_w), f32)],
        flops=2 * queries * nope_w * lat_w,
        nbytes=2 * heads * nope_w * lat_w,
    )
    all_queries = [shift(query, "head", n_head, k) for k in range(n_head)]
    w_cols = [shift_x(w_o.T, k) for k in range(NX)]

    slot_ids = jnp.arange(pages_row, dtype=jnp.int32)
    holds = (page_table[:, :, None] == slot_ids[None, None, :]).astype(jnp.int32)
    logical = jnp.sum(holds * slot_ids[None, :, None], axis=1)
    limit = lengths[:, None] - logical * page_len - head * piece
    limit = jnp.pad(limit.reshape(1, rows_dev * pages_row), ((0, 0), (0, TAIL - rows_dev * pages_row)))

    parts = call(
        functools.partial(attend_kernel, scale, piece, rope_w, pages_row),
        jax.ShapeDtypeStruct((n_head, lat_w + INFO, queries), bf16),
        [place, got, limit] + all_queries,
        flops=2 * n_head * queries * slots * (2 * lat_w + TAIL),
        nbytes=2 * (slots + 2 * n_head * queries) * (lat_w + TAIL),
    )
    parts = lax.all_to_all(parts, "head", split_axis=0, concat_axis=0, tiled=True)
    head_out = call(
        functools.partial(merge_kernel, width),
        jax.ShapeDtypeStruct((NZ, width, heads * value_w), bf16),
        [fresh_part, fresh_lse, w_uv, parts],
        scratch=[pltpu.VMEM((queries, lat_w), f32)],
        flops=2 * queries * lat_w * value_w,
        nbytes=2 * heads * lat_w * value_w,
    )

    rings = [[a * NZ + b for b in range(NZ)] for a in range(NX)]
    ring = lax.all_to_all(
        head_out, "row", split_axis=0, concat_axis=0, axis_index_groups=rings, tiled=True
    )
    cols = w_o.shape[1]
    cores = n_head // NX
    per_core = NZ // cores
    sums = call(
        functools.partial(project_kernel, width),
        jax.ShapeDtypeStruct((n_head, per_core, width, cols), f32),
        [place, ring.reshape(NZ * width, heads * value_w)] + w_cols,
        flops=2 * NX * NZ * width * w_o.size,
        nbytes=2 * NX * w_o.size,
    )
    sums = lax.all_to_all(sums, "head", split_axis=0, concat_axis=0, tiled=True)
    pieces = call(
        sum_kernel,
        tuple(jax.ShapeDtypeStruct((width, cols), bf16) for _ in range(per_core)),
        [place, sums],
    )
    moved = []
    for j in range(per_core):
        pairs = []
        for r in range(n_row):
            for h in range(n_head):
                ring_at, (a, i) = r // NZ, divmod(r % NZ, per_core)
                y, c = divmod(h, cores)
                to_row = ring_at * NZ + c * per_core + (i + j) % per_core
                pairs.append((r * n_head + h, to_row * n_head + y * cores + a))
        moved.append(lax.ppermute(pieces[j], ("row", "head"), pairs))
    blocks = []
    for i in range(per_core):
        turn = (row - i) % per_core
        block = moved[0]
        for j in range(1, per_core):
            block = jnp.where(turn == j, moved[j], block)
        blocks.append(block)
    out = jnp.concatenate(blocks, axis=1)
    return out.reshape(steps, rows_dev, per_core * cols)


def solution(mesh):
    placed = (
        P(None, "row", "head", None),
        P(None, "row", "head"),
        P(None, "row", None),
        P(None, "row", None),
        P("row", None, None),
        P("row", None),
        P("row"),
        P("row"),
        P("row", None),
        P("row"),
        P("head", None, None),
        P("head", None, None),
        P("head", "row"),
    )
    return jax.shard_map(
        on_device, mesh=mesh, in_specs=placed, out_specs=P(None, "row", "head"), check_vma=False
    )
```

```python
import functools

import jax
import jax.numpy as jnp
from jax import lax
from jax.experimental import pallas as pl
from jax.experimental.pallas import tpu as pltpu
from jax.sharding import PartitionSpec as P

NX = 4
NZ = 8
TAIL = 128
INFO = 16
NEG = -1e30
LOG2E = 1.4426950408889634
LN2 = 0.6931471805599453

VMEM = pl.BlockSpec(memory_space=pltpu.VMEM)
SMEM = pl.BlockSpec(memory_space=pltpu.SMEM)
HBM = pl.BlockSpec(memory_space=pltpu.HBM)


def call(
    body, out_shape, ins, scratch=(), flops=0, nbytes=0, mem=48, out_spec=VMEM, in_hbm=()
):
    return pl.pallas_call(
        body,
        out_shape=out_shape,
        in_specs=[
            HBM if i in in_hbm else SMEM if a.dtype == jnp.int32 and a.ndim == 1 else VMEM
            for i, a in enumerate(ins)
        ],
        out_specs=jax.tree.map(lambda _: out_spec, out_shape),
        scratch_shapes=list(scratch),
        compiler_params=pltpu.CompilerParams(vmem_limit_bytes=mem * 2**20),
        cost_estimate=pl.CostEstimate(flops=flops, bytes_accessed=nbytes, transcendentals=0),
    )(*ins)


def dot(a, b):
    return lax.dot_general(a, b, (((1,), (0,)), ((), ())), preferred_element_type=jnp.float32)


def dot_t(a, b):
    return lax.dot_general(a, b, (((1,), (1,)), ((), ())), preferred_element_type=jnp.float32)


def iota(shape, dim):
    return lax.broadcasted_iota(jnp.int32, shape, dim)


def ones_where(mask):
    return jnp.where(mask, 1.0, 0.0).astype(jnp.bfloat16)


def pack_kernel(
    rows_dev,
    pages_row,
    per_pair,
    place_ref,
    rows_ref,
    slots_ref,
    lat_hbm,
    rope_hbm,
    out_hbm,
    lat_buf,
    rope_buf,
    buf_ref,
    in_sem,
    out_sem,
):
    pages, both, lat_w = lat_buf.shape
    piece = both // 2
    count, block, _ = buf_ref.shape
    chunks = out_sem.shape[0]
    cuts = lat_w // TAIL
    rope_rows = rope_buf.shape[1] // TAIL
    lat_rows = per_pair * cuts * piece
    head = place_ref[1]
    first = pl.multiple_of(head // 2 * both, both)
    lat_copy = pltpu.make_async_copy(lat_hbm.at[:, pl.ds(first, both), :], lat_buf, in_sem.at[0])
    lat_copy.start()
    lane0 = pl.multiple_of(head * rope_buf.shape[1], rope_buf.shape[1])
    rope_copy = pltpu.make_async_copy(
        rope_hbm.at[:, pl.ds(lane0, rope_buf.shape[1])], rope_buf, in_sem.at[1]
    )
    rope_copy.start()

    dest = rows_ref[...] // rows_dev
    label = (rows_ref[...] % rows_dev * pages_row + slots_ref[...] + 1).astype(jnp.float32)
    owned = jnp.where(iota((count, pages), 0) == dest, 1.0, 0.0)
    before = ones_where(iota((pages, pages), 0) < iota((pages, pages), 1))
    rank = jnp.sum(owned * dot(owned.astype(jnp.bfloat16), before), axis=0, keepdims=True)
    rank = rank.astype(jnp.int32)
    at_slot = (dest * per_pair + rank).astype(jnp.float32).astype(jnp.bfloat16)
    spread = ones_where(iota((pages, pages * piece), 0) == iota((pages, pages * piece), 1) // piece)
    at_slot = dot(jnp.broadcast_to(at_slot, (8, pages)), spread)[:1].astype(jnp.int32)
    place = at_slot * piece + iota((1, pages * piece), 1) % piece

    label_lane = iota((TAIL, pages), 0)
    named = ones_where((label_lane // piece == rank) & (label_lane < per_pair * piece))
    labels = dot_t((owned * label).astype(jnp.bfloat16), named).astype(jnp.bfloat16)
    rest = block - lat_rows
    row = iota((count * rest, 1), 0)
    tail = dot(
        ones_where(row == iota((1, count), 1) * rest + per_pair * rope_rows), labels
    )
    rope_copy.wait()
    for j in range(rope_rows):
        pick = ones_where(row == dest * rest + rank * rope_rows + j)
        tail = tail + dot(pick, rope_buf[:, j * TAIL : (j + 1) * TAIL])
    buf_ref[:, lat_rows:, :] = tail.reshape(count, rest, TAIL).astype(jnp.bfloat16)

    lat_copy.wait()
    lat = lat_buf[...].astype(jnp.float32).reshape(pages, 2, piece, lat_w)
    lat = jnp.where(head % 2 == 1, lat[:, 1], lat[:, 0]).reshape(pages * piece, lat_w)
    lat = lat.astype(jnp.bfloat16)
    step = count // chunks
    copies = []
    for i in range(chunks):
        rows = step * per_pair * piece
        value = dot(ones_where(iota((rows, 1), 0) + i * rows == place), lat)
        value = [
            value[:, c * TAIL : (c + 1) * TAIL].reshape(step * per_pair, 1, piece, TAIL)
            for c in range(cuts)
        ]
        value = jnp.concatenate(value, axis=1).reshape(step, lat_rows, TAIL)
        here = pl.ds(i * step, step)
        buf_ref[here, :lat_rows, :] = value.astype(jnp.bfloat16)
        copy = pltpu.make_async_copy(buf_ref.at[here], out_hbm.at[here], out_sem.at[i])
        copy.start()
        copies.append(copy)
    for copy in copies:
        copy.wait()


def split3(x):
    hi = x.astype(jnp.bfloat16)
    rest = x - hi.astype(jnp.float32)
    mid = rest.astype(jnp.bfloat16)
    low = (rest - mid.astype(jnp.float32)).astype(jnp.bfloat16)
    return hi.astype(jnp.float32), mid.astype(jnp.float32), low.astype(jnp.float32)


def query_kernel(
    scale, rows, qn_ref, qtail_ref, w_ref, fresh_ref, fresh_t_ref, q_ref, part_ref, lse_ref, acc_ref
):
    heads, width, _ = qn_ref.shape
    lat_w = w_ref.shape[2]
    steps = width // rows
    for head in range(heads):
        absorbed = dot(qn_ref[head], w_ref[head])
        for row in range(rows):
            at = (row * heads + head) * steps
            acc_ref[at : at + steps, :] = absorbed[row * steps : (row + 1) * steps]
    q_ref[:lat_w, :] = acc_ref[...].T.astype(jnp.bfloat16)
    q_ref[lat_w:, :] = qtail_ref[...].astype(jnp.float32).T.astype(jnp.bfloat16)
    scores = dot(fresh_ref[...], q_ref[...]) * scale
    shape = scores.shape
    token = iota(shape, 0)
    query = iota(shape, 1)
    allowed = (query // (heads * steps) == token % rows) & (token // rows <= query % steps)
    scores = jnp.where(allowed, scores, NEG)
    high = jnp.max(scores, axis=0, keepdims=True)
    weights = jnp.exp(scores - high)
    total = jnp.sum(weights, axis=0, keepdims=True)
    part_ref[...] = dot(fresh_t_ref[...], weights.astype(jnp.bfloat16)) * (1.0 / total)
    lse_ref[...] = jnp.broadcast_to(high + jnp.log(total), lse_ref.shape)


def attend_kernel(
    scale, piece, per_pair, rope_w, pages_row, place_ref, key_ref, bias_ref, q_ref, out_ref
):
    count, block, _ = key_ref.shape
    n_head, _, queries = out_ref.shape
    rows = q_ref.shape[0]
    cuts = (q_ref.shape[1] - TAIL) // TAIL
    lat_w = cuts * TAIL
    pair_tokens = per_pair * piece
    lat_rows = pair_tokens * cuts
    rest = block - lat_rows
    rope_rows = piece * rope_w // TAIL
    per_row = pages_row * piece
    half = per_row // 2

    lat = key_ref[:, :lat_rows, :].astype(jnp.float32)
    lat = lat.reshape(count * per_pair, cuts, piece, TAIL)
    lat = [lat[:, c].reshape(count * pair_tokens, TAIL) for c in range(cuts)]
    lat = jnp.concatenate(lat, axis=1).astype(jnp.bfloat16)
    tail = key_ref[:, lat_rows:, :].astype(jnp.float32)
    marked = iota(tail.shape, 1) == per_pair * rope_rows
    labels = jnp.sum(jnp.where(marked, tail, 0.0), axis=1).astype(jnp.bfloat16)

    def slot_of(columns, group, lane):
        spread = ones_where(iota((TAIL, columns), 0) == lane)
        wide = dot(labels, spread)
        own = iota((count, columns), 0) == iota((1, columns), 1) // group
        return jnp.sum(jnp.where(own, wide, 0.0), axis=0, keepdims=True).astype(jnp.int32) - 1

    columns = count * pair_tokens
    inner = iota((1, columns), 1) % pair_tokens
    slot = slot_of(columns, pair_tokens, inner)
    token = inner % piece
    row = (slot >= pages_row).astype(jnp.int32)
    target = row * (per_row - pages_row * (piece // 2)) + token % 2 * half
    target = target + slot * (piece // 2) + token // 2
    target = jnp.where(slot >= 0, target, -1)
    key = dot(ones_where(iota((rows * per_row, 1), 0) == target), lat).astype(jnp.bfloat16)

    columns = count * rest
    inner = iota((1, columns), 1) % rest
    lane = jnp.where(inner < per_pair * rope_rows, inner // rope_rows * piece, TAIL)
    slot = slot_of(columns, rest, lane)
    target = jnp.where(slot >= 0, slot * rope_rows + inner % rope_rows, -1)
    tail = tail.reshape(columns, TAIL).astype(jnp.bfloat16)
    rope = dot(ones_where(iota((rows * half, 1), 0) == target), tail)

    mark = iota((half, TAIL), 1)
    parts = []
    for b in range(rows):
        rope_b = rope[b * half : (b + 1) * half]
        rope_b = jnp.concatenate([rope_b, pltpu.roll(rope_b, TAIL - rope_w, 1)], axis=0)
        lane = iota(rope_b.shape, 1)
        bias = bias_ref[b * per_row : (b + 1) * per_row]
        rope_b = jnp.where(lane < rope_w, rope_b, jnp.where(lane == rope_w, bias, 0.0))
        key_b = key[b * per_row : (b + 1) * per_row]
        scores = dot(jnp.concatenate([key_b, rope_b.astype(jnp.bfloat16)], axis=1), q_ref[b])
        high = jnp.max(scores, axis=0, keepdims=True)
        weights = jnp.exp2((scores - high) * (scale * LOG2E))
        total = jnp.sum(weights, axis=0, keepdims=True)
        part = dot(key_b.T, weights.astype(jnp.bfloat16)) * (1.0 / total)
        hi, mid, low = split3(high * scale + jnp.log(total))
        mark = iota((INFO, part.shape[1]), 0)
        info = jnp.where(mark == 0, hi, jnp.where(mark == 1, mid, jnp.where(mark == 2, low, 0.0)))
        parts.append(jnp.concatenate([part, info], axis=0))
    head = place_ref[1]
    left = iota((lat_w + INFO, queries), 1) < queries // 2
    for k in range(0, n_head, 2):
        lanes = slice(k * queries // 2, (k + 2) * queries // 2)
        one, two = parts[0][:, lanes], parts[1][:, lanes]
        ready = (
            jnp.where(left, one, pltpu.roll(two, queries // 2, 1)),
            jnp.where(left, pltpu.roll(one, queries // 2, 1), two),
        )
        for i in range(2):
            owner = (head - (k + i) + n_head) % n_head
            out_ref[owner] = ready[i].astype(jnp.bfloat16)


def merge_kernel(rows_dev, fresh_ref, fresh_lse_ref, w_ref, part_ref, out_ref, lat_ref):
    heads, lat_w, value_w = w_ref.shape
    width = out_ref.shape[1]
    steps = width // rows_dev
    count = part_ref.shape[0]
    lses = [fresh_lse_ref[:1, :]]
    for k in range(count):
        info = part_ref[k, lat_w:, :].astype(jnp.float32)
        lses.append(jnp.sum(info, axis=0, keepdims=True))
    high = functools.reduce(jnp.maximum, lses)
    shares = [jnp.exp(lse - high) for lse in lses]
    inverse = 1.0 / functools.reduce(jnp.add, shares)
    total = fresh_ref[...] * (shares[0] * inverse)
    for k in range(count):
        total = total + part_ref[k, :lat_w, :].astype(jnp.float32) * (shares[k + 1] * inverse)
    shape = (heads * width, heads * width)
    to, at = iota(shape, 0), iota(shape, 1)
    wanted = (to % rows_dev * heads + to // width) * steps + to % width // rows_dev
    lat_ref[...] = dot_t(ones_where(at == wanted), total.astype(jnp.bfloat16))
    for head in range(heads):
        rows = lat_ref[head * width : (head + 1) * width, :].astype(jnp.bfloat16)
        value = dot(rows, w_ref[head]).astype(jnp.bfloat16)
        for copy in range(out_ref.shape[0]):
            out_ref[copy, :, head * value_w : (head + 1) * value_w] = value


def project_kernel(width, place_ref, x_ref, *refs):
    ws, out_ref = refs[:-1], refs[-1]
    per_core = out_ref.shape[1]
    cores = out_ref.shape[0] // NX
    depth = x_ref.shape[1] // 2
    here = place_ref[0] // NZ
    own, near, far, opposite_a, opposite_b = ws
    blocks = [
        (0, lambda: dot_t(x_ref[...], own[...])),
        (1, lambda: dot_t(x_ref[...], near[...])),
        (3, lambda: dot_t(x_ref[...], far[...])),
        (
            2,
            lambda: dot_t(x_ref[:, :depth], opposite_a[...])
            + dot_t(x_ref[:, depth:], opposite_b[...]),
        ),
    ]
    for k, make in blocks:
        block = make()
        owner = (here - k + NX) % NX
        for core in range(cores):
            for i in range(per_core):
                first = (core * per_core + i) * width
                out_ref[owner * cores + core, i] = block[first : first + width]


def sum_kernel(place_ref, in_ref, *outs):
    count = len(outs)
    for j in range(count):
        i = (place_ref[0] + j) % count
        parts = [in_ref[k, i] for k in range(in_ref.shape[0])]
        outs[j][...] = functools.reduce(jnp.add, parts).astype(outs[j].dtype)


def shift(x, axis, n, k):
    if k % n == 0:
        return x
    return lax.ppermute(x, axis, [(i, (i + k) % n) for i in range(n)])


def shift_x(x, k):
    if k % NX == 0:
        return x
    return lax.ppermute(
        x,
        "row",
        [(a * NZ + b, (a + k) % NX * NZ + b) for a in range(NX) for b in range(NZ)],
    )


def on_device(
    q_nope,
    q_rope,
    new_latent,
    new_rope,
    latent_pages,
    rope_pages,
    dest_rows,
    dest_slots,
    page_table,
    lengths,
    w_uk,
    w_uv,
    w_o,
):
    bf16, f32 = jnp.bfloat16, jnp.float32
    n_row = lax.axis_size("row")
    n_head = lax.axis_size("head")
    row, head = lax.axis_index("row"), lax.axis_index("head")
    rows_dev, pages_row = page_table.shape
    pages, page_len, lat_w = latent_pages.shape
    rope_w = new_rope.shape[-1]
    steps, _, heads, nope_w = q_nope.shape
    value_w = w_uv.shape[-1]
    piece = page_len // n_head
    per_pair = 2 * (pages // n_row) + min(pages % n_row, 1)
    scale = 1.0 / (nope_w + rope_w) ** 0.5
    width = steps * rows_dev
    queries = heads * width
    tokens = pages * piece
    slots = n_row * per_pair * piece

    place = jnp.stack([row, head]).astype(jnp.int32)
    lat_rows = per_pair * piece * lat_w // TAIL
    rope_rows = per_pair * piece * rope_w // TAIL
    block = lat_rows + (rope_rows + 8) // 8 * 8
    send = call(
        functools.partial(pack_kernel, rows_dev, pages_row, per_pair),
        jax.ShapeDtypeStruct((n_row, block, TAIL), bf16),
        [place, dest_rows[None, :], dest_slots[None, :], latent_pages, rope_pages],
        scratch=[
            pltpu.VMEM((pages, 2 * piece, lat_w), bf16),
            pltpu.VMEM((pages, piece * rope_w), bf16),
            pltpu.VMEM((n_row, block, TAIL), bf16),
            pltpu.SemaphoreType.DMA((2,)),
            pltpu.SemaphoreType.DMA((4,)),
        ],
        flops=2 * slots * tokens * lat_w,
        nbytes=2 * (slots + 2 * tokens) * lat_w,
        mem=60,
        out_spec=HBM,
        in_hbm=(3, 4),
    )
    got = lax.all_to_all(send, "row", split_axis=0, concat_axis=0, tiled=True)

    qn = jnp.transpose(q_nope, (2, 1, 0, 3)).reshape(heads, width, nope_w)
    qr = q_rope.reshape(steps, rows_dev, heads, rope_w)
    qr = jnp.transpose(qr, (1, 2, 0, 3)).reshape(queries, rope_w)
    one_lane = jnp.arange(TAIL - rope_w, dtype=jnp.int32)[None, :] == 0
    q_tail = jnp.concatenate(
        [qr, jnp.broadcast_to(one_lane, (queries, TAIL - rope_w)).astype(bf16)], axis=1
    )
    fresh = jnp.concatenate(
        [
            new_latent.reshape(width, lat_w),
            new_rope.reshape(width, rope_w),
            jnp.zeros((width, TAIL - rope_w), bf16),
        ],
        axis=1,
    )
    fresh = jnp.concatenate([fresh, jnp.zeros((-width % 16, lat_w + TAIL), bf16)], axis=0)
    query, fresh_part, fresh_lse = call(
        functools.partial(query_kernel, scale, rows_dev),
        (
            jax.ShapeDtypeStruct((lat_w + TAIL, queries), bf16),
            jax.ShapeDtypeStruct((lat_w, queries), f32),
            jax.ShapeDtypeStruct((8, queries), f32),
        ),
        [qn, q_tail, w_uk, fresh, fresh[:, :lat_w].T],
        scratch=[pltpu.VMEM((queries, lat_w), f32)],
        flops=2 * queries * nope_w * lat_w,
        nbytes=2 * heads * nope_w * lat_w,
    )
    all_queries = [shift(query, "head", n_head, k) for k in range(n_head)]
    per_row = queries // rows_dev
    all_queries = jnp.stack(
        [
            jnp.concatenate([q[:, b * per_row : (b + 1) * per_row] for q in all_queries], axis=1)
            for b in range(rows_dev)
        ]
    )

    w_t = w_o.T
    w_near, w_far = shift_x(w_t, 1), shift_x(w_t, -1)
    depth = w_t.shape[1] // 2

    slot_ids = jnp.arange(pages_row, dtype=jnp.int32)
    holds = (page_table[:, :, None] == slot_ids[None, None, :]).astype(jnp.int32)
    logical = jnp.sum(holds * slot_ids[None, :, None], axis=1)
    limit = lengths[:, None] - logical * page_len - head * piece
    within = jnp.arange(piece, dtype=jnp.int32).reshape(piece // 2, 2).T
    usable = within[None, :, None, :] < limit[:, None, :, None]
    bias = jnp.where(usable, 0.0, NEG).astype(f32).reshape(rows_dev * pages_row * piece, 1)

    got, w_near, w_far = lax.optimization_barrier((got, w_near, w_far))
    w_cols = [
        w_t,
        w_near,
        w_far,
        shift_x(w_near[:, :depth], 1),
        shift_x(w_far[:, depth:], -1),
    ]
    parts = call(
        functools.partial(attend_kernel, scale, piece, per_pair, rope_w, pages_row),
        jax.ShapeDtypeStruct((n_head, lat_w + INFO, queries), bf16),
        [place, got, bias, all_queries],
        flops=2 * n_head * queries * tokens * (2 * lat_w + TAIL) // 2 + 2 * slots * tokens * lat_w,
        nbytes=2 * (slots + 2 * n_head * queries) * (lat_w + TAIL),
    )
    parts = lax.all_to_all(parts, "head", split_axis=0, concat_axis=0, tiled=True)
    head_out = call(
        functools.partial(merge_kernel, rows_dev),
        jax.ShapeDtypeStruct((NZ, width, heads * value_w), bf16),
        [fresh_part, fresh_lse, w_uv, parts],
        scratch=[pltpu.VMEM((queries, lat_w), f32)],
        flops=2 * queries * lat_w * value_w,
        nbytes=2 * heads * lat_w * value_w,
    )

    rings = [[a * NZ + b for b in range(NZ)] for a in range(NX)]
    ring = lax.all_to_all(
        head_out, "row", split_axis=0, concat_axis=0, axis_index_groups=rings, tiled=True
    )
    cols = w_o.shape[1]
    cores = n_head // NX
    per_core = NZ // cores
    sums = call(
        functools.partial(project_kernel, width),
        jax.ShapeDtypeStruct((n_head, per_core, width, cols), f32),
        [place, ring.reshape(NZ * width, heads * value_w)] + w_cols,
        flops=2 * NX * NZ * width * w_o.size,
        nbytes=2 * NX * w_o.size,
    )
    sums = lax.all_to_all(sums, "head", split_axis=0, concat_axis=0, tiled=True)
    pieces = call(
        sum_kernel,
        tuple(jax.ShapeDtypeStruct((width, cols), bf16) for _ in range(per_core)),
        [place, sums],
    )
    moved = []
    for j in range(per_core):
        pairs = []
        for r in range(n_row):
            for h in range(n_head):
                ring_at, (a, i) = r // NZ, divmod(r % NZ, per_core)
                y, c = divmod(h, cores)
                to_row = ring_at * NZ + c * per_core + (i + j) % per_core
                pairs.append((r * n_head + h, to_row * n_head + y * cores + a))
        moved.append(lax.ppermute(pieces[j], ("row", "head"), pairs))
    blocks = []
    for i in range(per_core):
        turn = (row - i) % per_core
        block = moved[0]
        for j in range(1, per_core):
            block = jnp.where(turn == j, moved[j], block)
        blocks.append(block)
    out = jnp.concatenate(blocks, axis=1)
    return out.reshape(steps, rows_dev, per_core * cols)


def solution(mesh):
    placed = (
        P(None, "row", "head", None),
        P(None, "row", "head"),
        P(None, "row", None),
        P(None, "row", None),
        P("row", None, None),
        P("row", None),
        P("row"),
        P("row"),
        P("row", None),
        P("row"),
        P("head", None, None),
        P("head", None, None),
        P("head", "row"),
    )
    return jax.shard_map(
        on_device, mesh=mesh, in_specs=placed, out_specs=P(None, "row", "head"), check_vma=False
    )
```

```python
import functools

import jax
import jax.numpy as jnp
from jax import lax
from jax.experimental import pallas as pl
from jax.experimental.pallas import tpu as pltpu
from jax.sharding import PartitionSpec as P

NX = 4
NZ = 8
TAIL = 128
INFO = 16
NEG = -1e30
LOG2E = 1.4426950408889634
LN2 = 0.6931471805599453

VMEM = pl.BlockSpec(memory_space=pltpu.VMEM)
SMEM = pl.BlockSpec(memory_space=pltpu.SMEM)
HBM = pl.BlockSpec(memory_space=pltpu.HBM)


def call(
    body, out_shape, ins, scratch=(), flops=0, nbytes=0, mem=24, out_spec=VMEM, in_hbm=()
):
    return pl.pallas_call(
        body,
        out_shape=out_shape,
        in_specs=[
            HBM if i in in_hbm else SMEM if a.dtype == jnp.int32 and a.ndim == 1 else VMEM
            for i, a in enumerate(ins)
        ],
        out_specs=jax.tree.map(lambda _: out_spec, out_shape),
        scratch_shapes=list(scratch),
        compiler_params=pltpu.CompilerParams(vmem_limit_bytes=mem * 2**20),
        cost_estimate=pl.CostEstimate(flops=flops, bytes_accessed=nbytes, transcendentals=0),
    )(*ins)


def dot(a, b):
    return lax.dot_general(a, b, (((1,), (0,)), ((), ())), preferred_element_type=jnp.float32)


def dot_t(a, b):
    return lax.dot_general(a, b, (((1,), (1,)), ((), ())), preferred_element_type=jnp.float32)


def iota(shape, dim):
    return lax.broadcasted_iota(jnp.int32, shape, dim)


def ones_where(mask):
    return jnp.where(mask, 1.0, 0.0).astype(jnp.bfloat16)


def pack_kernel(
    rows_dev,
    pages_row,
    per_pair,
    rows_ref,
    slots_ref,
    lat_hbm,
    rope_hbm,
    out_hbm,
    lat_buf,
    rope_buf,
    buf_ref,
    in_sem,
    out_sem,
):
    pages, both, lat_w = lat_buf.shape
    piece = both // 2
    count, block, _ = buf_ref.shape
    chunks = out_sem.shape[0]
    cuts = lat_w // TAIL
    rope_rows = rope_buf.shape[1] // TAIL
    lat_rows = per_pair * cuts * piece
    head = lax.axis_index("head")
    first = pl.multiple_of(head // 2 * both, both)
    lat_copy = pltpu.make_async_copy(lat_hbm.at[:, pl.ds(first, both), :], lat_buf, in_sem.at[0])
    lat_copy.start()
    lane0 = pl.multiple_of(head * rope_buf.shape[1], rope_buf.shape[1])
    rope_copy = pltpu.make_async_copy(
        rope_hbm.at[:, pl.ds(lane0, rope_buf.shape[1])], rope_buf, in_sem.at[1]
    )
    rope_copy.start()

    dest = rows_ref[...] // rows_dev
    label = (rows_ref[...] % rows_dev * pages_row + slots_ref[...] + 1).astype(jnp.float32)
    owned = jnp.where(iota((count, pages), 0) == dest, 1.0, 0.0)
    before = ones_where(iota((pages, pages), 0) < iota((pages, pages), 1))
    rank = jnp.sum(owned * dot(owned.astype(jnp.bfloat16), before), axis=0, keepdims=True)
    rank = rank.astype(jnp.int32)
    at_slot = (dest * per_pair + rank).astype(jnp.float32).astype(jnp.bfloat16)
    spread = ones_where(iota((pages, pages * piece), 0) == iota((pages, pages * piece), 1) // piece)
    at_slot = dot(jnp.broadcast_to(at_slot, (8, pages)), spread)[:1].astype(jnp.int32)
    place = at_slot * piece + iota((1, pages * piece), 1) % piece

    label_lane = iota((TAIL, pages), 0)
    named = ones_where((label_lane // piece == rank) & (label_lane < per_pair * piece))
    labels = dot_t((owned * label).astype(jnp.bfloat16), named).astype(jnp.bfloat16)
    rest = block - lat_rows
    row = iota((count * rest, 1), 0)
    tail = dot(
        ones_where(row == iota((1, count), 1) * rest + per_pair * rope_rows), labels
    )
    rope_copy.wait()
    for j in range(rope_rows):
        pick = ones_where(row == dest * rest + rank * rope_rows + j)
        tail = tail + dot(pick, rope_buf[:, j * TAIL : (j + 1) * TAIL])
    buf_ref[:, lat_rows:, :] = tail.reshape(count, rest, TAIL).astype(jnp.bfloat16)

    lat_copy.wait()
    lat = lat_buf[...].astype(jnp.float32).reshape(pages, 2, piece, lat_w)
    lat = jnp.where(head % 2 == 1, lat[:, 1], lat[:, 0]).reshape(pages * piece, lat_w)
    lat = lat.astype(jnp.bfloat16)
    step = count // chunks
    copies = []
    for i in range(chunks):
        rows = step * per_pair * piece
        value = dot(ones_where(iota((rows, 1), 0) + i * rows == place), lat)
        value = [
            value[:, c * TAIL : (c + 1) * TAIL].reshape(step * per_pair, 1, piece, TAIL)
            for c in range(cuts)
        ]
        value = jnp.concatenate(value, axis=1).reshape(step, lat_rows, TAIL)
        here = pl.ds(i * step, step)
        buf_ref[here, :lat_rows, :] = value.astype(jnp.bfloat16)
        copy = pltpu.make_async_copy(buf_ref.at[here], out_hbm.at[here], out_sem.at[i])
        copy.start()
        copies.append(copy)
    for copy in copies:
        copy.wait()


def split3(x):
    hi = x.astype(jnp.bfloat16)
    rest = x - hi.astype(jnp.float32)
    mid = rest.astype(jnp.bfloat16)
    low = (rest - mid.astype(jnp.float32)).astype(jnp.bfloat16)
    return hi.astype(jnp.float32), mid.astype(jnp.float32), low.astype(jnp.float32)


def query_kernel(
    scale, rows, qn_ref, qtail_ref, w_ref, fresh_ref, fresh_t_ref, q_ref, swap_ref, part_ref, lse_ref, acc_ref
):
    heads, width, _ = qn_ref.shape
    lat_w = w_ref.shape[2]
    steps = width // rows
    for head in range(heads):
        absorbed = dot(qn_ref[head], w_ref[head])
        for row in range(rows):
            at = (row * heads + head) * steps
            acc_ref[at : at + steps, :] = absorbed[row * steps : (row + 1) * steps]
    half = rows * heads * steps // 2
    absorbed = acc_ref[...].T
    tail = qtail_ref[...].astype(jnp.float32).T
    q_ref[:lat_w, :] = absorbed.astype(jnp.bfloat16)
    q_ref[lat_w:, :] = tail.astype(jnp.bfloat16)
    swap_ref[:lat_w, :] = pltpu.roll(absorbed, half, 1).astype(jnp.bfloat16)
    swap_ref[lat_w:, :] = pltpu.roll(tail, half, 1).astype(jnp.bfloat16)
    scores = dot(fresh_ref[...], q_ref[...]) * scale
    shape = scores.shape
    token = iota(shape, 0)
    query = iota(shape, 1)
    allowed = (query // (heads * steps) == token % rows) & (token // rows <= query % steps)
    scores = jnp.where(allowed, scores, NEG)
    high = jnp.max(scores, axis=0, keepdims=True)
    weights = jnp.exp(scores - high)
    total = jnp.sum(weights, axis=0, keepdims=True)
    part_ref[...] = dot(fresh_t_ref[...], weights.astype(jnp.bfloat16)) * (1.0 / total)
    lse_ref[...] = jnp.broadcast_to(high + jnp.log(total), lse_ref.shape)


def attend_kernel(
    scale, piece, per_pair, rope_w, pages_row, key_ref, bias_ref, *refs
):
    q_refs, out_ref = refs[:-1], refs[-1]
    count, block, _ = key_ref.shape
    n_head, _, queries = out_ref.shape
    rows = 2
    cuts = (q_refs[0].shape[0] - TAIL) // TAIL
    lat_w = cuts * TAIL
    pair_tokens = per_pair * piece
    lat_rows = pair_tokens * cuts
    rest = block - lat_rows
    rope_rows = piece * rope_w // TAIL
    per_row = pages_row * piece
    half = per_row // 2

    lat = key_ref[:, :lat_rows, :].astype(jnp.float32)
    lat = lat.reshape(count * per_pair, cuts, piece, TAIL)
    lat = [lat[:, c].reshape(count * pair_tokens, TAIL) for c in range(cuts)]
    lat = jnp.concatenate(lat, axis=1).astype(jnp.bfloat16)
    tail = key_ref[:, lat_rows:, :].astype(jnp.float32)
    marked = iota(tail.shape, 1) == per_pair * rope_rows
    labels = jnp.sum(jnp.where(marked, tail, 0.0), axis=1).astype(jnp.bfloat16)

    def slot_of(columns, group, lane):
        spread = ones_where(iota((TAIL, columns), 0) == lane)
        wide = dot(labels, spread)
        own = iota((count, columns), 0) == iota((1, columns), 1) // group
        return jnp.sum(jnp.where(own, wide, 0.0), axis=0, keepdims=True).astype(jnp.int32) - 1

    columns = count * pair_tokens
    inner = iota((1, columns), 1) % pair_tokens
    slot = slot_of(columns, pair_tokens, inner)
    token = inner % piece
    row = (slot >= pages_row).astype(jnp.int32)
    target = row * (per_row - pages_row * (piece // 2)) + token % 2 * half
    target = target + slot * (piece // 2) + token // 2
    target = jnp.where(slot >= 0, target, -1)
    key = dot(ones_where(iota((rows * per_row, 1), 0) == target), lat).astype(jnp.bfloat16)

    columns = count * rest
    inner = iota((1, columns), 1) % rest
    lane = jnp.where(inner < per_pair * rope_rows, inner // rope_rows * piece, TAIL)
    slot = slot_of(columns, rest, lane)
    target = jnp.where(slot >= 0, slot * rope_rows + inner % rope_rows, -1)
    tail = tail.reshape(columns, TAIL).astype(jnp.bfloat16)
    rope = dot(ones_where(iota((rows * half, 1), 0) == target), tail)

    left = iota((lat_w + TAIL, queries), 1) < queries // 2
    asked = [[], []]
    for k in range(0, n_head, 2):
        one, two = q_refs[k][...].astype(jnp.float32), q_refs[k + 1][...].astype(jnp.float32)
        asked[0].append(jnp.where(left, one, two).astype(jnp.bfloat16))
        asked[1].append(jnp.where(left, two, one).astype(jnp.bfloat16))
    parts = []
    for b in range(rows):
        rope_b = rope[b * half : (b + 1) * half]
        rope_b = jnp.concatenate([rope_b, pltpu.roll(rope_b, TAIL - rope_w, 1)], axis=0)
        lane = iota(rope_b.shape, 1)
        bias = bias_ref[b * per_row : (b + 1) * per_row]
        rope_b = jnp.where(lane < rope_w, rope_b, jnp.where(lane == rope_w, bias, 0.0))
        key_b = key[b * per_row : (b + 1) * per_row]
        query = jnp.concatenate(asked[b], axis=1)
        scores = dot(jnp.concatenate([key_b, rope_b.astype(jnp.bfloat16)], axis=1), query)
        high = jnp.max(scores, axis=0, keepdims=True)
        weights = jnp.exp2((scores - high) * (scale * LOG2E))
        total = jnp.sum(weights, axis=0, keepdims=True)
        part = dot(key_b.T, weights.astype(jnp.bfloat16)) * (1.0 / total)
        hi, mid, low = split3(high * scale + jnp.log(total))
        mark = iota((INFO, part.shape[1]), 0)
        info = jnp.where(mark == 0, hi, jnp.where(mark == 1, mid, jnp.where(mark == 2, low, 0.0)))
        parts.append(jnp.concatenate([part, info], axis=0))
    head = lax.axis_index("head")
    left = iota((lat_w + INFO, queries), 1) < queries // 2
    for k in range(0, n_head, 2):
        lanes = slice(k * queries // 2, (k + 2) * queries // 2)
        one, two = parts[0][:, lanes], parts[1][:, lanes]
        ready = (jnp.where(left, one, two), jnp.where(left, two, one))
        for i in range(2):
            owner = (head - (k + i) + n_head) % n_head
            out_ref[owner] = ready[i].astype(jnp.bfloat16)


def merge_kernel(rows_dev, fresh_ref, fresh_lse_ref, w_ref, part_ref, out_ref, lat_ref):
    heads, lat_w, value_w = w_ref.shape
    width = out_ref.shape[1]
    steps = width // rows_dev
    count = part_ref.shape[0]
    odd = lax.axis_index("head") % 2
    half = part_ref.shape[2] // 2
    lses = [fresh_lse_ref[...]]
    for k in range(count):
        info = jnp.sum(part_ref[k, lat_w:, :].astype(jnp.float32), axis=0, keepdims=True)
        info = jnp.broadcast_to(info, lses[0].shape)
        lses.append(jnp.where(odd != k % 2, pltpu.roll(info, half, 1), info))
    high = functools.reduce(jnp.maximum, lses)
    shares = [jnp.exp(lse - high) for lse in lses]
    inverse = 1.0 / functools.reduce(jnp.add, shares)
    total = fresh_ref[...] * (shares[0] * inverse)[:1]
    sums = [0.0, 0.0]
    for k in range(count):
        share = shares[k + 1] * inverse
        share = jnp.where(odd != k % 2, pltpu.roll(share, half, 1), share)[:1]
        sums[k % 2] = sums[k % 2] + part_ref[k, :lat_w, :].astype(jnp.float32) * share
    same = jnp.where(odd == 1, sums[1], sums[0])
    other = jnp.where(odd == 1, sums[0], sums[1])
    total = total + same + pltpu.roll(other, half, 1)
    shape = (heads * width, heads * width)
    to, at = iota(shape, 0), iota(shape, 1)
    wanted = (to % rows_dev * heads + to // width) * steps + to % width // rows_dev
    lat_ref[...] = dot_t(ones_where(at == wanted), total.astype(jnp.bfloat16))
    for head in range(heads):
        rows = lat_ref[head * width : (head + 1) * width, :].astype(jnp.bfloat16)
        value = dot(rows, w_ref[head]).astype(jnp.bfloat16)
        for copy in range(out_ref.shape[0]):
            out_ref[copy, :, head * value_w : (head + 1) * value_w] = value


def project_kernel(width, x_ref, w_ref, out_ref):
    per_core = out_ref.shape[1]
    cores = out_ref.shape[0] // NX
    x = x_ref[...]
    for k in range(NX):
        block = dot_t(x, w_ref[k])
        for core in range(cores):
            for i in range(per_core):
                first = (core * per_core + i) * width
                out_ref[k * cores + core, i] = block[first : first + width]


def sum_kernel(in_ref, *outs):
    count = len(outs)
    for j in range(count):
        i = (lax.axis_index("row") + j) % count
        parts = [in_ref[k, i] for k in range(in_ref.shape[0])]
        outs[j][...] = functools.reduce(jnp.add, parts).astype(outs[j].dtype)


def shift(x, axis, n, k):
    if k % n == 0:
        return x
    return lax.ppermute(x, axis, [(i, (i + k) % n) for i in range(n)])


def on_device(
    q_nope,
    q_rope,
    new_latent,
    new_rope,
    latent_pages,
    rope_pages,
    dest_rows,
    dest_slots,
    page_table,
    lengths,
    w_uk,
    w_uv,
    w_o,
):
    bf16, f32 = jnp.bfloat16, jnp.float32
    n_row = lax.axis_size("row")
    n_head = lax.axis_size("head")
    row, head = lax.axis_index("row"), lax.axis_index("head")
    rows_dev, pages_row = page_table.shape
    pages, page_len, lat_w = latent_pages.shape
    rope_w = new_rope.shape[-1]
    steps, _, heads, nope_w = q_nope.shape
    value_w = w_uv.shape[-1]
    piece = page_len // n_head
    per_pair = 2 * (pages // n_row) + min(pages % n_row, 1)
    scale = 1.0 / (nope_w + rope_w) ** 0.5
    width = steps * rows_dev
    queries = heads * width
    tokens = pages * piece
    slots = n_row * per_pair * piece

    lat_rows = per_pair * piece * lat_w // TAIL
    rope_rows = per_pair * piece * rope_w // TAIL
    block = lat_rows + (rope_rows + 8) // 8 * 8
    send = call(
        functools.partial(pack_kernel, rows_dev, pages_row, per_pair),
        jax.ShapeDtypeStruct((n_row, block, TAIL), bf16),
        [dest_rows[None, :], dest_slots[None, :], latent_pages, rope_pages],
        scratch=[
            pltpu.VMEM((pages, 2 * piece, lat_w), bf16),
            pltpu.VMEM((pages, piece * rope_w), bf16),
            pltpu.VMEM((n_row, block, TAIL), bf16),
            pltpu.SemaphoreType.DMA((2,)),
            pltpu.SemaphoreType.DMA((4,)),
        ],
        flops=2 * slots * tokens * lat_w,
        nbytes=2 * (slots + 2 * tokens) * lat_w,
        mem=60,
        out_spec=HBM,
        in_hbm=(2, 3),
    )
    got = lax.all_to_all(send, "row", split_axis=0, concat_axis=0, tiled=True)

    qn = jnp.transpose(q_nope, (2, 1, 0, 3)).reshape(heads, width, nope_w)
    qr = q_rope.reshape(steps, rows_dev, heads, rope_w)
    qr = jnp.transpose(qr, (1, 2, 0, 3)).reshape(queries, rope_w)
    one_lane = jnp.arange(TAIL - rope_w, dtype=jnp.int32)[None, :] == 0
    q_tail = jnp.concatenate(
        [qr, jnp.broadcast_to(one_lane, (queries, TAIL - rope_w)).astype(bf16)], axis=1
    )
    fresh = jnp.concatenate(
        [
            new_latent.reshape(width, lat_w),
            new_rope.reshape(width, rope_w),
            jnp.zeros((width, TAIL - rope_w), bf16),
        ],
        axis=1,
    )
    fresh = jnp.concatenate([fresh, jnp.zeros((-width % 16, lat_w + TAIL), bf16)], axis=0)
    query, swapped, fresh_part, fresh_lse = call(
        functools.partial(query_kernel, scale, rows_dev),
        (
            jax.ShapeDtypeStruct((lat_w + TAIL, queries), bf16),
            jax.ShapeDtypeStruct((lat_w + TAIL, queries), bf16),
            jax.ShapeDtypeStruct((lat_w, queries), f32),
            jax.ShapeDtypeStruct((8, queries), f32),
        ),
        [qn, q_tail, w_uk, fresh, fresh[:, :lat_w].T],
        scratch=[pltpu.VMEM((queries, lat_w), f32)],
        flops=2 * queries * nope_w * lat_w,
        nbytes=2 * heads * nope_w * lat_w,
    )
    all_queries = [shift((query, swapped)[k % 2], "head", n_head, k) for k in range(n_head)]

    w_rings = [[a * NZ + b for a in range(NX)] for b in range(NZ)]
    w_cols = lax.all_gather(w_o.T, "row", axis_index_groups=w_rings)

    slot_ids = jnp.arange(pages_row, dtype=jnp.int32)
    holds = (page_table[:, :, None] == slot_ids[None, None, :]).astype(jnp.int32)
    logical = jnp.sum(holds * slot_ids[None, :, None], axis=1)
    limit = lengths[:, None] - logical * page_len - head * piece
    within = jnp.arange(piece, dtype=jnp.int32).reshape(piece // 2, 2).T
    usable = within[None, :, None, :] < limit[:, None, :, None]
    bias = jnp.where(usable, 0.0, NEG).astype(f32).reshape(rows_dev * pages_row * piece, 1)

    parts = call(
        functools.partial(attend_kernel, scale, piece, per_pair, rope_w, pages_row),
        jax.ShapeDtypeStruct((n_head, lat_w + INFO, queries), bf16),
        [got, bias] + all_queries,
        flops=2 * n_head * queries * tokens * (2 * lat_w + TAIL) // 2 + 2 * slots * tokens * lat_w,
        nbytes=2 * (slots + 2 * n_head * queries) * (lat_w + TAIL),
    )
    parts = lax.all_to_all(parts, "head", split_axis=0, concat_axis=0, tiled=True)
    head_out = call(
        functools.partial(merge_kernel, rows_dev),
        jax.ShapeDtypeStruct((NZ, width, heads * value_w), bf16),
        [fresh_part, fresh_lse, w_uv, parts],
        scratch=[pltpu.VMEM((queries, lat_w), f32)],
        flops=2 * queries * lat_w * value_w,
        nbytes=2 * heads * lat_w * value_w,
    )

    rings = [[a * NZ + b for b in range(NZ)] for a in range(NX)]
    ring = lax.all_to_all(
        head_out, "row", split_axis=0, concat_axis=0, axis_index_groups=rings, tiled=True
    )
    cols = w_o.shape[1]
    cores = n_head // NX
    per_core = NZ // cores
    sums = call(
        functools.partial(project_kernel, width),
        jax.ShapeDtypeStruct((n_head, per_core, width, cols), f32),
        [ring.reshape(NZ * width, heads * value_w), w_cols],
        flops=2 * NX * NZ * width * w_o.size,
        nbytes=2 * NX * w_o.size,
    )
    sums = lax.all_to_all(sums, "head", split_axis=0, concat_axis=0, tiled=True)
    pieces = call(
        sum_kernel,
        tuple(jax.ShapeDtypeStruct((width, cols), bf16) for _ in range(per_core)),
        [sums],
    )
    moved = []
    for j in range(per_core):
        pairs = []
        for r in range(n_row):
            for h in range(n_head):
                ring_at, (a, i) = r // NZ, divmod(r % NZ, per_core)
                y, c = divmod(h, cores)
                to_row = ring_at * NZ + c * per_core + (i + j) % per_core
                pairs.append((r * n_head + h, to_row * n_head + y * cores + a))
        moved.append(lax.ppermute(pieces[j], ("row", "head"), pairs))
    blocks = []
    for i in range(per_core):
        turn = (row - i) % per_core
        block = moved[0]
        for j in range(1, per_core):
            block = jnp.where(turn == j, moved[j], block)
        blocks.append(block)
    out = jnp.concatenate(blocks, axis=1)
    return out.reshape(steps, rows_dev, per_core * cols)


def solution(mesh):
    placed = (
        P(None, "row", "head", None),
        P(None, "row", "head"),
        P(None, "row", None),
        P(None, "row", None),
        P("row", None, None),
        P("row", None),
        P("row"),
        P("row"),
        P("row", None),
        P("row"),
        P("head", None, None),
        P("head", None, None),
        P("head", "row"),
    )
    return jax.shard_map(
        on_device, mesh=mesh, in_specs=placed, out_specs=P(None, "row", "head"), check_vma=False
    )
```

```python
import functools

import jax
import jax.numpy as jnp
from jax import lax
from jax.experimental import pallas as pl
from jax.experimental.pallas import tpu as pltpu
from jax.sharding import PartitionSpec as P

NX = 4
NZ = 8
TAIL = 128
INFO = 16
NEG = -1e30
LOG2E = 1.4426950408889634
LN2 = 0.6931471805599453

VMEM = pl.BlockSpec(memory_space=pltpu.VMEM)
SMEM = pl.BlockSpec(memory_space=pltpu.SMEM)
HBM = pl.BlockSpec(memory_space=pltpu.HBM)


def call(
    body, out_shape, ins, scratch=(), flops=0, nbytes=0, mem=24, out_spec=VMEM, in_hbm=()
):
    return pl.pallas_call(
        body,
        out_shape=out_shape,
        in_specs=[
            HBM if i in in_hbm else SMEM if a.dtype == jnp.int32 and a.ndim == 1 else VMEM
            for i, a in enumerate(ins)
        ],
        out_specs=jax.tree.map(lambda _: out_spec, out_shape),
        scratch_shapes=list(scratch),
        compiler_params=pltpu.CompilerParams(vmem_limit_bytes=mem * 2**20),
        cost_estimate=pl.CostEstimate(flops=flops, bytes_accessed=nbytes, transcendentals=0),
    )(*ins)


def dot(a, b):
    return lax.dot_general(a, b, (((1,), (0,)), ((), ())), preferred_element_type=jnp.float32)


def dot_t(a, b):
    return lax.dot_general(a, b, (((1,), (1,)), ((), ())), preferred_element_type=jnp.float32)


def iota(shape, dim):
    return lax.broadcasted_iota(jnp.int32, shape, dim)


def ones_where(mask):
    return jnp.where(mask, 1.0, 0.0).astype(jnp.bfloat16)


def pack_kernel(
    rows_dev,
    pages_row,
    per_pair,
    rows_ref,
    slots_ref,
    lat_hbm,
    rope_hbm,
    out_hbm,
    lat_buf,
    rope_buf,
    buf_ref,
    in_sem,
    out_sem,
):
    pages, both, lat_w = lat_buf.shape
    piece = both // 2
    count, block, _ = buf_ref.shape
    chunks = out_sem.shape[0]
    cuts = lat_w // TAIL
    rope_rows = rope_buf.shape[1] // TAIL
    lat_rows = per_pair * cuts * piece
    head = lax.axis_index("head")
    first = pl.multiple_of(head // 2 * both, both)
    lat_copy = pltpu.make_async_copy(lat_hbm.at[:, pl.ds(first, both), :], lat_buf, in_sem.at[0])
    lat_copy.start()
    lane0 = pl.multiple_of(head * rope_buf.shape[1], rope_buf.shape[1])
    rope_copy = pltpu.make_async_copy(
        rope_hbm.at[:, pl.ds(lane0, rope_buf.shape[1])], rope_buf, in_sem.at[1]
    )
    rope_copy.start()

    dest = rows_ref[...] // rows_dev
    label = (rows_ref[...] % rows_dev * pages_row + slots_ref[...] + 1).astype(jnp.float32)
    owned = jnp.where(iota((count, pages), 0) == dest, 1.0, 0.0)
    before = ones_where(iota((pages, pages), 0) < iota((pages, pages), 1))
    rank = jnp.sum(owned * dot(owned.astype(jnp.bfloat16), before), axis=0, keepdims=True)
    rank = rank.astype(jnp.int32)
    at_slot = (dest * per_pair + rank).astype(jnp.float32).astype(jnp.bfloat16)
    spread = ones_where(iota((pages, pages * piece), 0) == iota((pages, pages * piece), 1) // piece)
    at_slot = dot(jnp.broadcast_to(at_slot, (8, pages)), spread)[:1].astype(jnp.int32)
    place = at_slot * piece + iota((1, pages * piece), 1) % piece

    label_lane = iota((TAIL, pages), 0)
    named = ones_where((label_lane // piece == rank) & (label_lane < per_pair * piece))
    labels = dot_t((owned * label).astype(jnp.bfloat16), named).astype(jnp.bfloat16)
    rest = block - lat_rows
    row = iota((count * rest, 1), 0)
    tail = dot(
        ones_where(row == iota((1, count), 1) * rest + per_pair * rope_rows), labels
    )
    rope_copy.wait()
    for j in range(rope_rows):
        pick = ones_where(row == dest * rest + rank * rope_rows + j)
        tail = tail + dot(pick, rope_buf[:, j * TAIL : (j + 1) * TAIL])
    buf_ref[:, lat_rows:, :] = tail.reshape(count, rest, TAIL).astype(jnp.bfloat16)

    lat_copy.wait()
    lat = lat_buf[...].astype(jnp.float32).reshape(pages, 2, piece, lat_w)
    lat = jnp.where(head % 2 == 1, lat[:, 1], lat[:, 0]).reshape(pages * piece, lat_w)
    lat = lat.astype(jnp.bfloat16)
    step = count // chunks
    copies = []
    for i in range(chunks):
        rows = step * per_pair * piece
        value = dot(ones_where(iota((rows, 1), 0) + i * rows == place), lat)
        value = [
            value[:, c * TAIL : (c + 1) * TAIL].reshape(step * per_pair, 1, piece, TAIL)
            for c in range(cuts)
        ]
        value = jnp.concatenate(value, axis=1).reshape(step, lat_rows, TAIL)
        here = pl.ds(i * step, step)
        buf_ref[here, :lat_rows, :] = value.astype(jnp.bfloat16)
        copy = pltpu.make_async_copy(buf_ref.at[here], out_hbm.at[here], out_sem.at[i])
        copy.start()
        copies.append(copy)
    for copy in copies:
        copy.wait()


def split3(x):
    hi = x.astype(jnp.bfloat16)
    rest = x - hi.astype(jnp.float32)
    mid = rest.astype(jnp.bfloat16)
    low = (rest - mid.astype(jnp.float32)).astype(jnp.bfloat16)
    return hi.astype(jnp.float32), mid.astype(jnp.float32), low.astype(jnp.float32)


def query_kernel(
    scale, rows, qn_ref, qtail_ref, w_ref, fresh_ref, fresh_t_ref, q_ref, swap_ref, part_ref, lse_ref, acc_ref
):
    heads, width, _ = qn_ref.shape
    lat_w = w_ref.shape[2]
    steps = width // rows
    for head in range(heads):
        absorbed = dot(qn_ref[head], w_ref[head])
        for row in range(rows):
            at = (row * heads + head) * steps
            acc_ref[at : at + steps, :] = absorbed[row * steps : (row + 1) * steps]
    half = rows * heads * steps // 2
    absorbed = acc_ref[...].T
    tail = qtail_ref[...].astype(jnp.float32).T
    q_ref[:lat_w, :] = absorbed.astype(jnp.bfloat16)
    q_ref[lat_w:, :] = tail.astype(jnp.bfloat16)
    swap_ref[:lat_w, :] = pltpu.roll(absorbed, half, 1).astype(jnp.bfloat16)
    swap_ref[lat_w:, :] = pltpu.roll(tail, half, 1).astype(jnp.bfloat16)
    scores = dot(fresh_ref[...], q_ref[...]) * scale
    shape = scores.shape
    token = iota(shape, 0)
    query = iota(shape, 1)
    allowed = (query // (heads * steps) == token % rows) & (token // rows <= query % steps)
    scores = jnp.where(allowed, scores, NEG)
    high = jnp.max(scores, axis=0, keepdims=True)
    weights = jnp.exp(scores - high)
    total = jnp.sum(weights, axis=0, keepdims=True)
    part_ref[...] = dot(fresh_t_ref[...], weights.astype(jnp.bfloat16)) * (1.0 / total)
    lse_ref[...] = jnp.broadcast_to(high + jnp.log(total), lse_ref.shape)


def gather_kernel(piece, per_pair, rope_w, pages_row, block_ref, bias_ref, key_ref):
    rows, per_row, key_w = key_ref.shape
    count, block, _ = block_ref.shape
    cuts = (key_w - TAIL) // TAIL
    lat_w = cuts * TAIL
    pair_tokens = per_pair * piece
    lat_rows = pair_tokens * cuts
    rest = block - lat_rows
    rope_rows = piece * rope_w // TAIL
    half = per_row // 2

    tail = block_ref[:, lat_rows:, :].astype(jnp.float32)
    marked = iota(tail.shape, 1) == per_pair * rope_rows
    labels = jnp.sum(jnp.where(marked, tail, 0.0), axis=1).astype(jnp.bfloat16)

    def slot_of(columns, group, lane):
        spread = ones_where(iota((TAIL, columns), 0) == lane)
        wide = dot(labels, spread)
        own = iota((count, columns), 0) == iota((1, columns), 1) // group
        return jnp.sum(jnp.where(own, wide, 0.0), axis=0, keepdims=True).astype(jnp.int32) - 1

    columns = count * pair_tokens
    inner = iota((1, columns), 1) % pair_tokens
    slot = slot_of(columns, pair_tokens, inner)
    token = inner % piece
    row = (slot >= pages_row).astype(jnp.int32)
    target = row * (per_row - pages_row * (piece // 2)) + token % 2 * half
    target = target + slot * (piece // 2) + token // 2
    target = jnp.where(slot >= 0, target, -1)
    lat = block_ref[:, :lat_rows, :].astype(jnp.float32)
    lat = lat.reshape(count * per_pair, cuts, piece, TAIL)
    lat = [lat[:, c].reshape(count * pair_tokens, TAIL) for c in range(cuts)]
    lat = jnp.concatenate(lat, axis=1).astype(jnp.bfloat16)
    for b in range(rows):
        pick = ones_where(iota((per_row, 1), 0) + b * per_row == target)
        key_ref[b, :, :lat_w] = dot(pick, lat).astype(jnp.bfloat16)

    columns = count * rest
    inner = iota((1, columns), 1) % rest
    lane = jnp.where(inner < per_pair * rope_rows, inner // rope_rows * piece, TAIL)
    slot = slot_of(columns, rest, lane)
    target = jnp.where(slot >= 0, slot * rope_rows + inner % rope_rows, -1)
    tail = tail.reshape(columns, TAIL).astype(jnp.bfloat16)
    rope = dot(ones_where(iota((rows * half, 1), 0) == target), tail)
    for b in range(rows):
        rope_b = rope[b * half : (b + 1) * half]
        rope_b = jnp.concatenate([rope_b, pltpu.roll(rope_b, TAIL - rope_w, 1)], axis=0)
        lane = iota(rope_b.shape, 1)
        bias = bias_ref[b * per_row : (b + 1) * per_row]
        rope_b = jnp.where(lane < rope_w, rope_b, jnp.where(lane == rope_w, bias, 0.0))
        key_ref[b, :, lat_w:] = rope_b.astype(jnp.bfloat16)


def attend(scale, key, query, lat_w):
    scores = dot(key, query)
    high = jnp.max(scores, axis=0, keepdims=True)
    weights = jnp.exp2((scores - high) * (scale * LOG2E))
    total = jnp.sum(weights, axis=0, keepdims=True)
    return high, total, dot(key[:, :lat_w].T, weights.astype(jnp.bfloat16))


def ask(q_refs, b):
    left = iota(q_refs[0].shape, 1) < q_refs[0].shape[1] // 2
    tiles = []
    for k in range(0, len(q_refs), 2):
        one, two = q_refs[k][...].astype(jnp.float32), q_refs[k + 1][...].astype(jnp.float32)
        first, second = (one, two) if b == 0 else (two, one)
        tiles.append(jnp.where(left, first, second).astype(jnp.bfloat16))
    return jnp.concatenate(tiles, axis=1)


def own_kernel(scale, key_ref, *refs):
    q_refs, (part_ref, stat_ref) = refs[:-2], refs[-2:]
    for b in range(key_ref.shape[0]):
        high, total, part = attend(scale, key_ref[b], ask(q_refs, b), part_ref.shape[1])
        part_ref[b] = part
        stat_ref[b] = jnp.where(iota(stat_ref.shape[1:], 0) == 0, high, total)


def both_kernel(scale, key_ref, own_ref, stat_ref, *refs):
    count = len(refs) // 2
    q_refs, out_refs = refs[:count], refs[count:]
    lat_w = own_ref.shape[1]
    queries = q_refs[0].shape[1]
    parts = []
    for b in range(key_ref.shape[0]):
        high, total, part = attend(scale, key_ref[b], ask(q_refs, b), lat_w)
        high_own, total_own = stat_ref[b, 0:1], stat_ref[b, 1:2]
        top = jnp.maximum(high, high_own)
        keep = jnp.exp2((high - top) * (scale * LOG2E))
        keep_own = jnp.exp2((high_own - top) * (scale * LOG2E))
        total = total * keep + total_own * keep_own
        inverse = 1.0 / total
        part = part * (keep * inverse) + own_ref[b] * (keep_own * inverse)
        hi, mid, low = split3(top * scale + jnp.log(total))
        mark = iota((INFO, part.shape[1]), 0)
        info = jnp.where(mark == 0, hi, jnp.where(mark == 1, mid, jnp.where(mark == 2, low, 0.0)))
        parts.append(jnp.concatenate([part, info], axis=0))
    left = iota((lat_w + INFO, queries), 1) < queries // 2
    for k in range(0, count, 2):
        lanes = slice(k * queries // 2, (k + 2) * queries // 2)
        one, two = parts[0][:, lanes], parts[1][:, lanes]
        out_refs[k][...] = jnp.where(left, one, two).astype(jnp.bfloat16)
        out_refs[k + 1][...] = jnp.where(left, two, one).astype(jnp.bfloat16)


def merge_kernel(rows_dev, fresh_ref, fresh_lse_ref, w_ref, *refs):
    part_refs, out_ref, lat_ref = refs[:-2], refs[-2], refs[-1]
    heads, lat_w, value_w = w_ref.shape
    width = out_ref.shape[1]
    steps = width // rows_dev
    half = fresh_ref.shape[1] // 2
    lses = [fresh_lse_ref[...]]
    for k, part_ref in enumerate(part_refs):
        info = jnp.sum(part_ref[lat_w:, :].astype(jnp.float32), axis=0, keepdims=True)
        info = jnp.broadcast_to(info, lses[0].shape)
        lses.append(pltpu.roll(info, half, 1) if k % 2 else info)
    high = functools.reduce(jnp.maximum, lses)
    shares = [jnp.exp(lse - high) for lse in lses]
    inverse = 1.0 / functools.reduce(jnp.add, shares)
    total = fresh_ref[...] * (shares[0] * inverse)[:1]
    swapped = 0.0
    for k, part_ref in enumerate(part_refs):
        share = shares[k + 1] * inverse
        part = part_ref[:lat_w, :].astype(jnp.float32)
        if k % 2:
            swapped = swapped + part * pltpu.roll(share, half, 1)[:1]
        else:
            total = total + part * share[:1]
    total = total + pltpu.roll(swapped, half, 1)
    shape = (heads * width, heads * width)
    to, at = iota(shape, 0), iota(shape, 1)
    wanted = (to % rows_dev * heads + to // width) * steps + to % width // rows_dev
    lat_ref[...] = dot_t(ones_where(at == wanted), total.astype(jnp.bfloat16))
    for head in range(heads):
        rows = lat_ref[head * width : (head + 1) * width, :].astype(jnp.bfloat16)
        value = dot(rows, w_ref[head]).astype(jnp.bfloat16)
        for copy in range(out_ref.shape[0]):
            out_ref[copy, :, head * value_w : (head + 1) * value_w] = value


def project_kernel(width, x_ref, own_ref, near_ref, far_ref, opp_a_ref, opp_b_ref, out_ref):
    per_core = out_ref.shape[1]
    cores = out_ref.shape[0] // NX
    here = lax.axis_index("row") // NZ
    depth = x_ref.shape[1] // 2

    def put(k, block):
        owner = (here - k + NX) % NX
        for core in range(cores):
            for i in range(per_core):
                first = (core * per_core + i) * width
                out_ref[owner * cores + core, i] = block[first : first + width]

    put(0, dot_t(x_ref[...], own_ref[...]))
    put(1, dot_t(x_ref[...], near_ref[...]))
    put(NX - 1, dot_t(x_ref[...], far_ref[...]))
    opposite = dot_t(x_ref[:, :depth], opp_a_ref[...]) + dot_t(x_ref[:, depth:], opp_b_ref[...])
    put(NX // 2, opposite)


def sum_kernel(in_ref, *outs):
    count = len(outs)
    for j in range(count):
        i = (lax.axis_index("row") + j) % count
        parts = [in_ref[k, i] for k in range(in_ref.shape[0])]
        outs[j][...] = functools.reduce(jnp.add, parts).astype(outs[j].dtype)


def shift_y(x, n_head, k):
    cores = n_head // NX
    if k % NX == 0:
        return x
    return lax.ppermute(x, "head", [(h, (h + k * cores) % n_head) for h in range(n_head)])


def shift_x(x, k):
    return lax.ppermute(
        x,
        "row",
        [(a * NZ + b, (a + k) % NX * NZ + b) for a in range(NX) for b in range(NZ)],
    )


def on_device(
    q_nope,
    q_rope,
    new_latent,
    new_rope,
    latent_pages,
    rope_pages,
    dest_rows,
    dest_slots,
    page_table,
    lengths,
    w_uk,
    w_uv,
    w_o,
):
    bf16, f32 = jnp.bfloat16, jnp.float32
    n_row = lax.axis_size("row")
    n_head = lax.axis_size("head")
    row, head = lax.axis_index("row"), lax.axis_index("head")
    rows_dev, pages_row = page_table.shape
    pages, page_len, lat_w = latent_pages.shape
    rope_w = new_rope.shape[-1]
    steps, _, heads, nope_w = q_nope.shape
    value_w = w_uv.shape[-1]
    piece = page_len // n_head
    per_pair = 2 * (pages // n_row) + min(pages % n_row, 1)
    scale = 1.0 / (nope_w + rope_w) ** 0.5
    width = steps * rows_dev
    queries = heads * width
    tokens = pages * piece
    slots = n_row * per_pair * piece

    lat_rows = per_pair * piece * lat_w // TAIL
    rope_rows = per_pair * piece * rope_w // TAIL
    block = lat_rows + (rope_rows + 8) // 8 * 8
    send = call(
        functools.partial(pack_kernel, rows_dev, pages_row, per_pair),
        jax.ShapeDtypeStruct((n_row, block, TAIL), bf16),
        [dest_rows[None, :], dest_slots[None, :], latent_pages, rope_pages],
        scratch=[
            pltpu.VMEM((pages, 2 * piece, lat_w), bf16),
            pltpu.VMEM((pages, piece * rope_w), bf16),
            pltpu.VMEM((n_row, block, TAIL), bf16),
            pltpu.SemaphoreType.DMA((2,)),
            pltpu.SemaphoreType.DMA((4,)),
        ],
        flops=2 * slots * tokens * lat_w,
        nbytes=2 * (slots + 2 * tokens) * lat_w,
        mem=60,
        out_spec=HBM,
        in_hbm=(2, 3),
    )
    got = lax.all_to_all(send, "row", split_axis=0, concat_axis=0, tiled=True)

    qn = jnp.transpose(q_nope, (2, 1, 0, 3)).reshape(heads, width, nope_w)
    qr = q_rope.reshape(steps, rows_dev, heads, rope_w)
    qr = jnp.transpose(qr, (1, 2, 0, 3)).reshape(queries, rope_w)
    one_lane = jnp.arange(TAIL - rope_w, dtype=jnp.int32)[None, :] == 0
    q_tail = jnp.concatenate(
        [qr, jnp.broadcast_to(one_lane, (queries, TAIL - rope_w)).astype(bf16)], axis=1
    )
    fresh = jnp.concatenate(
        [
            new_latent.reshape(width, lat_w),
            new_rope.reshape(width, rope_w),
            jnp.zeros((width, TAIL - rope_w), bf16),
        ],
        axis=1,
    )
    fresh = jnp.concatenate([fresh, jnp.zeros((-width % 16, lat_w + TAIL), bf16)], axis=0)
    query, swapped, fresh_part, fresh_lse = call(
        functools.partial(query_kernel, scale, rows_dev),
        (
            jax.ShapeDtypeStruct((lat_w + TAIL, queries), bf16),
            jax.ShapeDtypeStruct((lat_w + TAIL, queries), bf16),
            jax.ShapeDtypeStruct((lat_w, queries), f32),
            jax.ShapeDtypeStruct((8, queries), f32),
        ),
        [qn, q_tail, w_uk, fresh, fresh[:, :lat_w].T],
        scratch=[pltpu.VMEM((queries, lat_w), f32)],
        flops=2 * queries * nope_w * lat_w,
        nbytes=2 * heads * nope_w * lat_w,
    )
    all_queries = [shift_y((query, swapped)[k % 2], n_head, k) for k in range(NX)]

    w_t = w_o.T
    w_near, w_far = shift_x(w_t, 1), shift_x(w_t, -1)
    depth = w_t.shape[1] // 2

    slot_ids = jnp.arange(pages_row, dtype=jnp.int32)
    holds = (page_table[:, :, None] == slot_ids[None, None, :]).astype(jnp.int32)
    logical = jnp.sum(holds * slot_ids[None, :, None], axis=1)
    limit = lengths[:, None] - logical * page_len - head * piece
    within = jnp.arange(piece, dtype=jnp.int32).reshape(piece // 2, 2).T
    usable = within[None, :, None, :] < limit[:, None, :, None]
    bias = jnp.where(usable, 0.0, NEG).astype(f32).reshape(rows_dev * pages_row * piece, 1)

    got, w_near, w_far = lax.optimization_barrier((got, w_near, w_far))
    w_cols = [
        w_t,
        w_near,
        w_far,
        shift_x(w_near[:, :depth], 1),
        shift_x(w_far[:, depth:], -1),
    ]
    key = call(
        functools.partial(gather_kernel, piece, per_pair, rope_w, pages_row),
        jax.ShapeDtypeStruct((rows_dev, pages_row * piece, lat_w + TAIL), bf16),
        [got, bias],
        flops=2 * slots * tokens * lat_w,
        nbytes=2 * slots * lat_w,
    )
    other = lax.ppermute(key, "head", [(h, h ^ 1) for h in range(n_head)])
    asked = NX * queries // rows_dev
    own_part, own_stat = call(
        functools.partial(own_kernel, scale),
        (
            jax.ShapeDtypeStruct((rows_dev, lat_w, asked), f32),
            jax.ShapeDtypeStruct((rows_dev, 8, asked), f32),
        ),
        [key] + all_queries,
        flops=2 * tokens * asked * (2 * lat_w + TAIL),
        nbytes=2 * tokens * lat_w,
    )
    parts = call(
        functools.partial(both_kernel, scale),
        tuple(jax.ShapeDtypeStruct((lat_w + INFO, queries), bf16) for _ in range(NX)),
        [other, own_part, own_stat] + all_queries,
        flops=2 * tokens * asked * (2 * lat_w + TAIL),
        nbytes=2 * tokens * lat_w,
    )
    parts = [shift_y(part, n_head, -k) for k, part in enumerate(parts)]
    head_out = call(
        functools.partial(merge_kernel, rows_dev),
        jax.ShapeDtypeStruct((NZ, width, heads * value_w), bf16),
        [fresh_part, fresh_lse, w_uv] + parts,
        scratch=[pltpu.VMEM((queries, lat_w), f32)],
        flops=2 * queries * lat_w * value_w,
        nbytes=2 * heads * lat_w * value_w,
    )

    rings = [[a * NZ + b for b in range(NZ)] for a in range(NX)]
    ring = lax.all_to_all(
        head_out, "row", split_axis=0, concat_axis=0, axis_index_groups=rings, tiled=True
    )
    cols = w_o.shape[1]
    cores = n_head // NX
    per_core = NZ // cores
    sums = call(
        functools.partial(project_kernel, width),
        jax.ShapeDtypeStruct((n_head, per_core, width, cols), f32),
        [ring.reshape(NZ * width, heads * value_w)] + w_cols,
        flops=2 * NX * NZ * width * w_o.size,
        nbytes=2 * NX * w_o.size,
    )
    sums = lax.all_to_all(sums, "head", split_axis=0, concat_axis=0, tiled=True)
    pieces = call(
        sum_kernel,
        tuple(jax.ShapeDtypeStruct((width, cols), bf16) for _ in range(per_core)),
        [sums],
    )
    moved = []
    for j in range(per_core):
        pairs = []
        for r in range(n_row):
            for h in range(n_head):
                ring_at, (a, i) = r // NZ, divmod(r % NZ, per_core)
                y, c = divmod(h, cores)
                to_row = ring_at * NZ + c * per_core + (i + j) % per_core
                pairs.append((r * n_head + h, to_row * n_head + y * cores + a))
        moved.append(lax.ppermute(pieces[j], ("row", "head"), pairs))
    blocks = []
    for i in range(per_core):
        turn = (row - i) % per_core
        block = moved[0]
        for j in range(1, per_core):
            block = jnp.where(turn == j, moved[j], block)
        blocks.append(block)
    out = jnp.concatenate(blocks, axis=1)
    return out.reshape(steps, rows_dev, per_core * cols)


def solution(mesh):
    placed = (
        P(None, "row", "head", None),
        P(None, "row", "head"),
        P(None, "row", None),
        P(None, "row", None),
        P("row", None, None),
        P("row", None),
        P("row"),
        P("row"),
        P("row", None),
        P("row"),
        P("head", None, None),
        P("head", None, None),
        P("head", "row"),
    )
    return jax.shard_map(
        on_device, mesh=mesh, in_specs=placed, out_specs=P(None, "row", "head"), check_vma=False
    )
```

```python
import functools

import jax
import jax.numpy as jnp
from jax import lax
from jax.experimental import pallas as pl
from jax.experimental.pallas import tpu as pltpu
from jax.sharding import PartitionSpec as P

NX = 4
NZ = 8
TAIL = 128
INFO = 16
NEG = -1e30
LOG2E = 1.4426950408889634
LN2 = 0.6931471805599453

VMEM = pl.BlockSpec(memory_space=pltpu.VMEM)
SMEM = pl.BlockSpec(memory_space=pltpu.SMEM)
HBM = pl.BlockSpec(memory_space=pltpu.HBM)


def call(
    body, out_shape, ins, scratch=(), flops=0, nbytes=0, mem=24, out_spec=VMEM, in_hbm=()
):
    return pl.pallas_call(
        body,
        out_shape=out_shape,
        in_specs=[
            HBM if i in in_hbm else SMEM if a.dtype == jnp.int32 and a.ndim == 1 else VMEM
            for i, a in enumerate(ins)
        ],
        out_specs=jax.tree.map(lambda _: out_spec, out_shape),
        scratch_shapes=list(scratch),
        compiler_params=pltpu.CompilerParams(vmem_limit_bytes=mem * 2**20),
        cost_estimate=pl.CostEstimate(flops=flops, bytes_accessed=nbytes, transcendentals=0),
    )(*ins)


def dot(a, b):
    return lax.dot_general(a, b, (((1,), (0,)), ((), ())), preferred_element_type=jnp.float32)


def dot_t(a, b):
    return lax.dot_general(a, b, (((1,), (1,)), ((), ())), preferred_element_type=jnp.float32)


def iota(shape, dim):
    return lax.broadcasted_iota(jnp.int32, shape, dim)


def ones_where(mask):
    return jnp.where(mask, 1.0, 0.0).astype(jnp.bfloat16)


def pack_kernel(
    rows_dev,
    pages_row,
    per_pair,
    rows_ref,
    slots_ref,
    lat_hbm,
    rope_hbm,
    out_hbm,
    lat_buf,
    rope_buf,
    buf_ref,
    in_sem,
    out_sem,
):
    pages, both, lat_w = lat_buf.shape
    piece = both // 2
    count, block, _ = buf_ref.shape
    chunks = out_sem.shape[0]
    cuts = lat_w // TAIL
    rope_rows = rope_buf.shape[1] // TAIL
    lat_rows = per_pair * cuts * piece
    head = lax.axis_index("head")
    first = pl.multiple_of(head // 2 * both, both)
    lat_copy = pltpu.make_async_copy(lat_hbm.at[:, pl.ds(first, both), :], lat_buf, in_sem.at[0])
    lat_copy.start()
    lane0 = pl.multiple_of(head * rope_buf.shape[1], rope_buf.shape[1])
    rope_copy = pltpu.make_async_copy(
        rope_hbm.at[:, pl.ds(lane0, rope_buf.shape[1])], rope_buf, in_sem.at[1]
    )
    rope_copy.start()

    dest = rows_ref[...] // rows_dev
    label = (rows_ref[...] % rows_dev * pages_row + slots_ref[...] + 1).astype(jnp.float32)
    owned = jnp.where(iota((count, pages), 0) == dest, 1.0, 0.0)
    before = ones_where(iota((pages, pages), 0) < iota((pages, pages), 1))
    rank = jnp.sum(owned * dot(owned.astype(jnp.bfloat16), before), axis=0, keepdims=True)
    rank = rank.astype(jnp.int32)
    at_slot = (dest * per_pair + rank).astype(jnp.float32).astype(jnp.bfloat16)
    spread = ones_where(iota((pages, pages * piece), 0) == iota((pages, pages * piece), 1) // piece)
    at_slot = dot(jnp.broadcast_to(at_slot, (8, pages)), spread)[:1].astype(jnp.int32)
    place = at_slot * piece + iota((1, pages * piece), 1) % piece

    label_lane = iota((TAIL, pages), 0)
    named = ones_where((label_lane // piece == rank) & (label_lane < per_pair * piece))
    labels = dot_t((owned * label).astype(jnp.bfloat16), named).astype(jnp.bfloat16)
    rest = block - lat_rows
    row = iota((count * rest, 1), 0)
    tail = dot(
        ones_where(row == iota((1, count), 1) * rest + per_pair * rope_rows), labels
    )
    rope_copy.wait()
    for j in range(rope_rows):
        pick = ones_where(row == dest * rest + rank * rope_rows + j)
        tail = tail + dot(pick, rope_buf[:, j * TAIL : (j + 1) * TAIL])
    buf_ref[:, lat_rows:, :] = tail.reshape(count, rest, TAIL).astype(jnp.bfloat16)

    lat_copy.wait()
    lat = lat_buf[...].astype(jnp.float32).reshape(pages, 2, piece, lat_w)
    lat = jnp.where(head % 2 == 1, lat[:, 1], lat[:, 0]).reshape(pages * piece, lat_w)
    lat = lat.astype(jnp.bfloat16)
    step = count // chunks
    copies = []
    for i in range(chunks):
        rows = step * per_pair * piece
        value = dot(ones_where(iota((rows, 1), 0) + i * rows == place), lat)
        value = [
            value[:, c * TAIL : (c + 1) * TAIL].reshape(step * per_pair, 1, piece, TAIL)
            for c in range(cuts)
        ]
        value = jnp.concatenate(value, axis=1).reshape(step, lat_rows, TAIL)
        here = pl.ds(i * step, step)
        buf_ref[here, :lat_rows, :] = value.astype(jnp.bfloat16)
        copy = pltpu.make_async_copy(buf_ref.at[here], out_hbm.at[here], out_sem.at[i])
        copy.start()
        copies.append(copy)
    for copy in copies:
        copy.wait()


def split3(x):
    hi = x.astype(jnp.bfloat16)
    rest = x - hi.astype(jnp.float32)
    mid = rest.astype(jnp.bfloat16)
    low = (rest - mid.astype(jnp.float32)).astype(jnp.bfloat16)
    return hi.astype(jnp.float32), mid.astype(jnp.float32), low.astype(jnp.float32)


def query_kernel(
    scale, rows, qn_ref, qtail_ref, w_ref, fresh_ref, fresh_t_ref, q_ref, swap_ref, part_ref, lse_ref, acc_ref
):
    heads, width, _ = qn_ref.shape
    lat_w = w_ref.shape[2]
    steps = width // rows
    for head in range(heads):
        absorbed = dot(qn_ref[head], w_ref[head])
        for row in range(rows):
            at = (row * heads + head) * steps
            acc_ref[at : at + steps, :] = absorbed[row * steps : (row + 1) * steps]
    half = rows * heads * steps // 2
    absorbed = acc_ref[...].T
    tail = qtail_ref[...].astype(jnp.float32).T
    q_ref[:lat_w, :] = absorbed.astype(jnp.bfloat16)
    q_ref[lat_w:, :] = tail.astype(jnp.bfloat16)
    swap_ref[:lat_w, :] = pltpu.roll(absorbed, half, 1).astype(jnp.bfloat16)
    swap_ref[lat_w:, :] = pltpu.roll(tail, half, 1).astype(jnp.bfloat16)
    scores = dot(fresh_ref[...], q_ref[...]) * scale
    shape = scores.shape
    token = iota(shape, 0)
    query = iota(shape, 1)
    allowed = (query // (heads * steps) == token % rows) & (token // rows <= query % steps)
    scores = jnp.where(allowed, scores, NEG)
    high = jnp.max(scores, axis=0, keepdims=True)
    weights = jnp.exp(scores - high)
    total = jnp.sum(weights, axis=0, keepdims=True)
    part_ref[...] = dot(fresh_t_ref[...], weights.astype(jnp.bfloat16)) * (1.0 / total)
    lse_ref[...] = jnp.broadcast_to(high + jnp.log(total), lse_ref.shape)


def gather_kernel(
    piece,
    per_pair,
    rope_w,
    pages_row,
    block_hbm,
    bias_ref,
    key_hbm,
    block_ref,
    lat_ref,
    tail_ref,
    key_ref,
    in_sem,
    out_sem,
):
    rows, per_row, key_w = key_ref.shape
    count, block, _ = block_ref.shape
    cuts = (key_w - TAIL) // TAIL
    lat_w = cuts * TAIL
    pair_tokens = per_pair * piece
    lat_rows = pair_tokens * cuts
    rest = block - lat_rows
    rope_rows = piece * rope_w // TAIL
    half = per_row // 2

    chunks = in_sem.shape[0]
    step = count // chunks
    copies = []
    for i in range(chunks):
        here = pl.ds(i * step, step)
        copy = pltpu.make_async_copy(block_hbm.at[here], block_ref.at[here], in_sem.at[i])
        copy.start()
        copies.append(copy)
    labels = []
    for i, copy in enumerate(copies):
        copy.wait()
        here = slice(i * step, (i + 1) * step)
        tail = block_ref[here, lat_rows:, :].astype(jnp.float32)
        marked = iota(tail.shape, 1) == per_pair * rope_rows
        labels.append(jnp.sum(jnp.where(marked, tail, 0.0), axis=1))
        tail_ref[i * step * rest : (i + 1) * step * rest, :] = tail.reshape(
            step * rest, TAIL
        ).astype(jnp.bfloat16)
        lat = block_ref[here, :lat_rows, :].astype(jnp.float32)
        lat = lat.reshape(step * per_pair, cuts, piece, TAIL)
        for c in range(cuts):
            lat_ref[i * step * pair_tokens : (i + 1) * step * pair_tokens, pl.ds(c * TAIL, TAIL)] = (
                lat[:, c].reshape(step * pair_tokens, TAIL).astype(jnp.bfloat16)
            )
    labels = jnp.concatenate(labels, axis=0).astype(jnp.bfloat16)

    def slot_of(columns, group, lane):
        spread = ones_where(iota((TAIL, columns), 0) == lane)
        wide = dot(labels, spread)
        own = iota((count, columns), 0) == iota((1, columns), 1) // group
        return jnp.sum(jnp.where(own, wide, 0.0), axis=0, keepdims=True).astype(jnp.int32) - 1

    columns = count * pair_tokens
    inner = iota((1, columns), 1) % pair_tokens
    slot = slot_of(columns, pair_tokens, inner)
    token = inner % piece
    row = (slot >= pages_row).astype(jnp.int32)
    target = row * (per_row - pages_row * (piece // 2)) + token % 2 * half
    target = target + slot * (piece // 2) + token // 2
    target = jnp.where(slot >= 0, target, -1)
    columns = count * rest
    inner = iota((1, columns), 1) % rest
    lane = jnp.where(inner < per_pair * rope_rows, inner // rope_rows * piece, TAIL)
    slot = slot_of(columns, rest, lane)
    rope_target = jnp.where(slot >= 0, slot * rope_rows + inner % rope_rows, -1)
    copies = []
    for b in range(rows):
        pick = ones_where(iota((half, 1), 0) + b * half == rope_target)
        rope_b = dot(pick, tail_ref[...])
        rope_b = jnp.concatenate([rope_b, pltpu.roll(rope_b, TAIL - rope_w, 1)], axis=0)
        lane = iota(rope_b.shape, 1)
        bias = bias_ref[b * per_row : (b + 1) * per_row]
        rope_b = jnp.where(lane < rope_w, rope_b, jnp.where(lane == rope_w, bias, 0.0))
        key_ref[b, :, lat_w:] = rope_b.astype(jnp.bfloat16)
        pick = ones_where(iota((per_row, 1), 0) + b * per_row == target)
        key_ref[b, :, :lat_w] = dot(pick, lat_ref[...]).astype(jnp.bfloat16)
        copy = pltpu.make_async_copy(key_ref.at[b], key_hbm.at[b], out_sem.at[b])
        copy.start()
        copies.append(copy)
    for copy in copies:
        copy.wait()


def attend(scale, key, query, lat_w):
    scores = dot(key, query)
    high = jnp.max(scores, axis=0, keepdims=True)
    weights = jnp.exp2((scores - high) * (scale * LOG2E))
    total = jnp.sum(weights, axis=0, keepdims=True)
    return high, total, dot(key[:, :lat_w].T, weights.astype(jnp.bfloat16))


def ask(q_refs, b):
    left = iota(q_refs[0].shape, 1) < q_refs[0].shape[1] // 2
    tiles = []
    for k in range(0, len(q_refs), 2):
        one, two = q_refs[k][...].astype(jnp.float32), q_refs[k + 1][...].astype(jnp.float32)
        first, second = (one, two) if b == 0 else (two, one)
        tiles.append(jnp.where(left, first, second).astype(jnp.bfloat16))
    return jnp.concatenate(tiles, axis=1)


def own_kernel(scale, key_ref, *refs):
    q_refs, (part_ref, stat_ref) = refs[:-2], refs[-2:]
    for b in range(key_ref.shape[0]):
        high, total, part = attend(scale, key_ref[b], ask(q_refs, b), part_ref.shape[1])
        part_ref[b] = part
        stat_ref[b] = jnp.where(iota(stat_ref.shape[1:], 0) == 0, high, total)


def both_kernel(scale, key_ref, own_ref, stat_ref, *refs):
    count = len(refs) // 2
    q_refs, out_refs = refs[:count], refs[count:]
    lat_w = own_ref.shape[1]
    queries = q_refs[0].shape[1]
    parts = []
    for b in range(key_ref.shape[0]):
        high, total, part = attend(scale, key_ref[b], ask(q_refs, b), lat_w)
        high_own, total_own = stat_ref[b, 0:1], stat_ref[b, 1:2]
        top = jnp.maximum(high, high_own)
        keep = jnp.exp2((high - top) * (scale * LOG2E))
        keep_own = jnp.exp2((high_own - top) * (scale * LOG2E))
        total = total * keep + total_own * keep_own
        inverse = 1.0 / total
        part = part * (keep * inverse) + own_ref[b] * (keep_own * inverse)
        hi, mid, low = split3(top * scale + jnp.log(total))
        mark = iota((INFO, part.shape[1]), 0)
        info = jnp.where(mark == 0, hi, jnp.where(mark == 1, mid, jnp.where(mark == 2, low, 0.0)))
        parts.append(jnp.concatenate([part, info], axis=0))
    left = iota((lat_w + INFO, queries), 1) < queries // 2
    for k in range(0, count, 2):
        lanes = slice(k * queries // 2, (k + 2) * queries // 2)
        one, two = parts[0][:, lanes], parts[1][:, lanes]
        out_refs[k][...] = jnp.where(left, one, two).astype(jnp.bfloat16)
        out_refs[k + 1][...] = jnp.where(left, two, one).astype(jnp.bfloat16)


def merge_kernel(rows_dev, fresh_ref, fresh_lse_ref, w_ref, *refs):
    part_refs, out_ref, lat_ref = refs[:-2], refs[-2], refs[-1]
    heads, lat_w, value_w = w_ref.shape
    width = out_ref.shape[1]
    steps = width // rows_dev
    half = fresh_ref.shape[1] // 2
    lses = [fresh_lse_ref[...]]
    for k, part_ref in enumerate(part_refs):
        info = jnp.sum(part_ref[lat_w:, :].astype(jnp.float32), axis=0, keepdims=True)
        info = jnp.broadcast_to(info, lses[0].shape)
        lses.append(pltpu.roll(info, half, 1) if k % 2 else info)
    high = functools.reduce(jnp.maximum, lses)
    shares = [jnp.exp(lse - high) for lse in lses]
    inverse = 1.0 / functools.reduce(jnp.add, shares)
    total = fresh_ref[...] * (shares[0] * inverse)[:1]
    swapped = 0.0
    for k, part_ref in enumerate(part_refs):
        share = shares[k + 1] * inverse
        part = part_ref[:lat_w, :].astype(jnp.float32)
        if k % 2:
            swapped = swapped + part * pltpu.roll(share, half, 1)[:1]
        else:
            total = total + part * share[:1]
    total = total + pltpu.roll(swapped, half, 1)
    shape = (heads * width, heads * width)
    to, at = iota(shape, 0), iota(shape, 1)
    wanted = (to % rows_dev * heads + to // width) * steps + to % width // rows_dev
    lat_ref[...] = dot_t(ones_where(at == wanted), total.astype(jnp.bfloat16))
    for head in range(heads):
        rows = lat_ref[head * width : (head + 1) * width, :].astype(jnp.bfloat16)
        value = dot(rows, w_ref[head]).astype(jnp.bfloat16)
        for copy in range(out_ref.shape[0]):
            out_ref[copy, :, head * value_w : (head + 1) * value_w] = value


def project_kernel(width, x_ref, *refs):
    w_hbm, out_ref, w_refs, sem_ref = refs[:5], refs[5], refs[6:11], refs[11]
    copies = [
        pltpu.make_async_copy(w_hbm[i], w_refs[i], sem_ref.at[i]) for i in range(len(w_refs))
    ]
    for copy in copies:
        copy.start()
    per_core = out_ref.shape[1]
    cores = out_ref.shape[0] // NX
    here = lax.axis_index("row") // NZ
    depth = x_ref.shape[1] // 2

    def put(k, block):
        owner = (here - k + NX) % NX
        for core in range(cores):
            for i in range(per_core):
                first = (core * per_core + i) * width
                out_ref[owner * cores + core, i] = block[first : first + width]

    for i, k in enumerate((0, 1, NX - 1)):
        copies[i].wait()
        put(k, dot_t(x_ref[...], w_refs[i][...]))
    copies[3].wait()
    opposite = dot_t(x_ref[:, :depth], w_refs[3][...])
    copies[4].wait()
    put(NX // 2, opposite + dot_t(x_ref[:, depth:], w_refs[4][...]))


def sum_kernel(in_ref, *outs):
    count = len(outs)
    for j in range(count):
        i = (lax.axis_index("row") + j) % count
        parts = [in_ref[k, i] for k in range(in_ref.shape[0])]
        outs[j][...] = functools.reduce(jnp.add, parts).astype(outs[j].dtype)


def shift_y(x, n_head, k):
    cores = n_head // NX
    if k % NX == 0:
        return x
    return lax.ppermute(x, "head", [(h, (h + k * cores) % n_head) for h in range(n_head)])


def shift_x(x, k):
    return lax.ppermute(
        x,
        "row",
        [(a * NZ + b, (a + k) % NX * NZ + b) for a in range(NX) for b in range(NZ)],
    )


def on_device(
    q_nope,
    q_rope,
    new_latent,
    new_rope,
    latent_pages,
    rope_pages,
    dest_rows,
    dest_slots,
    page_table,
    lengths,
    w_uk,
    w_uv,
    w_o,
):
    bf16, f32 = jnp.bfloat16, jnp.float32
    n_row = lax.axis_size("row")
    n_head = lax.axis_size("head")
    row, head = lax.axis_index("row"), lax.axis_index("head")
    rows_dev, pages_row = page_table.shape
    pages, page_len, lat_w = latent_pages.shape
    rope_w = new_rope.shape[-1]
    steps, _, heads, nope_w = q_nope.shape
    value_w = w_uv.shape[-1]
    piece = page_len // n_head
    per_pair = 2 * (pages // n_row) + min(pages % n_row, 1)
    scale = 1.0 / (nope_w + rope_w) ** 0.5
    width = steps * rows_dev
    queries = heads * width
    tokens = pages * piece
    slots = n_row * per_pair * piece

    lat_rows = per_pair * piece * lat_w // TAIL
    rope_rows = per_pair * piece * rope_w // TAIL
    block = lat_rows + (rope_rows + 8) // 8 * 8
    send = call(
        functools.partial(pack_kernel, rows_dev, pages_row, per_pair),
        jax.ShapeDtypeStruct((n_row, block, TAIL), bf16),
        [dest_rows[None, :], dest_slots[None, :], latent_pages, rope_pages],
        scratch=[
            pltpu.VMEM((pages, 2 * piece, lat_w), bf16),
            pltpu.VMEM((pages, piece * rope_w), bf16),
            pltpu.VMEM((n_row, block, TAIL), bf16),
            pltpu.SemaphoreType.DMA((2,)),
            pltpu.SemaphoreType.DMA((4,)),
        ],
        flops=2 * slots * tokens * lat_w,
        nbytes=2 * (slots + 2 * tokens) * lat_w,
        mem=60,
        out_spec=HBM,
        in_hbm=(2, 3),
    )
    got = lax.all_to_all(send, "row", split_axis=0, concat_axis=0, tiled=True)

    qn = jnp.transpose(q_nope, (2, 1, 0, 3)).reshape(heads, width, nope_w)
    qr = q_rope.reshape(steps, rows_dev, heads, rope_w)
    qr = jnp.transpose(qr, (1, 2, 0, 3)).reshape(queries, rope_w)
    one_lane = jnp.arange(TAIL - rope_w, dtype=jnp.int32)[None, :] == 0
    q_tail = jnp.concatenate(
        [qr, jnp.broadcast_to(one_lane, (queries, TAIL - rope_w)).astype(bf16)], axis=1
    )
    fresh = jnp.concatenate(
        [
            new_latent.reshape(width, lat_w),
            new_rope.reshape(width, rope_w),
            jnp.zeros((width, TAIL - rope_w), bf16),
        ],
        axis=1,
    )
    fresh = jnp.concatenate([fresh, jnp.zeros((-width % 16, lat_w + TAIL), bf16)], axis=0)
    query, swapped, fresh_part, fresh_lse = call(
        functools.partial(query_kernel, scale, rows_dev),
        (
            jax.ShapeDtypeStruct((lat_w + TAIL, queries), bf16),
            jax.ShapeDtypeStruct((lat_w + TAIL, queries), bf16),
            jax.ShapeDtypeStruct((lat_w, queries), f32),
            jax.ShapeDtypeStruct((8, queries), f32),
        ),
        [qn, q_tail, w_uk, fresh, fresh[:, :lat_w].T],
        scratch=[pltpu.VMEM((queries, lat_w), f32)],
        flops=2 * queries * nope_w * lat_w,
        nbytes=2 * heads * nope_w * lat_w,
    )
    all_queries = [shift_y((query, swapped)[k % 2], n_head, k) for k in range(NX)]

    w_t = w_o.T
    w_near, w_far = shift_x(w_t, 1), shift_x(w_t, -1)
    depth = w_t.shape[1] // 2

    slot_ids = jnp.arange(pages_row, dtype=jnp.int32)
    holds = (page_table[:, :, None] == slot_ids[None, None, :]).astype(jnp.int32)
    logical = jnp.sum(holds * slot_ids[None, :, None], axis=1)
    limit = lengths[:, None] - logical * page_len - head * piece
    within = jnp.arange(piece, dtype=jnp.int32).reshape(piece // 2, 2).T
    usable = within[None, :, None, :] < limit[:, None, :, None]
    bias = jnp.where(usable, 0.0, NEG).astype(f32).reshape(rows_dev * pages_row * piece, 1)

    got, w_near, w_far, all_queries = lax.optimization_barrier((got, w_near, w_far, all_queries))
    w_cols = [
        w_t,
        w_near,
        w_far,
        shift_x(w_near[:, :depth], 1),
        shift_x(w_far[:, depth:], -1),
    ]
    key = call(
        functools.partial(gather_kernel, piece, per_pair, rope_w, pages_row),
        jax.ShapeDtypeStruct((rows_dev, pages_row * piece, lat_w + TAIL), bf16),
        [got, bias],
        scratch=[
            pltpu.VMEM(got.shape, bf16),
            pltpu.VMEM((slots, lat_w), bf16),
            pltpu.VMEM((n_row * (block - lat_rows), TAIL), bf16),
            pltpu.VMEM((rows_dev, pages_row * piece, lat_w + TAIL), bf16),
            pltpu.SemaphoreType.DMA((4,)),
            pltpu.SemaphoreType.DMA((rows_dev,)),
        ],
        flops=2 * slots * tokens * lat_w,
        nbytes=2 * slots * lat_w,
        out_spec=HBM,
        in_hbm=(0,),
    )
    other = lax.ppermute(key, "head", [(h, h ^ 1) for h in range(n_head)])
    asked = NX * queries // rows_dev
    own_part, own_stat = call(
        functools.partial(own_kernel, scale),
        (
            jax.ShapeDtypeStruct((rows_dev, lat_w, asked), f32),
            jax.ShapeDtypeStruct((rows_dev, 8, asked), f32),
        ),
        [key] + all_queries,
        flops=2 * tokens * asked * (2 * lat_w + TAIL),
        nbytes=2 * tokens * lat_w,
    )
    parts = call(
        functools.partial(both_kernel, scale),
        tuple(jax.ShapeDtypeStruct((lat_w + INFO, queries), bf16) for _ in range(NX)),
        [other, own_part, own_stat] + all_queries,
        flops=2 * tokens * asked * (2 * lat_w + TAIL),
        nbytes=2 * tokens * lat_w,
    )
    parts = [shift_y(part, n_head, -k) for k, part in enumerate(parts)]
    head_out = call(
        functools.partial(merge_kernel, rows_dev),
        jax.ShapeDtypeStruct((NZ, width, heads * value_w), bf16),
        [fresh_part, fresh_lse, w_uv] + parts,
        scratch=[pltpu.VMEM((queries, lat_w), f32)],
        flops=2 * queries * lat_w * value_w,
        nbytes=2 * heads * lat_w * value_w,
    )

    rings = [[a * NZ + b for b in range(NZ)] for a in range(NX)]
    ring = lax.all_to_all(
        head_out, "row", split_axis=0, concat_axis=0, axis_index_groups=rings, tiled=True
    )
    cols = w_o.shape[1]
    cores = n_head // NX
    per_core = NZ // cores
    sums = call(
        functools.partial(project_kernel, width),
        jax.ShapeDtypeStruct((n_head, per_core, width, cols), f32),
        [ring.reshape(NZ * width, heads * value_w)] + w_cols,
        scratch=[pltpu.VMEM(w.shape, bf16) for w in w_cols] + [pltpu.SemaphoreType.DMA((5,))],
        flops=2 * NX * NZ * width * w_o.size,
        nbytes=2 * NX * w_o.size,
        in_hbm=(1, 2, 3, 4, 5),
    )
    sums = lax.all_to_all(sums, "head", split_axis=0, concat_axis=0, tiled=True)
    pieces = call(
        sum_kernel,
        tuple(jax.ShapeDtypeStruct((width, cols), bf16) for _ in range(per_core)),
        [sums],
    )
    moved = []
    for j in range(per_core):
        pairs = []
        for r in range(n_row):
            for h in range(n_head):
                ring_at, (a, i) = r // NZ, divmod(r % NZ, per_core)
                y, c = divmod(h, cores)
                to_row = ring_at * NZ + c * per_core + (i + j) % per_core
                pairs.append((r * n_head + h, to_row * n_head + y * cores + a))
        moved.append(lax.ppermute(pieces[j], ("row", "head"), pairs))
    blocks = []
    for i in range(per_core):
        turn = (row - i) % per_core
        block = moved[0]
        for j in range(1, per_core):
            block = jnp.where(turn == j, moved[j], block)
        blocks.append(block)
    out = jnp.concatenate(blocks, axis=1)
    return out.reshape(steps, rows_dev, per_core * cols)


def solution(mesh):
    placed = (
        P(None, "row", "head", None),
        P(None, "row", "head"),
        P(None, "row", None),
        P(None, "row", None),
        P("row", None, None),
        P("row", None),
        P("row"),
        P("row"),
        P("row", None),
        P("row"),
        P("head", None, None),
        P("head", None, None),
        P("head", "row"),
    )
    return jax.shard_map(
        on_device, mesh=mesh, in_specs=placed, out_specs=P(None, "row", "head"), check_vma=False
    )
```

```python
import functools

import jax
import jax.numpy as jnp
from jax import lax
from jax.experimental import pallas as pl
from jax.experimental.pallas import tpu as pltpu
from jax.sharding import PartitionSpec as P

NX = 4
NZ = 8
TAIL = 128
INFO = 16
NEG = -1e30
LOG2E = 1.4426950408889634
LN2 = 0.6931471805599453

VMEM = pl.BlockSpec(memory_space=pltpu.VMEM)
SMEM = pl.BlockSpec(memory_space=pltpu.SMEM)
HBM = pl.BlockSpec(memory_space=pltpu.HBM)


def call(
    body, out_shape, ins, scratch=(), flops=0, nbytes=0, mem=24, out_spec=VMEM, in_hbm=()
):
    return pl.pallas_call(
        body,
        out_shape=out_shape,
        in_specs=[
            HBM if i in in_hbm else SMEM if a.dtype == jnp.int32 and a.ndim == 1 else VMEM
            for i, a in enumerate(ins)
        ],
        out_specs=jax.tree.map(lambda _: out_spec, out_shape),
        scratch_shapes=list(scratch),
        compiler_params=pltpu.CompilerParams(vmem_limit_bytes=mem * 2**20),
        cost_estimate=pl.CostEstimate(flops=flops, bytes_accessed=nbytes, transcendentals=0),
    )(*ins)


def dot(a, b):
    return lax.dot_general(a, b, (((1,), (0,)), ((), ())), preferred_element_type=jnp.float32)


def dot_t(a, b):
    return lax.dot_general(a, b, (((1,), (1,)), ((), ())), preferred_element_type=jnp.float32)


def iota(shape, dim):
    return lax.broadcasted_iota(jnp.int32, shape, dim)


def ones_where(mask):
    return jnp.where(mask, 1.0, 0.0).astype(jnp.bfloat16)


def pack_kernel(
    rows_dev,
    pages_row,
    per_pair,
    rows_ref,
    slots_ref,
    lat_hbm,
    rope_hbm,
    out_hbm,
    lat_buf,
    rope_buf,
    buf_ref,
    in_sem,
    out_sem,
):
    pages, both, lat_w = lat_buf.shape
    piece = both // 2
    count, block, _ = buf_ref.shape
    chunks = out_sem.shape[0]
    cuts = lat_w // TAIL
    rope_rows = rope_buf.shape[1] // TAIL
    lat_rows = per_pair * cuts * piece
    head = lax.axis_index("head")
    first = pl.multiple_of(head // 2 * both, both)
    lat_copy = pltpu.make_async_copy(lat_hbm.at[:, pl.ds(first, both), :], lat_buf, in_sem.at[0])
    lat_copy.start()
    lane0 = pl.multiple_of(head * rope_buf.shape[1], rope_buf.shape[1])
    rope_copy = pltpu.make_async_copy(
        rope_hbm.at[:, pl.ds(lane0, rope_buf.shape[1])], rope_buf, in_sem.at[1]
    )
    rope_copy.start()

    dest = rows_ref[...] // rows_dev
    label = (rows_ref[...] % rows_dev * pages_row + slots_ref[...] + 1).astype(jnp.float32)
    owned = jnp.where(iota((count, pages), 0) == dest, 1.0, 0.0)
    before = ones_where(iota((pages, pages), 0) < iota((pages, pages), 1))
    rank = jnp.sum(owned * dot(owned.astype(jnp.bfloat16), before), axis=0, keepdims=True)
    rank = rank.astype(jnp.int32)
    at_slot = (dest * per_pair + rank).astype(jnp.float32).astype(jnp.bfloat16)
    spread = ones_where(iota((pages, pages * piece), 0) == iota((pages, pages * piece), 1) // piece)
    at_slot = dot(jnp.broadcast_to(at_slot, (8, pages)), spread)[:1].astype(jnp.int32)
    place = at_slot * piece + iota((1, pages * piece), 1) % piece

    label_lane = iota((TAIL, pages), 0)
    named = ones_where((label_lane // piece == rank) & (label_lane < per_pair * piece))
    labels = dot_t((owned * label).astype(jnp.bfloat16), named).astype(jnp.bfloat16)
    rest = block - lat_rows
    row = iota((count * rest, 1), 0)
    tail = dot(
        ones_where(row == iota((1, count), 1) * rest + per_pair * rope_rows), labels
    )
    rope_copy.wait()
    for j in range(rope_rows):
        pick = ones_where(row == dest * rest + rank * rope_rows + j)
        tail = tail + dot(pick, rope_buf[:, j * TAIL : (j + 1) * TAIL])
    buf_ref[:, lat_rows:, :] = tail.reshape(count, rest, TAIL).astype(jnp.bfloat16)

    lat_copy.wait()
    lat = lat_buf[...].astype(jnp.float32).reshape(pages, 2, piece, lat_w)
    lat = jnp.where(head % 2 == 1, lat[:, 1], lat[:, 0]).reshape(pages * piece, lat_w)
    lat = lat.astype(jnp.bfloat16)
    step = count // chunks
    copies = []
    for i in range(chunks):
        rows = step * per_pair * piece
        value = dot(ones_where(iota((rows, 1), 0) + i * rows == place), lat)
        value = [
            value[:, c * TAIL : (c + 1) * TAIL].reshape(step * per_pair, 1, piece, TAIL)
            for c in range(cuts)
        ]
        value = jnp.concatenate(value, axis=1).reshape(step, lat_rows, TAIL)
        here = pl.ds(i * step, step)
        buf_ref[here, :lat_rows, :] = value.astype(jnp.bfloat16)
        copy = pltpu.make_async_copy(buf_ref.at[here], out_hbm.at[here], out_sem.at[i])
        copy.start()
        copies.append(copy)
    for copy in copies:
        copy.wait()


def split3(x):
    hi = x.astype(jnp.bfloat16)
    rest = x - hi.astype(jnp.float32)
    mid = rest.astype(jnp.bfloat16)
    low = (rest - mid.astype(jnp.float32)).astype(jnp.bfloat16)
    return hi.astype(jnp.float32), mid.astype(jnp.float32), low.astype(jnp.float32)


def query_kernel(
    scale, rows, qn_ref, qtail_ref, w_ref, fresh_ref, fresh_t_ref, q_ref, swap_ref, part_ref, lse_ref, acc_ref
):
    heads, width, _ = qn_ref.shape
    lat_w = w_ref.shape[2]
    steps = width // rows
    for head in range(heads):
        absorbed = dot(qn_ref[head], w_ref[head])
        for row in range(rows):
            at = (row * heads + head) * steps
            acc_ref[at : at + steps, :] = absorbed[row * steps : (row + 1) * steps]
    half = rows * heads * steps // 2
    absorbed = acc_ref[...].T
    tail = qtail_ref[...].astype(jnp.float32).T
    q_ref[:lat_w, :] = absorbed.astype(jnp.bfloat16)
    q_ref[lat_w:, :] = tail.astype(jnp.bfloat16)
    swap_ref[:lat_w, :] = pltpu.roll(absorbed, half, 1).astype(jnp.bfloat16)
    swap_ref[lat_w:, :] = pltpu.roll(tail, half, 1).astype(jnp.bfloat16)
    scores = dot(fresh_ref[...], q_ref[...]) * scale
    shape = scores.shape
    token = iota(shape, 0)
    query = iota(shape, 1)
    allowed = (query // (heads * steps) == token % rows) & (token // rows <= query % steps)
    scores = jnp.where(allowed, scores, NEG)
    high = jnp.max(scores, axis=0, keepdims=True)
    weights = jnp.exp(scores - high)
    total = jnp.sum(weights, axis=0, keepdims=True)
    part_ref[...] = dot(fresh_t_ref[...], weights.astype(jnp.bfloat16)) * (1.0 / total)
    lse_ref[...] = jnp.broadcast_to(high + jnp.log(total), lse_ref.shape)


def gather_kernel(
    piece,
    per_pair,
    rope_w,
    pages_row,
    block_hbm,
    bias_ref,
    key_hbm,
    block_ref,
    lat_ref,
    tail_ref,
    key_ref,
    in_sem,
    out_sem,
):
    rows, per_row, key_w = key_ref.shape
    count, block, _ = block_ref.shape
    cuts = (key_w - TAIL) // TAIL
    lat_w = cuts * TAIL
    pair_tokens = per_pair * piece
    lat_rows = pair_tokens * cuts
    rest = block - lat_rows
    rope_rows = piece * rope_w // TAIL
    half = per_row // 2

    chunks = in_sem.shape[0]
    step = count // chunks
    copies = []
    for i in range(chunks):
        here = pl.ds(i * step, step)
        copy = pltpu.make_async_copy(block_hbm.at[here], block_ref.at[here], in_sem.at[i])
        copy.start()
        copies.append(copy)
    labels = []
    for i, copy in enumerate(copies):
        copy.wait()
        here = slice(i * step, (i + 1) * step)
        tail = block_ref[here, lat_rows:, :].astype(jnp.float32)
        marked = iota(tail.shape, 1) == per_pair * rope_rows
        labels.append(jnp.sum(jnp.where(marked, tail, 0.0), axis=1))
        tail_ref[i * step * rest : (i + 1) * step * rest, :] = tail.reshape(
            step * rest, TAIL
        ).astype(jnp.bfloat16)
        lat = block_ref[here, :lat_rows, :].astype(jnp.float32)
        lat = lat.reshape(step * per_pair, cuts, piece, TAIL)
        for c in range(cuts):
            lat_ref[i * step * pair_tokens : (i + 1) * step * pair_tokens, pl.ds(c * TAIL, TAIL)] = (
                lat[:, c].reshape(step * pair_tokens, TAIL).astype(jnp.bfloat16)
            )
    labels = jnp.concatenate(labels, axis=0).astype(jnp.bfloat16)

    def slot_of(columns, group, lane):
        spread = ones_where(iota((TAIL, columns), 0) == lane)
        wide = dot(labels, spread)
        own = iota((count, columns), 0) == iota((1, columns), 1) // group
        return jnp.sum(jnp.where(own, wide, 0.0), axis=0, keepdims=True).astype(jnp.int32) - 1

    columns = count * pair_tokens
    inner = iota((1, columns), 1) % pair_tokens
    slot = slot_of(columns, pair_tokens, inner)
    token = inner % piece
    row = (slot >= pages_row).astype(jnp.int32)
    target = row * (per_row - pages_row * (piece // 2)) + token % 2 * half
    target = target + slot * (piece // 2) + token // 2
    target = jnp.where(slot >= 0, target, -1)
    columns = count * rest
    inner = iota((1, columns), 1) % rest
    lane = jnp.where(inner < per_pair * rope_rows, inner // rope_rows * piece, TAIL)
    slot = slot_of(columns, rest, lane)
    rope_target = jnp.where(slot >= 0, slot * rope_rows + inner % rope_rows, -1)
    copies = []
    for b in range(rows):
        pick = ones_where(iota((half, 1), 0) + b * half == rope_target)
        rope_b = dot(pick, tail_ref[...])
        rope_b = jnp.concatenate([rope_b, pltpu.roll(rope_b, TAIL - rope_w, 1)], axis=0)
        lane = iota(rope_b.shape, 1)
        bias = bias_ref[b * per_row : (b + 1) * per_row]
        rope_b = jnp.where(lane < rope_w, rope_b, jnp.where(lane == rope_w, bias, 0.0))
        key_ref[b, :, lat_w:] = rope_b.astype(jnp.bfloat16)
        pick = ones_where(iota((per_row, 1), 0) + b * per_row == target)
        key_ref[b, :, :lat_w] = dot(pick, lat_ref[...]).astype(jnp.bfloat16)
        copy = pltpu.make_async_copy(key_ref.at[b], key_hbm.at[b], out_sem.at[b])
        copy.start()
        copies.append(copy)
    for copy in copies:
        copy.wait()


def attend(scale, key, query, lat_w):
    scores = dot(key, query)
    high = jnp.max(scores, axis=0, keepdims=True)
    weights = jnp.exp2((scores - high) * (scale * LOG2E))
    total = jnp.sum(weights, axis=0, keepdims=True)
    return high, total, dot(key[:, :lat_w].T, weights.astype(jnp.bfloat16))


def ask(q_refs, b):
    left = iota(q_refs[0].shape, 1) < q_refs[0].shape[1] // 2
    tiles = []
    for k in range(0, len(q_refs), 2):
        one, two = q_refs[k][...].astype(jnp.float32), q_refs[k + 1][...].astype(jnp.float32)
        first, second = (one, two) if b == 0 else (two, one)
        tiles.append(jnp.where(left, first, second).astype(jnp.bfloat16))
    return jnp.concatenate(tiles, axis=1)


def own_kernel(scale, key_ref, *refs):
    q_refs, (part_ref, stat_ref) = refs[:-2], refs[-2:]
    for b in range(key_ref.shape[0]):
        high, total, part = attend(scale, key_ref[b], ask(q_refs, b), part_ref.shape[1])
        part_ref[b] = part
        stat_ref[b] = jnp.where(iota(stat_ref.shape[1:], 0) == 0, high, total)


def both_kernel(scale, key_ref, own_ref, stat_ref, *refs):
    count = len(refs) // 2
    q_refs, out_refs = refs[:count], refs[count:]
    lat_w = own_ref.shape[1]
    queries = q_refs[0].shape[1]
    parts = []
    for b in range(key_ref.shape[0]):
        high, total, part = attend(scale, key_ref[b], ask(q_refs, b), lat_w)
        high_own, total_own = stat_ref[b, 0:1], stat_ref[b, 1:2]
        top = jnp.maximum(high, high_own)
        keep = jnp.exp2((high - top) * (scale * LOG2E))
        keep_own = jnp.exp2((high_own - top) * (scale * LOG2E))
        total = total * keep + total_own * keep_own
        inverse = 1.0 / total
        part = part * (keep * inverse) + own_ref[b] * (keep_own * inverse)
        hi, mid, low = split3(top * scale + jnp.log(total))
        mark = iota((INFO, part.shape[1]), 0)
        info = jnp.where(mark == 0, hi, jnp.where(mark == 1, mid, jnp.where(mark == 2, low, 0.0)))
        parts.append(jnp.concatenate([part, info], axis=0))
    left = iota((lat_w + INFO, queries), 1) < queries // 2
    for k in range(0, count, 2):
        lanes = slice(k * queries // 2, (k + 2) * queries // 2)
        one, two = parts[0][:, lanes], parts[1][:, lanes]
        out_refs[k][...] = jnp.where(left, one, two).astype(jnp.bfloat16)
        out_refs[k + 1][...] = jnp.where(left, two, one).astype(jnp.bfloat16)


def merge_kernel(rows_dev, fresh_ref, fresh_lse_ref, w_ref, *refs):
    part_refs, out_ref, lat_ref = refs[:-2], refs[-2], refs[-1]
    heads, lat_w, value_w = w_ref.shape
    width = out_ref.shape[1]
    steps = width // rows_dev
    half = fresh_ref.shape[1] // 2
    lses = [fresh_lse_ref[...]]
    for k, part_ref in enumerate(part_refs):
        info = jnp.sum(part_ref[lat_w:, :].astype(jnp.float32), axis=0, keepdims=True)
        info = jnp.broadcast_to(info, lses[0].shape)
        lses.append(pltpu.roll(info, half, 1) if k % 2 else info)
    high = functools.reduce(jnp.maximum, lses)
    shares = [jnp.exp(lse - high) for lse in lses]
    inverse = 1.0 / functools.reduce(jnp.add, shares)
    total = fresh_ref[...] * (shares[0] * inverse)[:1]
    swapped = 0.0
    for k, part_ref in enumerate(part_refs):
        share = shares[k + 1] * inverse
        part = part_ref[:lat_w, :].astype(jnp.float32)
        if k % 2:
            swapped = swapped + part * pltpu.roll(share, half, 1)[:1]
        else:
            total = total + part * share[:1]
    total = total + pltpu.roll(swapped, half, 1)
    shape = (heads * width, heads * width)
    to, at = iota(shape, 0), iota(shape, 1)
    wanted = (to % rows_dev * heads + to // width) * steps + to % width // rows_dev
    lat_ref[...] = dot_t(ones_where(at == wanted), total.astype(jnp.bfloat16))
    for head in range(heads):
        rows = lat_ref[head * width : (head + 1) * width, :].astype(jnp.bfloat16)
        value = dot(rows, w_ref[head]).astype(jnp.bfloat16)
        for copy in range(out_ref.shape[0]):
            out_ref[copy, :, head * value_w : (head + 1) * value_w] = value


def stage_kernel(own_hbm, near_hbm, far_hbm, opp_a_hbm, opp_b_hbm, out_ref, sem_ref):
    here = lax.axis_index("row") // NZ
    depth = opp_a_hbm.shape[1]
    near, far, opposite = [(here + k) % NX for k in (NX - 1, 1, 2)]
    copies = [
        pltpu.make_async_copy(own_hbm, out_ref.at[here], sem_ref.at[0]),
        pltpu.make_async_copy(near_hbm, out_ref.at[near], sem_ref.at[1]),
        pltpu.make_async_copy(far_hbm, out_ref.at[far], sem_ref.at[2]),
        pltpu.make_async_copy(opp_a_hbm, out_ref.at[opposite, :, :depth], sem_ref.at[3]),
        pltpu.make_async_copy(opp_b_hbm, out_ref.at[opposite, :, depth:], sem_ref.at[4]),
    ]
    for copy in copies:
        copy.start()
    for copy in copies:
        copy.wait()


def project_kernel(width, x_ref, w_ref, out_ref):
    x = x_ref[...]
    for k in range(NX):
        block = dot_t(x, w_ref[k])
        for z in range(NZ):
            out_ref[z * NX + k] = block[z * width : (z + 1) * width]


def sum_kernel(in_ref, keep_ref, send_ref):
    core = lax.axis_index("head") % 2
    per_core = keep_ref.shape[0]
    for i in range(per_core):
        for ref, half in ((keep_ref, core), (send_ref, 1 - core)):
            first = (half * per_core + i) * NX
            ref[i] = functools.reduce(jnp.add, [in_ref[first + y] for y in range(NX)])


def final_kernel(keep_ref, got_ref, out_ref):
    count, width, _ = keep_ref.shape
    value = [(keep_ref[i] + got_ref[i]).astype(jnp.bfloat16) for i in range(count)]
    out_ref[...] = jnp.concatenate(value, axis=1)


def shift_y(x, n_head, k):
    cores = n_head // NX
    if k % NX == 0:
        return x
    return lax.ppermute(x, "head", [(h, (h + k * cores) % n_head) for h in range(n_head)])


def shift_x(x, k):
    return lax.ppermute(
        x,
        "row",
        [(a * NZ + b, (a + k) % NX * NZ + b) for a in range(NX) for b in range(NZ)],
    )


def on_device(
    q_nope,
    q_rope,
    new_latent,
    new_rope,
    latent_pages,
    rope_pages,
    dest_rows,
    dest_slots,
    page_table,
    lengths,
    w_uk,
    w_uv,
    w_o,
):
    bf16, f32 = jnp.bfloat16, jnp.float32
    n_row = lax.axis_size("row")
    n_head = lax.axis_size("head")
    row, head = lax.axis_index("row"), lax.axis_index("head")
    rows_dev, pages_row = page_table.shape
    pages, page_len, lat_w = latent_pages.shape
    rope_w = new_rope.shape[-1]
    steps, _, heads, nope_w = q_nope.shape
    value_w = w_uv.shape[-1]
    piece = page_len // n_head
    per_pair = 2 * (pages // n_row) + min(pages % n_row, 1)
    scale = 1.0 / (nope_w + rope_w) ** 0.5
    width = steps * rows_dev
    queries = heads * width
    tokens = pages * piece
    slots = n_row * per_pair * piece

    lat_rows = per_pair * piece * lat_w // TAIL
    rope_rows = per_pair * piece * rope_w // TAIL
    block = lat_rows + (rope_rows + 8) // 8 * 8
    send = call(
        functools.partial(pack_kernel, rows_dev, pages_row, per_pair),
        jax.ShapeDtypeStruct((n_row, block, TAIL), bf16),
        [dest_rows[None, :], dest_slots[None, :], latent_pages, rope_pages],
        scratch=[
            pltpu.VMEM((pages, 2 * piece, lat_w), bf16),
            pltpu.VMEM((pages, piece * rope_w), bf16),
            pltpu.VMEM((n_row, block, TAIL), bf16),
            pltpu.SemaphoreType.DMA((2,)),
            pltpu.SemaphoreType.DMA((4,)),
        ],
        flops=2 * slots * tokens * lat_w,
        nbytes=2 * (slots + 2 * tokens) * lat_w,
        mem=60,
        out_spec=HBM,
        in_hbm=(2, 3),
    )
    got = lax.all_to_all(send, "row", split_axis=0, concat_axis=0, tiled=True)

    qn = jnp.transpose(q_nope, (2, 1, 0, 3)).reshape(heads, width, nope_w)
    qr = q_rope.reshape(steps, rows_dev, heads, rope_w)
    qr = jnp.transpose(qr, (1, 2, 0, 3)).reshape(queries, rope_w)
    one_lane = jnp.arange(TAIL - rope_w, dtype=jnp.int32)[None, :] == 0
    q_tail = jnp.concatenate(
        [qr, jnp.broadcast_to(one_lane, (queries, TAIL - rope_w)).astype(bf16)], axis=1
    )
    fresh = jnp.concatenate(
        [
            new_latent.reshape(width, lat_w),
            new_rope.reshape(width, rope_w),
            jnp.zeros((width, TAIL - rope_w), bf16),
        ],
        axis=1,
    )
    fresh = jnp.concatenate([fresh, jnp.zeros((-width % 16, lat_w + TAIL), bf16)], axis=0)
    query, swapped, fresh_part, fresh_lse = call(
        functools.partial(query_kernel, scale, rows_dev),
        (
            jax.ShapeDtypeStruct((lat_w + TAIL, queries), bf16),
            jax.ShapeDtypeStruct((lat_w + TAIL, queries), bf16),
            jax.ShapeDtypeStruct((lat_w, queries), f32),
            jax.ShapeDtypeStruct((8, queries), f32),
        ),
        [qn, q_tail, w_uk, fresh, fresh[:, :lat_w].T],
        scratch=[pltpu.VMEM((queries, lat_w), f32)],
        flops=2 * queries * nope_w * lat_w,
        nbytes=2 * heads * nope_w * lat_w,
    )
    all_queries = [shift_y((query, swapped)[k % 2], n_head, k) for k in range(NX)]

    w_t = w_o.T
    w_near, w_far = shift_x(w_t, 1), shift_x(w_t, -1)
    depth = w_t.shape[1] // 2

    slot_ids = jnp.arange(pages_row, dtype=jnp.int32)
    holds = (page_table[:, :, None] == slot_ids[None, None, :]).astype(jnp.int32)
    logical = jnp.sum(holds * slot_ids[None, :, None], axis=1)
    limit = lengths[:, None] - logical * page_len - head * piece
    within = jnp.arange(piece, dtype=jnp.int32).reshape(piece // 2, 2).T
    usable = within[None, :, None, :] < limit[:, None, :, None]
    bias = jnp.where(usable, 0.0, NEG).astype(f32).reshape(rows_dev * pages_row * piece, 1)

    got, w_near, w_far, all_queries = lax.optimization_barrier((got, w_near, w_far, all_queries))
    w_cols = [
        w_t,
        w_near,
        w_far,
        shift_x(w_near[:, :depth], 1),
        shift_x(w_far[:, depth:], -1),
    ]
    key = call(
        functools.partial(gather_kernel, piece, per_pair, rope_w, pages_row),
        jax.ShapeDtypeStruct((rows_dev, pages_row * piece, lat_w + TAIL), bf16),
        [got, bias],
        scratch=[
            pltpu.VMEM(got.shape, bf16),
            pltpu.VMEM((slots, lat_w), bf16),
            pltpu.VMEM((n_row * (block - lat_rows), TAIL), bf16),
            pltpu.VMEM((rows_dev, pages_row * piece, lat_w + TAIL), bf16),
            pltpu.SemaphoreType.DMA((4,)),
            pltpu.SemaphoreType.DMA((rows_dev,)),
        ],
        flops=2 * slots * tokens * lat_w,
        nbytes=2 * slots * lat_w,
        out_spec=HBM,
        in_hbm=(0,),
    )
    other = lax.ppermute(key, "head", [(h, h ^ 1) for h in range(n_head)])
    asked = NX * queries // rows_dev
    own_part, own_stat = call(
        functools.partial(own_kernel, scale),
        (
            jax.ShapeDtypeStruct((rows_dev, lat_w, asked), f32),
            jax.ShapeDtypeStruct((rows_dev, 8, asked), f32),
        ),
        [key] + all_queries,
        flops=2 * tokens * asked * (2 * lat_w + TAIL),
        nbytes=2 * tokens * lat_w,
    )
    parts = call(
        functools.partial(both_kernel, scale),
        tuple(jax.ShapeDtypeStruct((lat_w + INFO, queries), bf16) for _ in range(NX)),
        [other, own_part, own_stat] + all_queries,
        flops=2 * tokens * asked * (2 * lat_w + TAIL),
        nbytes=2 * tokens * lat_w,
    )
    parts = [shift_y(part, n_head, -k) for k, part in enumerate(parts)]
    head_out = call(
        functools.partial(merge_kernel, rows_dev),
        jax.ShapeDtypeStruct((NZ, width, heads * value_w), bf16),
        [fresh_part, fresh_lse, w_uv] + parts,
        scratch=[pltpu.VMEM((queries, lat_w), f32)],
        flops=2 * queries * lat_w * value_w,
        nbytes=2 * heads * lat_w * value_w,
    )

    rings = [[a * NZ + b for b in range(NZ)] for a in range(NX)]
    ring = lax.all_to_all(
        head_out, "row", split_axis=0, concat_axis=0, axis_index_groups=rings, tiled=True
    )
    cols = w_o.shape[1]
    cores = n_head // NX
    w_ring = call(
        stage_kernel,
        jax.ShapeDtypeStruct((NX,) + w_t.shape, bf16),
        w_cols,
        scratch=[pltpu.SemaphoreType.DMA((5,))],
        nbytes=4 * NX * w_o.size,
        in_hbm=(0, 1, 2, 3, 4),
    )
    sums = call(
        functools.partial(project_kernel, width),
        jax.ShapeDtypeStruct((NZ * NX, width, cols), f32),
        [ring.reshape(NZ * width, heads * value_w), w_ring],
        flops=2 * NX * NZ * width * w_o.size,
        nbytes=2 * NX * w_o.size,
    )
    planes = [
        [(x * NZ + z) * n_head + y * cores + core for z in range(NZ) for y in range(NX)]
        for x in range(NX)
        for core in range(cores)
    ]
    sums = lax.all_to_all(
        sums,
        ("row", "head"),
        split_axis=0,
        concat_axis=0,
        axis_index_groups=planes,
        tiled=True,
    )
    half = jax.ShapeDtypeStruct((NZ // cores, width, cols), f32)
    keep, give = call(sum_kernel, (half, half), [sums])
    taken = lax.ppermute(give, "head", [(h, h ^ 1) for h in range(n_head)])
    out = call(
        final_kernel,
        jax.ShapeDtypeStruct((width, NZ // cores * cols), bf16),
        [keep, taken],
    )
    return out.reshape(steps, rows_dev, NZ // cores * cols)


def solution(mesh):
    placed = (
        P(None, "row", "head", None),
        P(None, "row", "head"),
        P(None, "row", None),
        P(None, "row", None),
        P("row", None, None),
        P("row", None),
        P("row"),
        P("row"),
        P("row", None),
        P("row"),
        P("head", None, None),
        P("head", None, None),
        P("head", "row"),
    )
    return jax.shard_map(
        on_device, mesh=mesh, in_specs=placed, out_specs=P(None, "row", "head"), check_vma=False
    )
```

```python
import functools

import jax
import jax.numpy as jnp
from jax import lax
from jax.experimental import pallas as pl
from jax.experimental.pallas import tpu as pltpu
from jax.sharding import PartitionSpec as P

NX = 4
NZ = 8
TAIL = 128
INFO = 16
NEG = -1e30
LOG2E = 1.4426950408889634
LN2 = 0.6931471805599453

VMEM = pl.BlockSpec(memory_space=pltpu.VMEM)
SMEM = pl.BlockSpec(memory_space=pltpu.SMEM)
HBM = pl.BlockSpec(memory_space=pltpu.HBM)


def call(
    body, out_shape, ins, scratch=(), flops=0, nbytes=0, mem=24, out_spec=VMEM, in_hbm=()
):
    return pl.pallas_call(
        body,
        out_shape=out_shape,
        in_specs=[
            HBM if i in in_hbm else SMEM if a.dtype == jnp.int32 and a.ndim == 1 else VMEM
            for i, a in enumerate(ins)
        ],
        out_specs=jax.tree.map(lambda _: out_spec, out_shape),
        scratch_shapes=list(scratch),
        compiler_params=pltpu.CompilerParams(vmem_limit_bytes=mem * 2**20),
        cost_estimate=pl.CostEstimate(flops=flops, bytes_accessed=nbytes, transcendentals=0),
    )(*ins)


def dot(a, b):
    return lax.dot_general(a, b, (((1,), (0,)), ((), ())), preferred_element_type=jnp.float32)


def dot_t(a, b):
    return lax.dot_general(a, b, (((1,), (1,)), ((), ())), preferred_element_type=jnp.float32)


def iota(shape, dim):
    return lax.broadcasted_iota(jnp.int32, shape, dim)


def ones_where(mask):
    return jnp.where(mask, 1.0, 0.0).astype(jnp.bfloat16)


def pack_kernel(
    rows_dev,
    pages_row,
    per_pair,
    rows_hbm,
    slots_hbm,
    lat_hbm,
    rope_hbm,
    out_hbm,
    rows_ref,
    slots_ref,
    lat_ref,
    lat_buf,
    rope_buf,
    buf_ref,
    in_sem,
    out_sem,
):
    pages, both, lat_w = lat_buf.shape
    piece = both // 2
    count, block, _ = buf_ref.shape
    chunks = out_sem.shape[0]
    cuts = lat_w // TAIL
    rope_rows = rope_buf.shape[1] // TAIL
    lat_rows = per_pair * cuts * piece
    head = lax.axis_index("head")
    lists = [
        pltpu.make_async_copy(rows_hbm, rows_ref, in_sem.at[0]),
        pltpu.make_async_copy(slots_hbm, slots_ref, in_sem.at[1]),
    ]
    for copy in lists:
        copy.start()
    lane0 = pl.multiple_of(head * rope_buf.shape[1], rope_buf.shape[1])
    rope_copy = pltpu.make_async_copy(
        rope_hbm.at[:, pl.ds(lane0, rope_buf.shape[1])], rope_buf, in_sem.at[2]
    )
    rope_copy.start()
    first = pl.multiple_of(head // 2 * both, both)
    cut = pages // chunks
    lat_copies = []
    for i in range(chunks):
        here = pl.ds(i * cut, cut)
        copy = pltpu.make_async_copy(
            lat_hbm.at[here, pl.ds(first, both), :], lat_buf.at[here], in_sem.at[3 + i]
        )
        copy.start()
        lat_copies.append(copy)
    for copy in lists:
        copy.wait()

    dest = rows_ref[...] // rows_dev
    label = (rows_ref[...] % rows_dev * pages_row + slots_ref[...] + 1).astype(jnp.float32)
    owned = jnp.where(iota((count, pages), 0) == dest, 1.0, 0.0)
    before = ones_where(iota((pages, pages), 0) < iota((pages, pages), 1))
    rank = jnp.sum(owned * dot(owned.astype(jnp.bfloat16), before), axis=0, keepdims=True)
    rank = rank.astype(jnp.int32)
    at_slot = (dest * per_pair + rank).astype(jnp.float32).astype(jnp.bfloat16)
    spread = ones_where(iota((pages, pages * piece), 0) == iota((pages, pages * piece), 1) // piece)
    at_slot = dot(jnp.broadcast_to(at_slot, (8, pages)), spread)[:1].astype(jnp.int32)
    place = at_slot * piece + iota((1, pages * piece), 1) % piece

    label_lane = iota((TAIL, pages), 0)
    named = ones_where((label_lane // piece == rank) & (label_lane < per_pair * piece))
    labels = dot_t((owned * label).astype(jnp.bfloat16), named).astype(jnp.bfloat16)
    rest = block - lat_rows
    row = iota((count * rest, 1), 0)
    tail = dot(
        ones_where(row == iota((1, count), 1) * rest + per_pair * rope_rows), labels
    )
    rope_copy.wait()
    for j in range(rope_rows):
        pick = ones_where(row == dest * rest + rank * rope_rows + j)
        tail = tail + dot(pick, rope_buf[:, j * TAIL : (j + 1) * TAIL])
    buf_ref[:, lat_rows:, :] = tail.reshape(count, rest, TAIL).astype(jnp.bfloat16)

    for i, copy in enumerate(lat_copies):
        copy.wait()
        lat = lat_buf[i * cut : (i + 1) * cut].astype(jnp.float32).reshape(cut, 2, piece, lat_w)
        lat = jnp.where(head % 2 == 1, lat[:, 1], lat[:, 0]).reshape(cut * piece, lat_w)
        lat_ref[i * cut * piece : (i + 1) * cut * piece, :] = lat.astype(jnp.bfloat16)
    lat = lat_ref[...]
    step = count // chunks
    copies = []
    for i in range(chunks):
        rows = step * per_pair * piece
        value = dot(ones_where(iota((rows, 1), 0) + i * rows == place), lat)
        value = [
            value[:, c * TAIL : (c + 1) * TAIL].reshape(step * per_pair, 1, piece, TAIL)
            for c in range(cuts)
        ]
        value = jnp.concatenate(value, axis=1).reshape(step, lat_rows, TAIL)
        here = pl.ds(i * step, step)
        buf_ref[here, :lat_rows, :] = value.astype(jnp.bfloat16)
        copy = pltpu.make_async_copy(buf_ref.at[here], out_hbm.at[here], out_sem.at[i])
        copy.start()
        copies.append(copy)
    for copy in copies:
        copy.wait()


def split3(x):
    hi = x.astype(jnp.bfloat16)
    rest = x - hi.astype(jnp.float32)
    mid = rest.astype(jnp.bfloat16)
    low = (rest - mid.astype(jnp.float32)).astype(jnp.bfloat16)
    return hi.astype(jnp.float32), mid.astype(jnp.float32), low.astype(jnp.float32)


def query_kernel(
    scale, rows, qn_ref, qtail_ref, w_ref, fresh_ref, fresh_t_ref, q_ref, swap_ref, part_ref, lse_ref, acc_ref
):
    heads, width, _ = qn_ref.shape
    lat_w = w_ref.shape[2]
    steps = width // rows
    for head in range(heads):
        absorbed = dot(qn_ref[head], w_ref[head])
        for row in range(rows):
            at = (row * heads + head) * steps
            acc_ref[at : at + steps, :] = absorbed[row * steps : (row + 1) * steps]
    half = rows * heads * steps // 2
    absorbed = acc_ref[...].T
    tail = qtail_ref[...].astype(jnp.float32).T
    q_ref[:lat_w, :] = absorbed.astype(jnp.bfloat16)
    q_ref[lat_w:, :] = tail.astype(jnp.bfloat16)
    swap_ref[:lat_w, :] = pltpu.roll(absorbed, half, 1).astype(jnp.bfloat16)
    swap_ref[lat_w:, :] = pltpu.roll(tail, half, 1).astype(jnp.bfloat16)
    scores = dot(fresh_ref[...], q_ref[...]) * scale
    shape = scores.shape
    token = iota(shape, 0)
    query = iota(shape, 1)
    allowed = (query // (heads * steps) == token % rows) & (token // rows <= query % steps)
    scores = jnp.where(allowed, scores, NEG)
    high = jnp.max(scores, axis=0, keepdims=True)
    weights = jnp.exp(scores - high)
    total = jnp.sum(weights, axis=0, keepdims=True)
    part_ref[...] = dot(fresh_t_ref[...], weights.astype(jnp.bfloat16)) * (1.0 / total)
    lse_ref[...] = jnp.broadcast_to(high + jnp.log(total), lse_ref.shape)


def gather_kernel(
    piece,
    per_pair,
    rope_w,
    pages_row,
    block_hbm,
    bias_ref,
    key_hbm,
    block_ref,
    lat_ref,
    tail_ref,
    key_ref,
    in_sem,
    out_sem,
):
    rows, per_row, key_w = key_ref.shape
    count, block, _ = block_ref.shape
    cuts = (key_w - TAIL) // TAIL
    lat_w = cuts * TAIL
    pair_tokens = per_pair * piece
    lat_rows = pair_tokens * cuts
    rest = block - lat_rows
    rope_rows = piece * rope_w // TAIL
    half = per_row // 2

    chunks = in_sem.shape[0]
    step = count // chunks
    copies = []
    for i in range(chunks):
        here = pl.ds(i * step, step)
        copy = pltpu.make_async_copy(block_hbm.at[here], block_ref.at[here], in_sem.at[i])
        copy.start()
        copies.append(copy)
    labels = []
    for i, copy in enumerate(copies):
        copy.wait()
        here = slice(i * step, (i + 1) * step)
        tail = block_ref[here, lat_rows:, :].astype(jnp.float32)
        marked = iota(tail.shape, 1) == per_pair * rope_rows
        labels.append(jnp.sum(jnp.where(marked, tail, 0.0), axis=1))
        tail_ref[i * step * rest : (i + 1) * step * rest, :] = tail.reshape(
            step * rest, TAIL
        ).astype(jnp.bfloat16)
        lat = block_ref[here, :lat_rows, :].astype(jnp.float32)
        lat = lat.reshape(step * per_pair, cuts, piece, TAIL)
        for c in range(cuts):
            lat_ref[i * step * pair_tokens : (i + 1) * step * pair_tokens, pl.ds(c * TAIL, TAIL)] = (
                lat[:, c].reshape(step * pair_tokens, TAIL).astype(jnp.bfloat16)
            )
    labels = jnp.concatenate(labels, axis=0).astype(jnp.bfloat16)

    def slot_of(columns, group, lane):
        spread = ones_where(iota((TAIL, columns), 0) == lane)
        wide = dot(labels, spread)
        own = iota((count, columns), 0) == iota((1, columns), 1) // group
        return jnp.sum(jnp.where(own, wide, 0.0), axis=0, keepdims=True).astype(jnp.int32) - 1

    columns = count * pair_tokens
    inner = iota((1, columns), 1) % pair_tokens
    slot = slot_of(columns, pair_tokens, inner)
    token = inner % piece
    row = (slot >= pages_row).astype(jnp.int32)
    target = row * (per_row - pages_row * (piece // 2)) + token % 2 * half
    target = target + slot * (piece // 2) + token // 2
    target = jnp.where(slot >= 0, target, -1)
    columns = count * rest
    inner = iota((1, columns), 1) % rest
    lane = jnp.where(inner < per_pair * rope_rows, inner // rope_rows * piece, TAIL)
    slot = slot_of(columns, rest, lane)
    rope_target = jnp.where(slot >= 0, slot * rope_rows + inner % rope_rows, -1)
    copies = []
    for b in range(rows):
        pick = ones_where(iota((half, 1), 0) + b * half == rope_target)
        rope_b = dot(pick, tail_ref[...])
        rope_b = jnp.concatenate([rope_b, pltpu.roll(rope_b, TAIL - rope_w, 1)], axis=0)
        lane = iota(rope_b.shape, 1)
        bias = bias_ref[b * per_row : (b + 1) * per_row]
        rope_b = jnp.where(lane < rope_w, rope_b, jnp.where(lane == rope_w, bias, 0.0))
        key_ref[b, :, lat_w:] = rope_b.astype(jnp.bfloat16)
        pick = ones_where(iota((per_row, 1), 0) + b * per_row == target)
        key_ref[b, :, :lat_w] = dot(pick, lat_ref[...]).astype(jnp.bfloat16)
        copy = pltpu.make_async_copy(key_ref.at[b], key_hbm.at[b], out_sem.at[b])
        copy.start()
        copies.append(copy)
    for copy in copies:
        copy.wait()


def attend(scale, key, query, lat_w):
    scores = dot(key, query)
    high = jnp.max(scores, axis=0, keepdims=True)
    weights = jnp.exp2((scores - high) * (scale * LOG2E))
    total = jnp.sum(weights, axis=0, keepdims=True)
    return high, total, dot(key[:, :lat_w].T, weights.astype(jnp.bfloat16))


def ask(q_refs, b):
    left = iota(q_refs[0].shape, 1) < q_refs[0].shape[1] // 2
    tiles = []
    for k in range(0, len(q_refs), 2):
        one, two = q_refs[k][...].astype(jnp.float32), q_refs[k + 1][...].astype(jnp.float32)
        first, second = (one, two) if b == 0 else (two, one)
        tiles.append(jnp.where(left, first, second).astype(jnp.bfloat16))
    return jnp.concatenate(tiles, axis=1)


def own_kernel(scale, key_ref, *refs):
    q_refs, (part_ref, stat_ref) = refs[:-2], refs[-2:]
    for b in range(key_ref.shape[0]):
        high, total, part = attend(scale, key_ref[b], ask(q_refs, b), part_ref.shape[1])
        part_ref[b] = part
        stat_ref[b] = jnp.where(iota(stat_ref.shape[1:], 0) == 0, high, total)


def both_kernel(scale, key_ref, own_ref, stat_ref, *refs):
    count = len(refs) // 2
    q_refs, out_refs = refs[:count], refs[count:]
    lat_w = own_ref.shape[1]
    queries = q_refs[0].shape[1]
    parts = []
    for b in range(key_ref.shape[0]):
        high, total, part = attend(scale, key_ref[b], ask(q_refs, b), lat_w)
        high_own, total_own = stat_ref[b, 0:1], stat_ref[b, 1:2]
        top = jnp.maximum(high, high_own)
        keep = jnp.exp2((high - top) * (scale * LOG2E))
        keep_own = jnp.exp2((high_own - top) * (scale * LOG2E))
        total = total * keep + total_own * keep_own
        inverse = 1.0 / total
        part = part * (keep * inverse) + own_ref[b] * (keep_own * inverse)
        hi, mid, low = split3(top * scale + jnp.log(total))
        mark = iota((INFO, part.shape[1]), 0)
        info = jnp.where(mark == 0, hi, jnp.where(mark == 1, mid, jnp.where(mark == 2, low, 0.0)))
        parts.append(jnp.concatenate([part, info], axis=0))
    left = iota((lat_w + INFO, queries), 1) < queries // 2
    for k in range(0, count, 2):
        lanes = slice(k * queries // 2, (k + 2) * queries // 2)
        one, two = parts[0][:, lanes], parts[1][:, lanes]
        out_refs[k][...] = jnp.where(left, one, two).astype(jnp.bfloat16)
        out_refs[k + 1][...] = jnp.where(left, two, one).astype(jnp.bfloat16)


def merge_kernel(rows_dev, fresh_ref, fresh_lse_ref, w_ref, *refs):
    part_refs, out_ref, lat_ref = refs[:-2], refs[-2], refs[-1]
    heads, lat_w, value_w = w_ref.shape
    width = out_ref.shape[1]
    steps = width // rows_dev
    half = fresh_ref.shape[1] // 2
    lses = [fresh_lse_ref[...]]
    for k, part_ref in enumerate(part_refs):
        info = jnp.sum(part_ref[lat_w:, :].astype(jnp.float32), axis=0, keepdims=True)
        info = jnp.broadcast_to(info, lses[0].shape)
        lses.append(pltpu.roll(info, half, 1) if k % 2 else info)
    high = functools.reduce(jnp.maximum, lses)
    shares = [jnp.exp(lse - high) for lse in lses]
    inverse = 1.0 / functools.reduce(jnp.add, shares)
    total = fresh_ref[...] * (shares[0] * inverse)[:1]
    swapped = 0.0
    for k, part_ref in enumerate(part_refs):
        share = shares[k + 1] * inverse
        part = part_ref[:lat_w, :].astype(jnp.float32)
        if k % 2:
            swapped = swapped + part * pltpu.roll(share, half, 1)[:1]
        else:
            total = total + part * share[:1]
    total = total + pltpu.roll(swapped, half, 1)
    shape = (heads * width, heads * width)
    to, at = iota(shape, 0), iota(shape, 1)
    wanted = (to % rows_dev * heads + to // width) * steps + to % width // rows_dev
    lat_ref[...] = dot_t(ones_where(at == wanted), total.astype(jnp.bfloat16))
    for head in range(heads):
        rows = lat_ref[head * width : (head + 1) * width, :].astype(jnp.bfloat16)
        value = dot(rows, w_ref[head]).astype(jnp.bfloat16)
        for copy in range(out_ref.shape[0]):
            out_ref[copy, :, head * value_w : (head + 1) * value_w] = value


def stage_kernel(own_hbm, near_hbm, far_hbm, out_ref, sem_ref):
    copies = [
        pltpu.make_async_copy(ref, out_ref.at[i], sem_ref.at[i])
        for i, ref in enumerate((own_hbm, near_hbm, far_hbm))
    ]
    for copy in copies:
        copy.start()
    for copy in copies:
        copy.wait()


def project_kernel(
    width, x_ref, w_ref, opp_a_hbm, opp_b_hbm, out_ref, opp_a_ref, opp_b_ref, sem_ref
):
    copies = [
        pltpu.make_async_copy(opp_a_hbm, opp_a_ref, sem_ref.at[0]),
        pltpu.make_async_copy(opp_b_hbm, opp_b_ref, sem_ref.at[1]),
    ]
    for copy in copies:
        copy.start()
    here = lax.axis_index("row") // NZ
    depth = opp_a_hbm.shape[1]

    def put(k, block):
        owner = (here + k) % NX
        for z in range(NZ):
            rows = block[z * width : (z + 1) * width]
            out_ref[z * NX + owner] = rows.astype(out_ref.dtype)

    for i, k in enumerate((0, NX - 1, 1)):
        put(k, dot_t(x_ref[...], w_ref[i]))
    copies[0].wait()
    opposite = dot_t(x_ref[:, :depth], opp_a_ref[...])
    copies[1].wait()
    put(2, opposite + dot_t(x_ref[:, depth:], opp_b_ref[...]))


def sum_kernel(in_ref, keep_ref, send_ref):
    core = lax.axis_index("head") % 2
    per_core = keep_ref.shape[0]
    for i in range(per_core):
        for ref, half in ((keep_ref, core), (send_ref, 1 - core)):
            first = (half * per_core + i) * NX
            parts = [in_ref[first + y].astype(jnp.float32) for y in range(NX)]
            ref[i] = functools.reduce(jnp.add, parts)


def final_kernel(keep_ref, got_ref, out_ref):
    value = [keep_ref[i] + got_ref[i] for i in range(keep_ref.shape[0])]
    value = jnp.concatenate(value, axis=1)
    rows = out_ref.shape[1]
    for step in range(out_ref.shape[0]):
        out_ref[step] = value[step * rows : (step + 1) * rows].astype(out_ref.dtype)


def shift_y(x, n_head, k):
    cores = n_head // NX
    if k % NX == 0:
        return x
    return lax.ppermute(x, "head", [(h, (h + k * cores) % n_head) for h in range(n_head)])


def shift_x(x, k):
    return lax.ppermute(
        x,
        "row",
        [(a * NZ + b, (a + k) % NX * NZ + b) for a in range(NX) for b in range(NZ)],
    )


def on_device(
    q_nope,
    q_rope,
    new_latent,
    new_rope,
    latent_pages,
    rope_pages,
    dest_rows,
    dest_slots,
    page_table,
    lengths,
    w_uk,
    w_uv,
    w_o,
):
    bf16, f32 = jnp.bfloat16, jnp.float32
    n_row = lax.axis_size("row")
    n_head = lax.axis_size("head")
    row, head = lax.axis_index("row"), lax.axis_index("head")
    rows_dev, pages_row = page_table.shape
    pages, page_len, lat_w = latent_pages.shape
    rope_w = new_rope.shape[-1]
    steps, _, heads, nope_w = q_nope.shape
    value_w = w_uv.shape[-1]
    piece = page_len // n_head
    per_pair = 2 * (pages // n_row) + min(pages % n_row, 1)
    scale = 1.0 / (nope_w + rope_w) ** 0.5
    width = steps * rows_dev
    queries = heads * width
    tokens = pages * piece
    slots = n_row * per_pair * piece

    lat_rows = per_pair * piece * lat_w // TAIL
    rope_rows = per_pair * piece * rope_w // TAIL
    block = lat_rows + (rope_rows + 8) // 8 * 8
    send = call(
        functools.partial(pack_kernel, rows_dev, pages_row, per_pair),
        jax.ShapeDtypeStruct((n_row, block, TAIL), bf16),
        [dest_rows[None, :], dest_slots[None, :], latent_pages, rope_pages],
        scratch=[
            pltpu.VMEM((1, pages), jnp.int32),
            pltpu.VMEM((1, pages), jnp.int32),
            pltpu.VMEM((tokens, lat_w), bf16),
            pltpu.VMEM((pages, 2 * piece, lat_w), bf16),
            pltpu.VMEM((pages, piece * rope_w), bf16),
            pltpu.VMEM((n_row, block, TAIL), bf16),
            pltpu.SemaphoreType.DMA((7,)),
            pltpu.SemaphoreType.DMA((4,)),
        ],
        flops=2 * slots * tokens * lat_w,
        nbytes=2 * (slots + 2 * tokens) * lat_w,
        mem=60,
        out_spec=HBM,
        in_hbm=(0, 1, 2, 3),
    )
    got = lax.all_to_all(send, "row", split_axis=0, concat_axis=0, tiled=True)

    qn = jnp.transpose(q_nope, (2, 1, 0, 3)).reshape(heads, width, nope_w)
    qr = q_rope.reshape(steps, rows_dev, heads, rope_w)
    qr = jnp.transpose(qr, (1, 2, 0, 3)).reshape(queries, rope_w)
    one_lane = jnp.arange(TAIL - rope_w, dtype=jnp.int32)[None, :] == 0
    q_tail = jnp.concatenate(
        [qr, jnp.broadcast_to(one_lane, (queries, TAIL - rope_w)).astype(bf16)], axis=1
    )
    fresh = jnp.concatenate(
        [
            new_latent.reshape(width, lat_w),
            new_rope.reshape(width, rope_w),
            jnp.zeros((width, TAIL - rope_w), bf16),
        ],
        axis=1,
    )
    fresh = jnp.concatenate([fresh, jnp.zeros((-width % 16, lat_w + TAIL), bf16)], axis=0)
    query, swapped, fresh_part, fresh_lse = call(
        functools.partial(query_kernel, scale, rows_dev),
        (
            jax.ShapeDtypeStruct((lat_w + TAIL, queries), bf16),
            jax.ShapeDtypeStruct((lat_w + TAIL, queries), bf16),
            jax.ShapeDtypeStruct((lat_w, queries), f32),
            jax.ShapeDtypeStruct((8, queries), f32),
        ),
        [qn, q_tail, w_uk, fresh, fresh[:, :lat_w].T],
        scratch=[pltpu.VMEM((queries, lat_w), f32)],
        flops=2 * queries * nope_w * lat_w,
        nbytes=2 * heads * nope_w * lat_w,
    )
    all_queries = [shift_y((query, swapped)[k % 2], n_head, k) for k in range(NX)]

    w_t = w_o.T
    w_near, w_far = shift_x(w_t, 1), shift_x(w_t, -1)
    depth = w_t.shape[1] // 2

    slot_ids = jnp.arange(pages_row, dtype=jnp.int32)
    holds = (page_table[:, :, None] == slot_ids[None, None, :]).astype(jnp.int32)
    logical = jnp.sum(holds * slot_ids[None, :, None], axis=1)
    limit = lengths[:, None] - logical * page_len - head * piece
    within = jnp.arange(piece, dtype=jnp.int32).reshape(piece // 2, 2).T
    usable = within[None, :, None, :] < limit[:, None, :, None]
    bias = jnp.where(usable, 0.0, NEG).astype(f32).reshape(rows_dev * pages_row * piece, 1)

    got, w_near, w_far, all_queries = lax.optimization_barrier((got, w_near, w_far, all_queries))
    opposite = [shift_x(w_near[:, :depth], 1), shift_x(w_far[:, depth:], -1)]
    key = call(
        functools.partial(gather_kernel, piece, per_pair, rope_w, pages_row),
        jax.ShapeDtypeStruct((rows_dev, pages_row * piece, lat_w + TAIL), bf16),
        [got, bias],
        scratch=[
            pltpu.VMEM(got.shape, bf16),
            pltpu.VMEM((slots, lat_w), bf16),
            pltpu.VMEM((n_row * (block - lat_rows), TAIL), bf16),
            pltpu.VMEM((rows_dev, pages_row * piece, lat_w + TAIL), bf16),
            pltpu.SemaphoreType.DMA((4,)),
            pltpu.SemaphoreType.DMA((rows_dev,)),
        ],
        flops=2 * slots * tokens * lat_w,
        nbytes=2 * slots * lat_w,
        out_spec=HBM,
        in_hbm=(0,),
    )
    other = lax.ppermute(key, "head", [(h, h ^ 1) for h in range(n_head)])
    asked = NX * queries // rows_dev
    own_part, own_stat = call(
        functools.partial(own_kernel, scale),
        (
            jax.ShapeDtypeStruct((rows_dev, lat_w, asked), f32),
            jax.ShapeDtypeStruct((rows_dev, 8, asked), f32),
        ),
        [key] + all_queries,
        flops=2 * tokens * asked * (2 * lat_w + TAIL),
        nbytes=2 * tokens * lat_w,
    )
    parts = call(
        functools.partial(both_kernel, scale),
        tuple(jax.ShapeDtypeStruct((lat_w + INFO, queries), bf16) for _ in range(NX)),
        [other, own_part, own_stat] + all_queries,
        flops=2 * tokens * asked * (2 * lat_w + TAIL),
        nbytes=2 * tokens * lat_w,
    )
    parts = [shift_y(part, n_head, -k) for k, part in enumerate(parts)]
    head_out = call(
        functools.partial(merge_kernel, rows_dev),
        jax.ShapeDtypeStruct((NZ, width, heads * value_w), bf16),
        [fresh_part, fresh_lse, w_uv] + parts,
        scratch=[pltpu.VMEM((queries, lat_w), f32)],
        flops=2 * queries * lat_w * value_w,
        nbytes=2 * heads * lat_w * value_w,
    )

    rings = [[a * NZ + b for b in range(NZ)] for a in range(NX)]
    ring = lax.all_to_all(
        head_out, "row", split_axis=0, concat_axis=0, axis_index_groups=rings, tiled=True
    )
    cols = w_o.shape[1]
    cores = n_head // NX
    w_ring = call(
        stage_kernel,
        jax.ShapeDtypeStruct((3,) + w_t.shape, bf16),
        [w_t, w_near, w_far],
        scratch=[pltpu.SemaphoreType.DMA((3,))],
        nbytes=12 * w_o.size,
        in_hbm=(0, 1, 2),
    )
    sums = call(
        functools.partial(project_kernel, width),
        jax.ShapeDtypeStruct((NZ * NX, width, cols), bf16),
        [ring.reshape(NZ * width, heads * value_w), w_ring] + opposite,
        scratch=[pltpu.VMEM((cols, depth), bf16)] * 2 + [pltpu.SemaphoreType.DMA((2,))],
        flops=2 * NX * NZ * width * w_o.size,
        nbytes=2 * NX * w_o.size,
        in_hbm=(2, 3),
    )
    planes = [
        [(x * NZ + z) * n_head + y * cores + core for z in range(NZ) for y in range(NX)]
        for x in range(NX)
        for core in range(cores)
    ]
    sums = lax.all_to_all(
        sums,
        ("row", "head"),
        split_axis=0,
        concat_axis=0,
        axis_index_groups=planes,
        tiled=True,
    )
    half = jax.ShapeDtypeStruct((NZ // cores, width, cols), f32)
    keep, give = call(sum_kernel, (half, half), [sums])
    taken = lax.ppermute(give, "head", [(h, h ^ 1) for h in range(n_head)])
    return call(
        final_kernel,
        jax.ShapeDtypeStruct((steps, rows_dev, NZ // cores * cols), bf16),
        [keep, taken],
    )


def solution(mesh):
    placed = (
        P(None, "row", "head", None),
        P(None, "row", "head"),
        P(None, "row", None),
        P(None, "row", None),
        P("row", None, None),
        P("row", None),
        P("row"),
        P("row"),
        P("row", None),
        P("row"),
        P("head", None, None),
        P("head", None, None),
        P("head", "row"),
    )
    return jax.shard_map(
        on_device, mesh=mesh, in_specs=placed, out_specs=P(None, "row", "head"), check_vma=False
    )
```

```python
import functools

import jax
import jax.numpy as jnp
from jax import lax
from jax.experimental import pallas as pl
from jax.experimental.pallas import tpu as pltpu
from jax.sharding import PartitionSpec as P

NX = 4
NZ = 8
TAIL = 128
INFO = 16
NEG = -1e30
LOG2E = 1.4426950408889634
LN2 = 0.6931471805599453

VMEM = pl.BlockSpec(memory_space=pltpu.VMEM)
SMEM = pl.BlockSpec(memory_space=pltpu.SMEM)
HBM = pl.BlockSpec(memory_space=pltpu.HBM)


def call(
    body, out_shape, ins, scratch=(), flops=0, nbytes=0, mem=24, out_spec=VMEM, in_hbm=()
):
    return pl.pallas_call(
        body,
        out_shape=out_shape,
        in_specs=[
            HBM if i in in_hbm else SMEM if a.dtype == jnp.int32 and a.ndim == 1 else VMEM
            for i, a in enumerate(ins)
        ],
        out_specs=out_spec
        if isinstance(out_spec, tuple)
        else jax.tree.map(lambda _: out_spec, out_shape),
        scratch_shapes=list(scratch),
        compiler_params=pltpu.CompilerParams(vmem_limit_bytes=mem * 2**20),
        cost_estimate=pl.CostEstimate(flops=flops, bytes_accessed=nbytes, transcendentals=0),
    )(*ins)


def dot(a, b):
    return lax.dot_general(a, b, (((1,), (0,)), ((), ())), preferred_element_type=jnp.float32)


def dot_t(a, b):
    return lax.dot_general(a, b, (((1,), (1,)), ((), ())), preferred_element_type=jnp.float32)


def iota(shape, dim):
    return lax.broadcasted_iota(jnp.int32, shape, dim)


def ones_where(mask):
    return jnp.where(mask, 1.0, 0.0).astype(jnp.bfloat16)


def pack_kernel(
    rows_dev,
    pages_row,
    per_pair,
    rows_hbm,
    slots_hbm,
    lat_hbm,
    rope_hbm,
    out_hbm,
    rows_ref,
    slots_ref,
    lat_ref,
    lat_buf,
    rope_buf,
    buf_ref,
    in_sem,
    out_sem,
):
    pages, both, lat_w = lat_buf.shape
    piece = both // 2
    count, block, _ = buf_ref.shape
    chunks = out_sem.shape[0]
    cuts = lat_w // TAIL
    rope_rows = rope_buf.shape[1] // TAIL
    lat_rows = per_pair * cuts * piece
    head = lax.axis_index("head")
    lists = [
        pltpu.make_async_copy(rows_hbm, rows_ref, in_sem.at[0]),
        pltpu.make_async_copy(slots_hbm, slots_ref, in_sem.at[1]),
    ]
    for copy in lists:
        copy.start()
    lane0 = pl.multiple_of(head * rope_buf.shape[1], rope_buf.shape[1])
    rope_copy = pltpu.make_async_copy(
        rope_hbm.at[:, pl.ds(lane0, rope_buf.shape[1])], rope_buf, in_sem.at[2]
    )
    rope_copy.start()
    first = pl.multiple_of(head // 2 * both, both)
    cut = pages // chunks
    lat_copies = []
    for i in range(chunks):
        here = pl.ds(i * cut, cut)
        copy = pltpu.make_async_copy(
            lat_hbm.at[here, pl.ds(first, both), :], lat_buf.at[here], in_sem.at[3 + i]
        )
        copy.start()
        lat_copies.append(copy)
    for copy in lists:
        copy.wait()

    dest = rows_ref[...] // rows_dev
    label = (rows_ref[...] % rows_dev * pages_row + slots_ref[...] + 1).astype(jnp.float32)
    owned = jnp.where(iota((count, pages), 0) == dest, 1.0, 0.0)
    before = ones_where(iota((pages, pages), 0) < iota((pages, pages), 1))
    rank = jnp.sum(owned * dot(owned.astype(jnp.bfloat16), before), axis=0, keepdims=True)
    rank = rank.astype(jnp.int32)
    at_slot = (dest * per_pair + rank).astype(jnp.float32).astype(jnp.bfloat16)
    spread = ones_where(iota((pages, pages * piece), 0) == iota((pages, pages * piece), 1) // piece)
    at_slot = dot(jnp.broadcast_to(at_slot, (8, pages)), spread)[:1].astype(jnp.int32)
    place = at_slot * piece + iota((1, pages * piece), 1) % piece

    label_lane = iota((TAIL, pages), 0)
    named = ones_where((label_lane // piece == rank) & (label_lane < per_pair * piece))
    labels = dot_t((owned * label).astype(jnp.bfloat16), named).astype(jnp.bfloat16)
    rest = block - lat_rows
    row = iota((count * rest, 1), 0)
    tail = dot(
        ones_where(row == iota((1, count), 1) * rest + per_pair * rope_rows), labels
    )
    rope_copy.wait()
    for j in range(rope_rows):
        pick = ones_where(row == dest * rest + rank * rope_rows + j)
        tail = tail + dot(pick, rope_buf[:, j * TAIL : (j + 1) * TAIL])
    buf_ref[:, lat_rows:, :] = tail.reshape(count, rest, TAIL).astype(jnp.bfloat16)

    for i, copy in enumerate(lat_copies):
        copy.wait()
        lat = lat_buf[i * cut : (i + 1) * cut].astype(jnp.float32).reshape(cut, 2, piece, lat_w)
        lat = jnp.where(head % 2 == 1, lat[:, 1], lat[:, 0]).reshape(cut * piece, lat_w)
        lat_ref[i * cut * piece : (i + 1) * cut * piece, :] = lat.astype(jnp.bfloat16)
    lat = lat_ref[...]
    step = count // chunks
    copies = []
    for i in range(chunks):
        rows = step * per_pair * piece
        value = dot(ones_where(iota((rows, 1), 0) + i * rows == place), lat)
        value = [
            value[:, c * TAIL : (c + 1) * TAIL].reshape(step * per_pair, 1, piece, TAIL)
            for c in range(cuts)
        ]
        value = jnp.concatenate(value, axis=1).reshape(step, lat_rows, TAIL)
        here = pl.ds(i * step, step)
        buf_ref[here, :lat_rows, :] = value.astype(jnp.bfloat16)
        copy = pltpu.make_async_copy(buf_ref.at[here], out_hbm.at[here], out_sem.at[i])
        copy.start()
        copies.append(copy)
    for copy in copies:
        copy.wait()


def split3(x):
    hi = x.astype(jnp.bfloat16)
    rest = x - hi.astype(jnp.float32)
    mid = rest.astype(jnp.bfloat16)
    low = (rest - mid.astype(jnp.float32)).astype(jnp.bfloat16)
    return hi.astype(jnp.float32), mid.astype(jnp.float32), low.astype(jnp.float32)


def query_kernel(
    scale, rows, qn_ref, qtail_ref, w_ref, fresh_ref, fresh_t_ref, q_ref, swap_ref, part_ref, lse_ref, acc_ref
):
    heads, width, _ = qn_ref.shape
    lat_w = w_ref.shape[2]
    steps = width // rows
    for head in range(heads):
        absorbed = dot(qn_ref[head], w_ref[head])
        for row in range(rows):
            at = (row * heads + head) * steps
            acc_ref[at : at + steps, :] = absorbed[row * steps : (row + 1) * steps]
    half = rows * heads * steps // 2
    absorbed = acc_ref[...].T
    tail = qtail_ref[...].astype(jnp.float32).T
    q_ref[:lat_w, :] = absorbed.astype(jnp.bfloat16)
    q_ref[lat_w:, :] = tail.astype(jnp.bfloat16)
    swap_ref[:lat_w, :] = pltpu.roll(absorbed, half, 1).astype(jnp.bfloat16)
    swap_ref[lat_w:, :] = pltpu.roll(tail, half, 1).astype(jnp.bfloat16)
    scores = dot(fresh_ref[...], q_ref[...]) * scale
    shape = scores.shape
    token = iota(shape, 0)
    query = iota(shape, 1)
    allowed = (query // (heads * steps) == token % rows) & (token // rows <= query % steps)
    scores = jnp.where(allowed, scores, NEG)
    high = jnp.max(scores, axis=0, keepdims=True)
    weights = jnp.exp(scores - high)
    total = jnp.sum(weights, axis=0, keepdims=True)
    part_ref[...] = dot(fresh_t_ref[...], weights.astype(jnp.bfloat16)) * (1.0 / total)
    lse_ref[...] = jnp.broadcast_to(high + jnp.log(total), lse_ref.shape)


def gather_kernel(
    piece,
    per_pair,
    rope_w,
    pages_row,
    block_hbm,
    bias_ref,
    key_hbm,
    block_ref,
    lat_ref,
    tail_ref,
    key_ref,
    in_sem,
    out_sem,
):
    rows, per_row, key_w = key_ref.shape
    count, block, _ = block_ref.shape
    cuts = (key_w - TAIL) // TAIL
    lat_w = cuts * TAIL
    pair_tokens = per_pair * piece
    lat_rows = pair_tokens * cuts
    rest = block - lat_rows
    rope_rows = piece * rope_w // TAIL
    half = per_row // 2

    chunks = in_sem.shape[0]
    step = count // chunks
    copies = []
    for i in range(chunks):
        here = pl.ds(i * step, step)
        copy = pltpu.make_async_copy(block_hbm.at[here], block_ref.at[here], in_sem.at[i])
        copy.start()
        copies.append(copy)

    def spread_over(columns, group, lane):
        own = iota((count, columns), 0) == iota((1, columns), 1) // group
        return ones_where(iota((TAIL, columns), 0) == lane), jnp.where(own, 1.0, 0.0)

    lat_columns = count * pair_tokens
    lat_inner = iota((1, lat_columns), 1) % pair_tokens
    lat_spread = spread_over(lat_columns, pair_tokens, lat_inner)
    rope_columns = count * rest
    rope_inner = iota((1, rope_columns), 1) % rest
    lane = jnp.where(rope_inner < per_pair * rope_rows, rope_inner // rope_rows * piece, TAIL)
    rope_spread = spread_over(rope_columns, rest, lane)

    labels = []
    for i, copy in enumerate(copies):
        copy.wait()
        here = slice(i * step, (i + 1) * step)
        tail = block_ref[here, lat_rows:, :].astype(jnp.float32)
        marked = iota(tail.shape, 1) == per_pair * rope_rows
        labels.append(jnp.sum(jnp.where(marked, tail, 0.0), axis=1))
        tail_ref[i * step * rest : (i + 1) * step * rest, :] = tail.reshape(
            step * rest, TAIL
        ).astype(jnp.bfloat16)
        lat = block_ref[here, :lat_rows, :].astype(jnp.float32)
        lat = lat.reshape(step * per_pair, cuts, piece, TAIL)
        for c in range(cuts):
            lat_ref[i * step * pair_tokens : (i + 1) * step * pair_tokens, pl.ds(c * TAIL, TAIL)] = (
                lat[:, c].reshape(step * pair_tokens, TAIL).astype(jnp.bfloat16)
            )
    labels = jnp.concatenate(labels, axis=0).astype(jnp.bfloat16)

    def slot_of(spread, own):
        wide = dot(labels, spread) * own
        return jnp.sum(wide, axis=0, keepdims=True).astype(jnp.int32) - 1

    slot = slot_of(*lat_spread)
    token = lat_inner % piece
    row = (slot >= pages_row).astype(jnp.int32)
    target = row * (per_row - pages_row * (piece // 2)) + token % 2 * half
    target = target + slot * (piece // 2) + token // 2
    target = jnp.where(slot >= 0, target, -1)
    slot = slot_of(*rope_spread)
    rope_target = jnp.where(slot >= 0, slot * rope_rows + rope_inner % rope_rows, -1)
    copies = []
    for b in range(rows):
        pick = ones_where(iota((half, 1), 0) + b * half == rope_target)
        rope_b = dot(pick, tail_ref[...])
        rope_b = jnp.concatenate([rope_b, pltpu.roll(rope_b, TAIL - rope_w, 1)], axis=0)
        lane = iota(rope_b.shape, 1)
        bias = bias_ref[b * per_row : (b + 1) * per_row]
        rope_b = jnp.where(lane < rope_w, rope_b, jnp.where(lane == rope_w, bias, 0.0))
        key_ref[b, :, lat_w:] = rope_b.astype(jnp.bfloat16)
        pick = ones_where(iota((per_row, 1), 0) + b * per_row == target)
        key_ref[b, :, :lat_w] = dot(pick, lat_ref[...]).astype(jnp.bfloat16)
        copy = pltpu.make_async_copy(key_ref.at[b], key_hbm.at[b], out_sem.at[b])
        copy.start()
        copies.append(copy)
    for copy in copies:
        copy.wait()


def attend(scale, key, query, lat_w):
    scores = dot(key, query)
    high = jnp.max(scores, axis=0, keepdims=True)
    weights = jnp.exp2((scores - high) * (scale * LOG2E))
    total = jnp.sum(weights, axis=0, keepdims=True)
    return high, total, dot(key[:, :lat_w].T, weights.astype(jnp.bfloat16))


def ask(q_refs, b):
    left = iota(q_refs[0].shape, 1) < q_refs[0].shape[1] // 2
    tiles = []
    for k in range(0, len(q_refs), 2):
        one, two = q_refs[k][...].astype(jnp.float32), q_refs[k + 1][...].astype(jnp.float32)
        first, second = (one, two) if b == 0 else (two, one)
        tiles.append(jnp.where(left, first, second).astype(jnp.bfloat16))
    return jnp.concatenate(tiles, axis=1)


def own_kernel(scale, key_ref, near_hbm, far_hbm, *refs):
    q_refs, (part_ref, stat_ref, half_a, half_b, sem_ref) = refs[:-5], refs[-5:]
    size = half_a.shape[0]
    copies = [
        pltpu.make_async_copy(near_hbm.at[pl.ds(0, size)], half_a, sem_ref.at[0]),
        pltpu.make_async_copy(far_hbm.at[pl.ds(size, size)], half_b, sem_ref.at[1]),
    ]
    for copy in copies:
        copy.start()
    for b in range(key_ref.shape[0]):
        high, total, part = attend(scale, key_ref[b], ask(q_refs, b), part_ref.shape[1])
        part_ref[b] = part
        stat_ref[b] = jnp.where(iota(stat_ref.shape[1:], 0) == 0, high, total)
    for copy in copies:
        copy.wait()


def both_kernel(scale, key_ref, own_ref, stat_ref, *refs):
    count = len(refs) // 2
    q_refs, out_refs = refs[:count], refs[count:]
    lat_w = own_ref.shape[1]
    queries = q_refs[0].shape[1]
    parts = []
    for b in range(key_ref.shape[0]):
        high, total, part = attend(scale, key_ref[b], ask(q_refs, b), lat_w)
        high_own, total_own = stat_ref[b, 0:1], stat_ref[b, 1:2]
        top = jnp.maximum(high, high_own)
        keep = jnp.exp2((high - top) * (scale * LOG2E))
        keep_own = jnp.exp2((high_own - top) * (scale * LOG2E))
        total = total * keep + total_own * keep_own
        inverse = 1.0 / total
        part = part * (keep * inverse) + own_ref[b] * (keep_own * inverse)
        hi, mid, low = split3(top * scale + jnp.log(total))
        mark = iota((INFO, part.shape[1]), 0)
        info = jnp.where(mark == 0, hi, jnp.where(mark == 1, mid, jnp.where(mark == 2, low, 0.0)))
        parts.append(jnp.concatenate([part, info], axis=0))
    left = iota((lat_w + INFO, queries), 1) < queries // 2
    for k in range(0, count, 2):
        lanes = slice(k * queries // 2, (k + 2) * queries // 2)
        one, two = parts[0][:, lanes], parts[1][:, lanes]
        out_refs[k][...] = jnp.where(left, one, two).astype(jnp.bfloat16)
        out_refs[k + 1][...] = jnp.where(left, two, one).astype(jnp.bfloat16)


def merge_kernel(rows_dev, fresh_ref, fresh_lse_ref, w_ref, *refs):
    part_refs, out_ref, lat_ref = refs[:-2], refs[-2], refs[-1]
    heads, lat_w, value_w = w_ref.shape
    width = out_ref.shape[1]
    steps = width // rows_dev
    half = fresh_ref.shape[1] // 2
    lses = [fresh_lse_ref[...]]
    for k, part_ref in enumerate(part_refs):
        info = jnp.sum(part_ref[lat_w:, :].astype(jnp.float32), axis=0, keepdims=True)
        info = jnp.broadcast_to(info, lses[0].shape)
        lses.append(pltpu.roll(info, half, 1) if k % 2 else info)
    high = functools.reduce(jnp.maximum, lses)
    shares = [jnp.exp(lse - high) for lse in lses]
    inverse = 1.0 / functools.reduce(jnp.add, shares)
    total = fresh_ref[...] * (shares[0] * inverse)[:1]
    swapped = 0.0
    for k, part_ref in enumerate(part_refs):
        share = shares[k + 1] * inverse
        part = part_ref[:lat_w, :].astype(jnp.float32)
        if k % 2:
            swapped = swapped + part * pltpu.roll(share, half, 1)[:1]
        else:
            total = total + part * share[:1]
    total = total + pltpu.roll(swapped, half, 1)
    shape = (heads * width, heads * width)
    to, at = iota(shape, 0), iota(shape, 1)
    wanted = (to % rows_dev * heads + to // width) * steps + to % width // rows_dev
    lat_ref[...] = dot_t(ones_where(at == wanted), total.astype(jnp.bfloat16))
    for head in range(heads):
        rows = lat_ref[head * width : (head + 1) * width, :].astype(jnp.bfloat16)
        value = dot(rows, w_ref[head]).astype(jnp.bfloat16)
        for copy in range(out_ref.shape[0]):
            out_ref[copy, :, head * value_w : (head + 1) * value_w] = value


def stage_kernel(own_hbm, near_hbm, far_hbm, out_ref, sem_ref):
    copies = [
        pltpu.make_async_copy(ref, out_ref.at[i], sem_ref.at[i])
        for i, ref in enumerate((own_hbm, near_hbm, far_hbm))
    ]
    for copy in copies:
        copy.start()
    for copy in copies:
        copy.wait()


def project_kernel(width, x_ref, w_ref, opp_a_hbm, opp_b_hbm, out_ref, opp_ref, sem_ref):
    size = opp_a_hbm.shape[0]
    copies = [
        pltpu.make_async_copy(opp_a_hbm, opp_ref.at[pl.ds(0, size)], sem_ref.at[0]),
        pltpu.make_async_copy(opp_b_hbm, opp_ref.at[pl.ds(size, size)], sem_ref.at[1]),
    ]
    for copy in copies:
        copy.start()
    here = lax.axis_index("row") // NZ

    def put(k, block):
        owner = (here + k) % NX
        for z in range(NZ):
            rows = block[z * width : (z + 1) * width]
            out_ref[z * NX + owner] = rows.astype(out_ref.dtype)

    for i, k in enumerate((0, NX - 1, 1)):
        put(k, dot_t(x_ref[...], w_ref[i]))
    for copy in copies:
        copy.wait()
    put(2, dot_t(x_ref[...], opp_ref[...]))


def sum_kernel(in_ref, keep_ref, send_ref):
    core = lax.axis_index("head") % 2
    per_core = keep_ref.shape[0]
    for i in range(per_core):
        for ref, half in ((keep_ref, core), (send_ref, 1 - core)):
            first = (half * per_core + i) * NX
            parts = [in_ref[first + y].astype(jnp.float32) for y in range(NX)]
            ref[i] = functools.reduce(jnp.add, parts)


def final_kernel(keep_ref, got_ref, out_ref):
    value = [keep_ref[i] + got_ref[i] for i in range(keep_ref.shape[0])]
    value = jnp.concatenate(value, axis=1)
    rows = out_ref.shape[1]
    for step in range(out_ref.shape[0]):
        out_ref[step] = value[step * rows : (step + 1) * rows].astype(out_ref.dtype)


def shift_y(x, n_head, k):
    cores = n_head // NX
    if k % NX == 0:
        return x
    return lax.ppermute(x, "head", [(h, (h + k * cores) % n_head) for h in range(n_head)])


def shift_x(x, k):
    return lax.ppermute(
        x,
        "row",
        [(a * NZ + b, (a + k) % NX * NZ + b) for a in range(NX) for b in range(NZ)],
    )


def on_device(
    q_nope,
    q_rope,
    new_latent,
    new_rope,
    latent_pages,
    rope_pages,
    dest_rows,
    dest_slots,
    page_table,
    lengths,
    w_uk,
    w_uv,
    w_o,
):
    bf16, f32 = jnp.bfloat16, jnp.float32
    n_row = lax.axis_size("row")
    n_head = lax.axis_size("head")
    row, head = lax.axis_index("row"), lax.axis_index("head")
    rows_dev, pages_row = page_table.shape
    pages, page_len, lat_w = latent_pages.shape
    rope_w = new_rope.shape[-1]
    steps, _, heads, nope_w = q_nope.shape
    value_w = w_uv.shape[-1]
    piece = page_len // n_head
    per_pair = 2 * (pages // n_row) + min(pages % n_row, 1)
    scale = 1.0 / (nope_w + rope_w) ** 0.5
    width = steps * rows_dev
    queries = heads * width
    tokens = pages * piece
    slots = n_row * per_pair * piece

    lat_rows = per_pair * piece * lat_w // TAIL
    rope_rows = per_pair * piece * rope_w // TAIL
    block = lat_rows + (rope_rows + 8) // 8 * 8
    send = call(
        functools.partial(pack_kernel, rows_dev, pages_row, per_pair),
        jax.ShapeDtypeStruct((n_row, block, TAIL), bf16),
        [dest_rows[None, :], dest_slots[None, :], latent_pages, rope_pages],
        scratch=[
            pltpu.VMEM((1, pages), jnp.int32),
            pltpu.VMEM((1, pages), jnp.int32),
            pltpu.VMEM((tokens, lat_w), bf16),
            pltpu.VMEM((pages, 2 * piece, lat_w), bf16),
            pltpu.VMEM((pages, piece * rope_w), bf16),
            pltpu.VMEM((n_row, block, TAIL), bf16),
            pltpu.SemaphoreType.DMA((7,)),
            pltpu.SemaphoreType.DMA((4,)),
        ],
        flops=2 * slots * tokens * lat_w,
        nbytes=2 * (slots + 2 * tokens) * lat_w,
        mem=60,
        out_spec=HBM,
        in_hbm=(0, 1, 2, 3),
    )
    got = lax.all_to_all(send, "row", split_axis=0, concat_axis=0, tiled=True)

    qn = jnp.transpose(q_nope, (2, 1, 0, 3)).reshape(heads, width, nope_w)
    qr = q_rope.reshape(steps, rows_dev, heads, rope_w)
    qr = jnp.transpose(qr, (1, 2, 0, 3)).reshape(queries, rope_w)
    one_lane = jnp.arange(TAIL - rope_w, dtype=jnp.int32)[None, :] == 0
    q_tail = jnp.concatenate(
        [qr, jnp.broadcast_to(one_lane, (queries, TAIL - rope_w)).astype(bf16)], axis=1
    )
    fresh = jnp.concatenate(
        [
            new_latent.reshape(width, lat_w),
            new_rope.reshape(width, rope_w),
            jnp.zeros((width, TAIL - rope_w), bf16),
        ],
        axis=1,
    )
    fresh = jnp.concatenate([fresh, jnp.zeros((-width % 16, lat_w + TAIL), bf16)], axis=0)
    query, swapped, fresh_part, fresh_lse = call(
        functools.partial(query_kernel, scale, rows_dev),
        (
            jax.ShapeDtypeStruct((lat_w + TAIL, queries), bf16),
            jax.ShapeDtypeStruct((lat_w + TAIL, queries), bf16),
            jax.ShapeDtypeStruct((lat_w, queries), f32),
            jax.ShapeDtypeStruct((8, queries), f32),
        ),
        [qn, q_tail, w_uk, fresh, fresh[:, :lat_w].T],
        scratch=[pltpu.VMEM((queries, lat_w), f32)],
        flops=2 * queries * nope_w * lat_w,
        nbytes=2 * heads * nope_w * lat_w,
    )
    all_queries = [shift_y((query, swapped)[k % 2], n_head, k) for k in range(NX)]

    w_t = w_o.T
    w_near, w_far = shift_x(w_t, 1), shift_x(w_t, -1)

    slot_ids = jnp.arange(pages_row, dtype=jnp.int32)
    holds = (page_table[:, :, None] == slot_ids[None, None, :]).astype(jnp.int32)
    logical = jnp.sum(holds * slot_ids[None, :, None], axis=1)
    limit = lengths[:, None] - logical * page_len - head * piece
    within = jnp.arange(piece, dtype=jnp.int32).reshape(piece // 2, 2).T
    usable = within[None, :, None, :] < limit[:, None, :, None]
    bias = jnp.where(usable, 0.0, NEG).astype(f32).reshape(rows_dev * pages_row * piece, 1)

    got, w_near, w_far, all_queries = lax.optimization_barrier((got, w_near, w_far, all_queries))
    key = call(
        functools.partial(gather_kernel, piece, per_pair, rope_w, pages_row),
        jax.ShapeDtypeStruct((rows_dev, pages_row * piece, lat_w + TAIL), bf16),
        [got, bias],
        scratch=[
            pltpu.VMEM(got.shape, bf16),
            pltpu.VMEM((slots, lat_w), bf16),
            pltpu.VMEM((n_row * (block - lat_rows), TAIL), bf16),
            pltpu.VMEM((rows_dev, pages_row * piece, lat_w + TAIL), bf16),
            pltpu.SemaphoreType.DMA((4,)),
            pltpu.SemaphoreType.DMA((rows_dev,)),
        ],
        flops=2 * slots * tokens * lat_w,
        nbytes=2 * slots * lat_w,
        out_spec=HBM,
        in_hbm=(0,),
    )
    other = lax.ppermute(key, "head", [(h, h ^ 1) for h in range(n_head)])
    asked = NX * queries // rows_dev
    half_w = jax.ShapeDtypeStruct((w_t.shape[0] // 2, w_t.shape[1]), bf16)
    own_part, own_stat, half_a, half_b = call(
        functools.partial(own_kernel, scale),
        (
            jax.ShapeDtypeStruct((rows_dev, lat_w, asked), f32),
            jax.ShapeDtypeStruct((rows_dev, 8, asked), f32),
            half_w,
            half_w,
        ),
        [key, w_near, w_far] + all_queries,
        scratch=[pltpu.SemaphoreType.DMA((2,))],
        flops=2 * tokens * asked * (2 * lat_w + TAIL),
        nbytes=2 * tokens * lat_w,
        out_spec=(VMEM, VMEM, HBM, HBM),
        in_hbm=(1, 2),
    )
    opposite = [shift_x(half_a, 1), shift_x(half_b, -1)]
    parts = call(
        functools.partial(both_kernel, scale),
        tuple(jax.ShapeDtypeStruct((lat_w + INFO, queries), bf16) for _ in range(NX)),
        [other, own_part, own_stat] + all_queries,
        flops=2 * tokens * asked * (2 * lat_w + TAIL),
        nbytes=2 * tokens * lat_w,
    )
    parts = [shift_y(part, n_head, -k) for k, part in enumerate(parts)]
    head_out = call(
        functools.partial(merge_kernel, rows_dev),
        jax.ShapeDtypeStruct((NZ, width, heads * value_w), bf16),
        [fresh_part, fresh_lse, w_uv] + parts,
        scratch=[pltpu.VMEM((queries, lat_w), f32)],
        flops=2 * queries * lat_w * value_w,
        nbytes=2 * heads * lat_w * value_w,
    )

    rings = [[a * NZ + b for b in range(NZ)] for a in range(NX)]
    ring = lax.all_to_all(
        head_out, "row", split_axis=0, concat_axis=0, axis_index_groups=rings, tiled=True
    )
    cols = w_o.shape[1]
    cores = n_head // NX
    w_ring = call(
        stage_kernel,
        jax.ShapeDtypeStruct((3,) + w_t.shape, bf16),
        [w_t, w_near, w_far],
        scratch=[pltpu.SemaphoreType.DMA((3,))],
        nbytes=12 * w_o.size,
        in_hbm=(0, 1, 2),
    )
    sums = call(
        functools.partial(project_kernel, width),
        jax.ShapeDtypeStruct((NZ * NX, width, cols), bf16),
        [ring.reshape(NZ * width, heads * value_w), w_ring] + opposite,
        scratch=[pltpu.VMEM(w_t.shape, bf16), pltpu.SemaphoreType.DMA((2,))],
        flops=2 * NX * NZ * width * w_o.size,
        nbytes=2 * NX * w_o.size,
        in_hbm=(2, 3),
    )
    planes = [
        [(x * NZ + z) * n_head + y * cores + core for z in range(NZ) for y in range(NX)]
        for x in range(NX)
        for core in range(cores)
    ]
    sums = lax.all_to_all(
        sums,
        ("row", "head"),
        split_axis=0,
        concat_axis=0,
        axis_index_groups=planes,
        tiled=True,
    )
    half = jax.ShapeDtypeStruct((NZ // cores, width, cols), f32)
    keep, give = call(sum_kernel, (half, half), [sums])
    taken = lax.ppermute(give, "head", [(h, h ^ 1) for h in range(n_head)])
    return call(
        final_kernel,
        jax.ShapeDtypeStruct((steps, rows_dev, NZ // cores * cols), bf16),
        [keep, taken],
    )


def solution(mesh):
    placed = (
        P(None, "row", "head", None),
        P(None, "row", "head"),
        P(None, "row", None),
        P(None, "row", None),
        P("row", None, None),
        P("row", None),
        P("row"),
        P("row"),
        P("row", None),
        P("row"),
        P("head", None, None),
        P("head", None, None),
        P("head", "row"),
    )
    return jax.shard_map(
        on_device, mesh=mesh, in_specs=placed, out_specs=P(None, "row", "head"), check_vma=False
    )
```

```python
import functools

import jax
import jax.numpy as jnp
from jax import lax
from jax.experimental import pallas as pl
from jax.experimental.pallas import tpu as pltpu
from jax.sharding import PartitionSpec as P

NX = 4
NZ = 8
TAIL = 128
INFO = 16
NEG = -1e30
LOG2E = 1.4426950408889634
LN2 = 0.6931471805599453

VMEM = pl.BlockSpec(memory_space=pltpu.VMEM)
SMEM = pl.BlockSpec(memory_space=pltpu.SMEM)
HBM = pl.BlockSpec(memory_space=pltpu.HBM)


def call(
    body, out_shape, ins, scratch=(), flops=0, nbytes=0, mem=24, out_spec=VMEM, in_hbm=()
):
    return pl.pallas_call(
        body,
        out_shape=out_shape,
        in_specs=[
            HBM if i in in_hbm else SMEM if a.dtype == jnp.int32 and a.ndim == 1 else VMEM
            for i, a in enumerate(ins)
        ],
        out_specs=out_spec
        if isinstance(out_spec, tuple)
        else jax.tree.map(lambda _: out_spec, out_shape),
        scratch_shapes=list(scratch),
        compiler_params=pltpu.CompilerParams(vmem_limit_bytes=mem * 2**20),
        cost_estimate=pl.CostEstimate(flops=flops, bytes_accessed=nbytes, transcendentals=0),
    )(*ins)


def dot(a, b):
    return lax.dot_general(a, b, (((1,), (0,)), ((), ())), preferred_element_type=jnp.float32)


def dot_t(a, b):
    return lax.dot_general(a, b, (((1,), (1,)), ((), ())), preferred_element_type=jnp.float32)


def iota(shape, dim):
    return lax.broadcasted_iota(jnp.int32, shape, dim)


def ones_where(mask):
    return jnp.where(mask, 1.0, 0.0).astype(jnp.bfloat16)


def pack_kernel(
    rows_dev,
    pages_row,
    per_pair,
    rows_hbm,
    slots_hbm,
    lat_hbm,
    rope_hbm,
    out_hbm,
    rows_ref,
    slots_ref,
    lat_ref,
    lat_buf,
    rope_buf,
    buf_ref,
    in_sem,
    out_sem,
):
    pages, both, lat_w = lat_buf.shape
    piece = both // 2
    count, block, _ = buf_ref.shape
    chunks = out_sem.shape[0]
    cuts = lat_w // TAIL
    rope_rows = rope_buf.shape[1] // TAIL
    lat_rows = per_pair * cuts * piece
    head = lax.axis_index("head")
    lists = [
        pltpu.make_async_copy(rows_hbm, rows_ref, in_sem.at[0]),
        pltpu.make_async_copy(slots_hbm, slots_ref, in_sem.at[1]),
    ]
    for copy in lists:
        copy.start()
    lane0 = pl.multiple_of(head * rope_buf.shape[1], rope_buf.shape[1])
    rope_copy = pltpu.make_async_copy(
        rope_hbm.at[:, pl.ds(lane0, rope_buf.shape[1])], rope_buf, in_sem.at[2]
    )
    rope_copy.start()
    first = pl.multiple_of(head // 2 * both, both)
    cut = pages // chunks
    lat_copies = []
    for i in range(chunks):
        here = pl.ds(i * cut, cut)
        copy = pltpu.make_async_copy(
            lat_hbm.at[here, pl.ds(first, both), :], lat_buf.at[here], in_sem.at[3 + i]
        )
        copy.start()
        lat_copies.append(copy)
    for copy in lists:
        copy.wait()

    dest = rows_ref[...] // rows_dev
    label = (rows_ref[...] % rows_dev * pages_row + slots_ref[...] + 1).astype(jnp.float32)
    owned = jnp.where(iota((count, pages), 0) == dest, 1.0, 0.0)
    before = ones_where(iota((pages, pages), 0) < iota((pages, pages), 1))
    rank = jnp.sum(owned * dot(owned.astype(jnp.bfloat16), before), axis=0, keepdims=True)
    rank = rank.astype(jnp.int32)
    at_slot = (dest * per_pair + rank).astype(jnp.float32).astype(jnp.bfloat16)
    spread = ones_where(iota((pages, pages * piece), 0) == iota((pages, pages * piece), 1) // piece)
    at_slot = dot(jnp.broadcast_to(at_slot, (8, pages)), spread)[:1].astype(jnp.int32)
    place = at_slot * piece + iota((1, pages * piece), 1) % piece

    label_lane = iota((TAIL, pages), 0)
    named = ones_where((label_lane // piece == rank) & (label_lane < per_pair * piece))
    labels = dot_t((owned * label).astype(jnp.bfloat16), named).astype(jnp.bfloat16)
    rest = block - lat_rows
    row = iota((count * rest, 1), 0)
    tail = dot(
        ones_where(row == iota((1, count), 1) * rest + per_pair * rope_rows), labels
    )
    rope_copy.wait()
    for j in range(rope_rows):
        pick = ones_where(row == dest * rest + rank * rope_rows + j)
        tail = tail + dot(pick, rope_buf[:, j * TAIL : (j + 1) * TAIL])
    buf_ref[:, lat_rows:, :] = tail.reshape(count, rest, TAIL).astype(jnp.bfloat16)

    for i, copy in enumerate(lat_copies):
        copy.wait()
        lat = lat_buf[i * cut : (i + 1) * cut].astype(jnp.float32).reshape(cut, 2, piece, lat_w)
        lat = jnp.where(head % 2 == 1, lat[:, 1], lat[:, 0]).reshape(cut * piece, lat_w)
        lat_ref[i * cut * piece : (i + 1) * cut * piece, :] = lat.astype(jnp.bfloat16)
    lat = lat_ref[...]
    step = count // chunks
    copies = []
    for i in range(chunks):
        rows = step * per_pair * piece
        value = dot(ones_where(iota((rows, 1), 0) + i * rows == place), lat)
        value = [
            value[:, c * TAIL : (c + 1) * TAIL].reshape(step * per_pair, 1, piece, TAIL)
            for c in range(cuts)
        ]
        value = jnp.concatenate(value, axis=1).reshape(step, lat_rows, TAIL)
        here = pl.ds(i * step, step)
        buf_ref[here, :lat_rows, :] = value.astype(jnp.bfloat16)
        copy = pltpu.make_async_copy(buf_ref.at[here], out_hbm.at[here], out_sem.at[i])
        copy.start()
        copies.append(copy)
    for copy in copies:
        copy.wait()


def split3(x):
    hi = x.astype(jnp.bfloat16)
    rest = x - hi.astype(jnp.float32)
    mid = rest.astype(jnp.bfloat16)
    low = (rest - mid.astype(jnp.float32)).astype(jnp.bfloat16)
    return hi.astype(jnp.float32), mid.astype(jnp.float32), low.astype(jnp.float32)


def query_kernel(
    scale, rows, qn_ref, qtail_ref, w_ref, fresh_ref, fresh_t_ref, q_ref, swap_ref, part_ref, lse_ref, acc_ref
):
    heads, width, _ = qn_ref.shape
    lat_w = w_ref.shape[2]
    steps = width // rows
    for head in range(heads):
        absorbed = dot(qn_ref[head], w_ref[head])
        for row in range(rows):
            at = (row * heads + head) * steps
            acc_ref[at : at + steps, :] = absorbed[row * steps : (row + 1) * steps]
    half = rows * heads * steps // 2
    absorbed = acc_ref[...].T
    tail = qtail_ref[...].astype(jnp.float32).T
    q_ref[:lat_w, :] = absorbed.astype(jnp.bfloat16)
    q_ref[lat_w:, :] = tail.astype(jnp.bfloat16)
    swap_ref[:lat_w, :] = pltpu.roll(absorbed, half, 1).astype(jnp.bfloat16)
    swap_ref[lat_w:, :] = pltpu.roll(tail, half, 1).astype(jnp.bfloat16)
    scores = dot(fresh_ref[...], q_ref[...]) * scale
    shape = scores.shape
    token = iota(shape, 0)
    query = iota(shape, 1)
    allowed = (query // (heads * steps) == token % rows) & (token // rows <= query % steps)
    scores = jnp.where(allowed, scores, NEG)
    high = jnp.max(scores, axis=0, keepdims=True)
    weights = jnp.exp(scores - high)
    total = jnp.sum(weights, axis=0, keepdims=True)
    part_ref[...] = dot(fresh_t_ref[...], weights.astype(jnp.bfloat16)) * (1.0 / total)
    lse_ref[...] = jnp.broadcast_to(high + jnp.log(total), lse_ref.shape)


def gather_kernel(
    piece,
    per_pair,
    rope_w,
    pages_row,
    block_hbm,
    bias_ref,
    key_hbm,
    block_ref,
    lat_ref,
    tail_ref,
    key_ref,
    in_sem,
    out_sem,
):
    rows, per_row, key_w = key_ref.shape
    count, block, _ = block_ref.shape
    cuts = (key_w - TAIL) // TAIL
    lat_w = cuts * TAIL
    pair_tokens = per_pair * piece
    lat_rows = pair_tokens * cuts
    rest = block - lat_rows
    rope_rows = piece * rope_w // TAIL
    half = per_row // 2

    chunks = in_sem.shape[0]
    step = count // chunks
    copies = []
    for i in range(chunks):
        here = pl.ds(i * step, step)
        copy = pltpu.make_async_copy(block_hbm.at[here], block_ref.at[here], in_sem.at[i])
        copy.start()
        copies.append(copy)

    def spread_over(columns, group, lane):
        own = iota((count, columns), 0) == iota((1, columns), 1) // group
        return ones_where(iota((TAIL, columns), 0) == lane), jnp.where(own, 1.0, 0.0)

    lat_columns = count * pair_tokens
    lat_inner = iota((1, lat_columns), 1) % pair_tokens
    lat_spread = spread_over(lat_columns, pair_tokens, lat_inner)
    rope_columns = count * rest
    rope_inner = iota((1, rope_columns), 1) % rest
    lane = jnp.where(rope_inner < per_pair * rope_rows, rope_inner // rope_rows * piece, TAIL)
    rope_spread = spread_over(rope_columns, rest, lane)

    labels = []
    for i, copy in enumerate(copies):
        copy.wait()
        here = slice(i * step, (i + 1) * step)
        tail = block_ref[here, lat_rows:, :].astype(jnp.float32)
        marked = iota(tail.shape, 1) == per_pair * rope_rows
        labels.append(jnp.sum(jnp.where(marked, tail, 0.0), axis=1))
        tail_ref[i * step * rest : (i + 1) * step * rest, :] = tail.reshape(
            step * rest, TAIL
        ).astype(jnp.bfloat16)
        lat = block_ref[here, :lat_rows, :].astype(jnp.float32)
        lat = lat.reshape(step * per_pair, cuts, piece, TAIL)
        for c in range(cuts):
            lat_ref[i * step * pair_tokens : (i + 1) * step * pair_tokens, pl.ds(c * TAIL, TAIL)] = (
                lat[:, c].reshape(step * pair_tokens, TAIL).astype(jnp.bfloat16)
            )
    labels = jnp.concatenate(labels, axis=0).astype(jnp.bfloat16)

    def slot_of(spread, own):
        wide = dot(labels, spread) * own
        return jnp.sum(wide, axis=0, keepdims=True).astype(jnp.int32) - 1

    slot = slot_of(*lat_spread)
    token = lat_inner % piece
    row = (slot >= pages_row).astype(jnp.int32)
    target = row * (per_row - pages_row * (piece // 2)) + token % 2 * half
    target = target + slot * (piece // 2) + token // 2
    target = jnp.where(slot >= 0, target, -1)
    slot = slot_of(*rope_spread)
    rope_target = jnp.where(slot >= 0, slot * rope_rows + rope_inner % rope_rows, -1)
    copies = []
    for b in range(rows):
        pick = ones_where(iota((half, 1), 0) + b * half == rope_target)
        rope_b = dot(pick, tail_ref[...])
        rope_b = jnp.concatenate([rope_b, pltpu.roll(rope_b, TAIL - rope_w, 1)], axis=0)
        lane = iota(rope_b.shape, 1)
        bias = bias_ref[b * per_row : (b + 1) * per_row]
        rope_b = jnp.where(lane < rope_w, rope_b, jnp.where(lane == rope_w, bias, 0.0))
        key_ref[b, :, lat_w:] = rope_b.astype(jnp.bfloat16)
        pick = ones_where(iota((per_row, 1), 0) + b * per_row == target)
        key_ref[b, :, :lat_w] = dot(pick, lat_ref[...]).astype(jnp.bfloat16)
        copy = pltpu.make_async_copy(key_ref.at[b], key_hbm.at[b], out_sem.at[b])
        copy.start()
        copies.append(copy)
    for copy in copies:
        copy.wait()


def attend(scale, key, query, lat_w):
    scores = dot(key, query)
    high = jnp.max(scores, axis=0, keepdims=True)
    weights = jnp.exp2((scores - high) * (scale * LOG2E))
    total = jnp.sum(weights, axis=0, keepdims=True)
    return high, total, dot(key[:, :lat_w].T, weights.astype(jnp.bfloat16))


def ask(q_refs, b):
    left = iota(q_refs[0].shape, 1) < q_refs[0].shape[1] // 2
    tiles = []
    for k in range(0, len(q_refs), 2):
        one, two = q_refs[k][...].astype(jnp.float32), q_refs[k + 1][...].astype(jnp.float32)
        first, second = (one, two) if b == 0 else (two, one)
        tiles.append(jnp.where(left, first, second).astype(jnp.bfloat16))
    return jnp.concatenate(tiles, axis=1)


def own_kernel(scale, key_ref, *refs):
    q_refs, (part_ref, stat_ref) = refs[:-2], refs[-2:]
    for b in range(key_ref.shape[0]):
        high, total, part = attend(scale, key_ref[b], ask(q_refs, b), part_ref.shape[1])
        part_ref[b] = part
        stat_ref[b] = jnp.where(iota(stat_ref.shape[1:], 0) == 0, high, total)


def both_kernel(scale, key_ref, own_ref, stat_ref, *refs):
    count = len(refs) // 2
    q_refs, out_refs = refs[:count], refs[count:]
    lat_w = own_ref.shape[1]
    queries = q_refs[0].shape[1]
    parts = []
    for b in range(key_ref.shape[0]):
        high, total, part = attend(scale, key_ref[b], ask(q_refs, b), lat_w)
        high_own, total_own = stat_ref[b, 0:1], stat_ref[b, 1:2]
        top = jnp.maximum(high, high_own)
        keep = jnp.exp2((high - top) * (scale * LOG2E))
        keep_own = jnp.exp2((high_own - top) * (scale * LOG2E))
        total = total * keep + total_own * keep_own
        inverse = 1.0 / total
        part = part * (keep * inverse) + own_ref[b] * (keep_own * inverse)
        hi, mid, low = split3(top * scale + jnp.log(total))
        mark = iota((INFO, part.shape[1]), 0)
        info = jnp.where(mark == 0, hi, jnp.where(mark == 1, mid, jnp.where(mark == 2, low, 0.0)))
        parts.append(jnp.concatenate([part, info], axis=0))
    left = iota((lat_w + INFO, queries), 1) < queries // 2
    for k in range(0, count, 2):
        lanes = slice(k * queries // 2, (k + 2) * queries // 2)
        one, two = parts[0][:, lanes], parts[1][:, lanes]
        out_refs[k][...] = jnp.where(left, one, two).astype(jnp.bfloat16)
        out_refs[k + 1][...] = jnp.where(left, two, one).astype(jnp.bfloat16)


def merge_kernel(rows_dev, fresh_ref, fresh_lse_ref, w_ref, *refs):
    part_refs, out_ref, lat_ref = refs[:-2], refs[-2], refs[-1]
    heads, lat_w, value_w = w_ref.shape
    width = out_ref.shape[1]
    steps = width // rows_dev
    half = fresh_ref.shape[1] // 2
    lses = [fresh_lse_ref[...]]
    for k, part_ref in enumerate(part_refs):
        info = jnp.sum(part_ref[lat_w:, :].astype(jnp.float32), axis=0, keepdims=True)
        info = jnp.broadcast_to(info, lses[0].shape)
        lses.append(pltpu.roll(info, half, 1) if k % 2 else info)
    high = functools.reduce(jnp.maximum, lses)
    shares = [jnp.exp(lse - high) for lse in lses]
    inverse = 1.0 / functools.reduce(jnp.add, shares)
    total = fresh_ref[...] * (shares[0] * inverse)[:1]
    swapped = 0.0
    for k, part_ref in enumerate(part_refs):
        share = shares[k + 1] * inverse
        part = part_ref[:lat_w, :].astype(jnp.float32)
        if k % 2:
            swapped = swapped + part * pltpu.roll(share, half, 1)[:1]
        else:
            total = total + part * share[:1]
    total = total + pltpu.roll(swapped, half, 1)
    shape = (heads * width, heads * width)
    to, at = iota(shape, 0), iota(shape, 1)
    wanted = (to % rows_dev * heads + to // width) * steps + to % width // rows_dev
    lat_ref[...] = dot_t(ones_where(at == wanted), total.astype(jnp.bfloat16))
    for head in range(heads):
        rows = lat_ref[head * width : (head + 1) * width, :].astype(jnp.bfloat16)
        value = dot(rows, w_ref[head]).astype(jnp.bfloat16)
        for copy in range(out_ref.shape[0]):
            out_ref[copy, :, head * value_w : (head + 1) * value_w] = value


def stage_kernel(own_hbm, near_hbm, far_hbm, out_ref, sem_ref):
    copies = [
        pltpu.make_async_copy(ref, out_ref.at[i], sem_ref.at[i])
        for i, ref in enumerate((own_hbm, near_hbm, far_hbm))
    ]
    for copy in copies:
        copy.start()
    for copy in copies:
        copy.wait()


def project_kernel(width, x_ref, w_ref, opp_a_hbm, opp_b_hbm, out_ref, opp_ref, sem_ref):
    size = opp_a_hbm.shape[0]
    copies = [
        pltpu.make_async_copy(opp_a_hbm, opp_ref.at[pl.ds(0, size)], sem_ref.at[0]),
        pltpu.make_async_copy(opp_b_hbm, opp_ref.at[pl.ds(size, size)], sem_ref.at[1]),
    ]
    for copy in copies:
        copy.start()
    here = lax.axis_index("row") // NZ

    def put(k, block):
        owner = (here + k) % NX
        for z in range(NZ):
            rows = block[z * width : (z + 1) * width]
            out_ref[z * NX + owner] = rows.astype(out_ref.dtype)

    for i, k in enumerate((0, NX - 1, 1)):
        put(k, dot_t(x_ref[...], w_ref[i]))
    for copy in copies:
        copy.wait()
    put(2, dot_t(x_ref[...], opp_ref[...]))


def sum_kernel(in_ref, keep_ref, send_ref):
    core = lax.axis_index("head") % 2
    per_core = keep_ref.shape[0]
    for i in range(per_core):
        for ref, half in ((keep_ref, core), (send_ref, 1 - core)):
            first = (half * per_core + i) * NX
            parts = [in_ref[first + y].astype(jnp.float32) for y in range(NX)]
            ref[i] = functools.reduce(jnp.add, parts)


def final_kernel(keep_ref, got_ref, out_ref):
    value = [keep_ref[i] + got_ref[i] for i in range(keep_ref.shape[0])]
    value = jnp.concatenate(value, axis=1)
    rows = out_ref.shape[1]
    for step in range(out_ref.shape[0]):
        out_ref[step] = value[step * rows : (step + 1) * rows].astype(out_ref.dtype)


def shift_y(x, n_head, k):
    cores = n_head // NX
    if k % NX == 0:
        return x
    return lax.ppermute(x, "head", [(h, (h + k * cores) % n_head) for h in range(n_head)])


def shift_x(x, k):
    return lax.ppermute(
        x,
        "row",
        [(a * NZ + b, (a + k) % NX * NZ + b) for a in range(NX) for b in range(NZ)],
    )


def on_device(
    q_nope,
    q_rope,
    new_latent,
    new_rope,
    latent_pages,
    rope_pages,
    dest_rows,
    dest_slots,
    page_table,
    lengths,
    w_uk,
    w_uv,
    w_o,
):
    bf16, f32 = jnp.bfloat16, jnp.float32
    n_row = lax.axis_size("row")
    n_head = lax.axis_size("head")
    row, head = lax.axis_index("row"), lax.axis_index("head")
    rows_dev, pages_row = page_table.shape
    pages, page_len, lat_w = latent_pages.shape
    rope_w = new_rope.shape[-1]
    steps, _, heads, nope_w = q_nope.shape
    value_w = w_uv.shape[-1]
    piece = page_len // n_head
    per_pair = 2 * (pages // n_row) + min(pages % n_row, 1)
    scale = 1.0 / (nope_w + rope_w) ** 0.5
    width = steps * rows_dev
    queries = heads * width
    tokens = pages * piece
    slots = n_row * per_pair * piece

    lat_rows = per_pair * piece * lat_w // TAIL
    rope_rows = per_pair * piece * rope_w // TAIL
    block = lat_rows + (rope_rows + 8) // 8 * 8
    send = call(
        functools.partial(pack_kernel, rows_dev, pages_row, per_pair),
        jax.ShapeDtypeStruct((n_row, block, TAIL), bf16),
        [dest_rows[None, :], dest_slots[None, :], latent_pages, rope_pages],
        scratch=[
            pltpu.VMEM((1, pages), jnp.int32),
            pltpu.VMEM((1, pages), jnp.int32),
            pltpu.VMEM((tokens, lat_w), bf16),
            pltpu.VMEM((pages, 2 * piece, lat_w), bf16),
            pltpu.VMEM((pages, piece * rope_w), bf16),
            pltpu.VMEM((n_row, block, TAIL), bf16),
            pltpu.SemaphoreType.DMA((7,)),
            pltpu.SemaphoreType.DMA((4,)),
        ],
        flops=2 * slots * tokens * lat_w,
        nbytes=2 * (slots + 2 * tokens) * lat_w,
        mem=60,
        out_spec=HBM,
        in_hbm=(0, 1, 2, 3),
    )
    got = lax.all_to_all(send, "row", split_axis=0, concat_axis=0, tiled=True)

    qn = jnp.transpose(q_nope, (2, 1, 0, 3)).reshape(heads, width, nope_w)
    qr = q_rope.reshape(steps, rows_dev, heads, rope_w)
    qr = jnp.transpose(qr, (1, 2, 0, 3)).reshape(queries, rope_w)
    one_lane = jnp.arange(TAIL - rope_w, dtype=jnp.int32)[None, :] == 0
    q_tail = jnp.concatenate(
        [qr, jnp.broadcast_to(one_lane, (queries, TAIL - rope_w)).astype(bf16)], axis=1
    )
    fresh = jnp.concatenate(
        [
            new_latent.reshape(width, lat_w),
            new_rope.reshape(width, rope_w),
            jnp.zeros((width, TAIL - rope_w), bf16),
        ],
        axis=1,
    )
    fresh = jnp.concatenate([fresh, jnp.zeros((-width % 16, lat_w + TAIL), bf16)], axis=0)
    query, swapped, fresh_part, fresh_lse = call(
        functools.partial(query_kernel, scale, rows_dev),
        (
            jax.ShapeDtypeStruct((lat_w + TAIL, queries), bf16),
            jax.ShapeDtypeStruct((lat_w + TAIL, queries), bf16),
            jax.ShapeDtypeStruct((lat_w, queries), f32),
            jax.ShapeDtypeStruct((8, queries), f32),
        ),
        [qn, q_tail, w_uk, fresh, fresh[:, :lat_w].T],
        scratch=[pltpu.VMEM((queries, lat_w), f32)],
        flops=2 * queries * nope_w * lat_w,
        nbytes=2 * heads * nope_w * lat_w,
    )
    all_queries = [shift_y((query, swapped)[k % 2], n_head, k) for k in range(NX)]

    w_t = w_o.T
    w_near, w_far = shift_x(w_t, 1), shift_x(w_t, -1)

    slot_ids = jnp.arange(pages_row, dtype=jnp.int32)
    holds = (page_table[:, :, None] == slot_ids[None, None, :]).astype(jnp.int32)
    logical = jnp.sum(holds * slot_ids[None, :, None], axis=1)
    limit = lengths[:, None] - logical * page_len - head * piece
    within = jnp.arange(piece, dtype=jnp.int32).reshape(piece // 2, 2).T
    usable = within[None, :, None, :] < limit[:, None, :, None]
    bias = jnp.where(usable, 0.0, NEG).astype(f32).reshape(rows_dev * pages_row * piece, 1)

    got, w_near, w_far, all_queries = lax.optimization_barrier((got, w_near, w_far, all_queries))
    key = call(
        functools.partial(gather_kernel, piece, per_pair, rope_w, pages_row),
        jax.ShapeDtypeStruct((rows_dev, pages_row * piece, lat_w + TAIL), bf16),
        [got, bias],
        scratch=[
            pltpu.VMEM(got.shape, bf16),
            pltpu.VMEM((slots, lat_w), bf16),
            pltpu.VMEM((n_row * (block - lat_rows), TAIL), bf16),
            pltpu.VMEM((rows_dev, pages_row * piece, lat_w + TAIL), bf16),
            pltpu.SemaphoreType.DMA((4,)),
            pltpu.SemaphoreType.DMA((rows_dev,)),
        ],
        flops=2 * slots * tokens * lat_w,
        nbytes=2 * slots * lat_w,
        out_spec=HBM,
        in_hbm=(0,),
    )
    other = lax.ppermute(key, "head", [(h, h ^ 1) for h in range(n_head)])
    asked = NX * queries // rows_dev
    own_part, own_stat = call(
        functools.partial(own_kernel, scale),
        (
            jax.ShapeDtypeStruct((rows_dev, lat_w, asked), f32),
            jax.ShapeDtypeStruct((rows_dev, 8, asked), f32),
        ),
        [key] + all_queries,
        flops=2 * tokens * asked * (2 * lat_w + TAIL),
        nbytes=2 * tokens * lat_w,
    )
    size = w_t.shape[0] // 2
    opposite = [shift_x(w_near[:size], 1), shift_x(w_far[size:], -1)]
    parts = call(
        functools.partial(both_kernel, scale),
        tuple(jax.ShapeDtypeStruct((lat_w + INFO, queries), bf16) for _ in range(NX)),
        [other, own_part, own_stat] + all_queries,
        flops=2 * tokens * asked * (2 * lat_w + TAIL),
        nbytes=2 * tokens * lat_w,
    )
    parts = [shift_y(part, n_head, -k) for k, part in enumerate(parts)]
    head_out = call(
        functools.partial(merge_kernel, rows_dev),
        jax.ShapeDtypeStruct((NZ, width, heads * value_w), bf16),
        [fresh_part, fresh_lse, w_uv] + parts,
        scratch=[pltpu.VMEM((queries, lat_w), f32)],
        flops=2 * queries * lat_w * value_w,
        nbytes=2 * heads * lat_w * value_w,
    )

    rings = [[a * NZ + b for b in range(NZ)] for a in range(NX)]
    ring = lax.all_to_all(
        head_out, "row", split_axis=0, concat_axis=0, axis_index_groups=rings, tiled=True
    )
    cols = w_o.shape[1]
    cores = n_head // NX
    w_ring = call(
        stage_kernel,
        jax.ShapeDtypeStruct((3,) + w_t.shape, bf16),
        [w_t, w_near, w_far],
        scratch=[pltpu.SemaphoreType.DMA((3,))],
        nbytes=12 * w_o.size,
        in_hbm=(0, 1, 2),
    )
    sums = call(
        functools.partial(project_kernel, width),
        jax.ShapeDtypeStruct((NZ * NX, width, cols), bf16),
        [ring.reshape(NZ * width, heads * value_w), w_ring] + opposite,
        scratch=[pltpu.VMEM(w_t.shape, bf16), pltpu.SemaphoreType.DMA((2,))],
        flops=2 * NX * NZ * width * w_o.size,
        nbytes=2 * NX * w_o.size,
        in_hbm=(2, 3),
    )
    planes = [
        [(x * NZ + z) * n_head + y * cores + core for z in range(NZ) for y in range(NX)]
        for x in range(NX)
        for core in range(cores)
    ]
    sums = lax.all_to_all(
        sums,
        ("row", "head"),
        split_axis=0,
        concat_axis=0,
        axis_index_groups=planes,
        tiled=True,
    )
    half = jax.ShapeDtypeStruct((NZ // cores, width, cols), f32)
    keep, give = call(sum_kernel, (half, half), [sums])
    taken = lax.ppermute(give, "head", [(h, h ^ 1) for h in range(n_head)])
    return call(
        final_kernel,
        jax.ShapeDtypeStruct((steps, rows_dev, NZ // cores * cols), bf16),
        [keep, taken],
    )


def solution(mesh):
    placed = (
        P(None, "row", "head", None),
        P(None, "row", "head"),
        P(None, "row", None),
        P(None, "row", None),
        P("row", None, None),
        P("row", None),
        P("row"),
        P("row"),
        P("row", None),
        P("row"),
        P("head", None, None),
        P("head", None, None),
        P("head", "row"),
    )
    return jax.shard_map(
        on_device, mesh=mesh, in_specs=placed, out_specs=P(None, "row", "head"), check_vma=False
    )
```

```python
import functools

import jax
import jax.numpy as jnp
from jax import lax
from jax.experimental import pallas as pl
from jax.experimental.pallas import tpu as pltpu
from jax.sharding import PartitionSpec as P

NX = 4
NZ = 8
TAIL = 128
INFO = 16
NEG = -1e30
LOG2E = 1.4426950408889634
LN2 = 0.6931471805599453

VMEM = pl.BlockSpec(memory_space=pltpu.VMEM)
SMEM = pl.BlockSpec(memory_space=pltpu.SMEM)
HBM = pl.BlockSpec(memory_space=pltpu.HBM)


def call(
    body, out_shape, ins, scratch=(), flops=0, nbytes=0, mem=24, out_spec=VMEM, in_hbm=()
):
    return pl.pallas_call(
        body,
        out_shape=out_shape,
        in_specs=[
            HBM if i in in_hbm else SMEM if a.dtype == jnp.int32 and a.ndim == 1 else VMEM
            for i, a in enumerate(ins)
        ],
        out_specs=out_spec
        if isinstance(out_spec, tuple)
        else jax.tree.map(lambda _: out_spec, out_shape),
        scratch_shapes=list(scratch),
        compiler_params=pltpu.CompilerParams(vmem_limit_bytes=mem * 2**20),
        cost_estimate=pl.CostEstimate(flops=flops, bytes_accessed=nbytes, transcendentals=0),
    )(*ins)


def dot(a, b):
    return lax.dot_general(a, b, (((1,), (0,)), ((), ())), preferred_element_type=jnp.float32)


def dot_t(a, b):
    return lax.dot_general(a, b, (((1,), (1,)), ((), ())), preferred_element_type=jnp.float32)


def iota(shape, dim):
    return lax.broadcasted_iota(jnp.int32, shape, dim)


def ones_where(mask):
    return jnp.where(mask, 1.0, 0.0).astype(jnp.bfloat16)


def pack_kernel(
    rows_dev,
    pages_row,
    per_pair,
    rows_hbm,
    slots_hbm,
    lat_hbm,
    rope_hbm,
    out_hbm,
    rows_ref,
    slots_ref,
    lat_ref,
    lat_buf,
    rope_buf,
    buf_ref,
    in_sem,
    out_sem,
):
    pages, both, lat_w = lat_buf.shape
    piece = both // 2
    count, block, _ = buf_ref.shape
    chunks = out_sem.shape[0]
    cuts = lat_w // TAIL
    rope_rows = rope_buf.shape[1] // TAIL
    lat_rows = per_pair * cuts * piece
    head = lax.axis_index("head")
    lists = [
        pltpu.make_async_copy(rows_hbm, rows_ref, in_sem.at[0]),
        pltpu.make_async_copy(slots_hbm, slots_ref, in_sem.at[1]),
    ]
    for copy in lists:
        copy.start()
    lane0 = pl.multiple_of(head * rope_buf.shape[1], rope_buf.shape[1])
    rope_copy = pltpu.make_async_copy(
        rope_hbm.at[:, pl.ds(lane0, rope_buf.shape[1])], rope_buf, in_sem.at[2]
    )
    rope_copy.start()
    first = pl.multiple_of(head // 2 * both, both)
    cut = pages // chunks
    lat_copies = []
    for i in range(chunks):
        here = pl.ds(i * cut, cut)
        copy = pltpu.make_async_copy(
            lat_hbm.at[here, pl.ds(first, both), :], lat_buf.at[here], in_sem.at[3 + i]
        )
        copy.start()
        lat_copies.append(copy)
    for copy in lists:
        copy.wait()

    dest = rows_ref[...] // rows_dev
    label = (rows_ref[...] % rows_dev * pages_row + slots_ref[...] + 1).astype(jnp.float32)
    owned = jnp.where(iota((count, pages), 0) == dest, 1.0, 0.0)
    before = ones_where(iota((pages, pages), 0) < iota((pages, pages), 1))
    rank = jnp.sum(owned * dot(owned.astype(jnp.bfloat16), before), axis=0, keepdims=True)
    rank = rank.astype(jnp.int32)
    at_slot = (dest * per_pair + rank).astype(jnp.float32).astype(jnp.bfloat16)
    spread = ones_where(iota((pages, pages * piece), 0) == iota((pages, pages * piece), 1) // piece)
    at_slot = dot(jnp.broadcast_to(at_slot, (8, pages)), spread)[:1].astype(jnp.int32)
    place = at_slot * piece + iota((1, pages * piece), 1) % piece

    label_lane = iota((TAIL, pages), 0)
    named = ones_where((label_lane // piece == rank) & (label_lane < per_pair * piece))
    labels = dot_t((owned * label).astype(jnp.bfloat16), named).astype(jnp.bfloat16)
    rest = block - lat_rows
    row = iota((count * rest, 1), 0)
    tail = dot(
        ones_where(row == iota((1, count), 1) * rest + per_pair * rope_rows), labels
    )
    rope_copy.wait()
    for j in range(rope_rows):
        pick = ones_where(row == dest * rest + rank * rope_rows + j)
        tail = tail + dot(pick, rope_buf[:, j * TAIL : (j + 1) * TAIL])
    buf_ref[:, lat_rows:, :] = tail.reshape(count, rest, TAIL).astype(jnp.bfloat16)

    for i, copy in enumerate(lat_copies):
        copy.wait()
        lat = lat_buf[i * cut : (i + 1) * cut].astype(jnp.float32).reshape(cut, 2, piece, lat_w)
        lat = jnp.where(head % 2 == 1, lat[:, 1], lat[:, 0]).reshape(cut * piece, lat_w)
        lat_ref[i * cut * piece : (i + 1) * cut * piece, :] = lat.astype(jnp.bfloat16)
    lat = lat_ref[...]
    step = count // chunks
    copies = []
    for i in range(chunks):
        rows = step * per_pair * piece
        value = dot(ones_where(iota((rows, 1), 0) + i * rows == place), lat)
        value = [
            value[:, c * TAIL : (c + 1) * TAIL].reshape(step * per_pair, 1, piece, TAIL)
            for c in range(cuts)
        ]
        value = jnp.concatenate(value, axis=1).reshape(step, lat_rows, TAIL)
        here = pl.ds(i * step, step)
        buf_ref[here, :lat_rows, :] = value.astype(jnp.bfloat16)
        copy = pltpu.make_async_copy(buf_ref.at[here], out_hbm.at[here], out_sem.at[i])
        copy.start()
        copies.append(copy)
    for copy in copies:
        copy.wait()


def split3(x):
    hi = x.astype(jnp.bfloat16)
    rest = x - hi.astype(jnp.float32)
    mid = rest.astype(jnp.bfloat16)
    low = (rest - mid.astype(jnp.float32)).astype(jnp.bfloat16)
    return hi.astype(jnp.float32), mid.astype(jnp.float32), low.astype(jnp.float32)


def query_kernel(
    scale, rows, qn_ref, qtail_ref, w_ref, fresh_ref, fresh_t_ref, q_ref, swap_ref, part_ref, lse_ref, acc_ref
):
    heads, width, _ = qn_ref.shape
    lat_w = w_ref.shape[2]
    steps = width // rows
    for head in range(heads):
        absorbed = dot(qn_ref[head], w_ref[head])
        for row in range(rows):
            at = (row * heads + head) * steps
            acc_ref[at : at + steps, :] = absorbed[row * steps : (row + 1) * steps]
    half = rows * heads * steps // 2
    absorbed = acc_ref[...].T
    tail = qtail_ref[...].astype(jnp.float32).T
    q_ref[:lat_w, :] = absorbed.astype(jnp.bfloat16)
    q_ref[lat_w:, :] = tail.astype(jnp.bfloat16)
    swap_ref[:lat_w, :] = pltpu.roll(absorbed, half, 1).astype(jnp.bfloat16)
    swap_ref[lat_w:, :] = pltpu.roll(tail, half, 1).astype(jnp.bfloat16)
    scores = dot(fresh_ref[...], q_ref[...]) * scale
    shape = scores.shape
    token = iota(shape, 0)
    query = iota(shape, 1)
    allowed = (query // (heads * steps) == token % rows) & (token // rows <= query % steps)
    scores = jnp.where(allowed, scores, NEG)
    high = jnp.max(scores, axis=0, keepdims=True)
    weights = jnp.exp(scores - high)
    total = jnp.sum(weights, axis=0, keepdims=True)
    part_ref[...] = dot(fresh_t_ref[...], weights.astype(jnp.bfloat16)) * (1.0 / total)
    lse_ref[...] = jnp.broadcast_to(high + jnp.log(total), lse_ref.shape)


def gather_kernel(
    piece,
    per_pair,
    rope_w,
    pages_row,
    block_hbm,
    bias_ref,
    key_hbm,
    block_ref,
    lat_ref,
    tail_ref,
    key_ref,
    in_sem,
    out_sem,
):
    rows, per_row, key_w = key_ref.shape
    count, block, _ = block_ref.shape
    cuts = (key_w - TAIL) // TAIL
    lat_w = cuts * TAIL
    pair_tokens = per_pair * piece
    lat_rows = pair_tokens * cuts
    rest = block - lat_rows
    rope_rows = piece * rope_w // TAIL
    half = per_row // 2

    chunks = in_sem.shape[0]
    step = count // chunks
    copies = []
    for i in range(chunks):
        here = pl.ds(i * step, step)
        copy = pltpu.make_async_copy(block_hbm.at[here], block_ref.at[here], in_sem.at[i])
        copy.start()
        copies.append(copy)

    def spread_over(columns, group, lane):
        own = iota((count, columns), 0) == iota((1, columns), 1) // group
        return ones_where(iota((TAIL, columns), 0) == lane), jnp.where(own, 1.0, 0.0)

    lat_columns = count * pair_tokens
    lat_inner = iota((1, lat_columns), 1) % pair_tokens
    lat_spread = spread_over(lat_columns, pair_tokens, lat_inner)
    rope_columns = count * rest
    rope_inner = iota((1, rope_columns), 1) % rest
    lane = jnp.where(rope_inner < per_pair * rope_rows, rope_inner // rope_rows * piece, TAIL)
    rope_spread = spread_over(rope_columns, rest, lane)

    labels = []
    for i, copy in enumerate(copies):
        copy.wait()
        here = slice(i * step, (i + 1) * step)
        tail = block_ref[here, lat_rows:, :].astype(jnp.float32)
        marked = iota(tail.shape, 1) == per_pair * rope_rows
        labels.append(jnp.sum(jnp.where(marked, tail, 0.0), axis=1))
        tail_ref[i * step * rest : (i + 1) * step * rest, :] = tail.reshape(
            step * rest, TAIL
        ).astype(jnp.bfloat16)
        lat = block_ref[here, :lat_rows, :].astype(jnp.float32)
        lat = lat.reshape(step * per_pair, cuts, piece, TAIL)
        for c in range(cuts):
            lat_ref[i * step * pair_tokens : (i + 1) * step * pair_tokens, pl.ds(c * TAIL, TAIL)] = (
                lat[:, c].reshape(step * pair_tokens, TAIL).astype(jnp.bfloat16)
            )
    labels = jnp.concatenate(labels, axis=0).astype(jnp.bfloat16)

    def slot_of(spread, own):
        wide = dot(labels, spread) * own
        return jnp.sum(wide, axis=0, keepdims=True).astype(jnp.int32) - 1

    slot = slot_of(*lat_spread)
    token = lat_inner % piece
    row = (slot >= pages_row).astype(jnp.int32)
    target = row * (per_row - pages_row * (piece // 2)) + token % 2 * half
    target = target + slot * (piece // 2) + token // 2
    target = jnp.where(slot >= 0, target, -1)
    slot = slot_of(*rope_spread)
    rope_target = jnp.where(slot >= 0, slot * rope_rows + rope_inner % rope_rows, -1)
    copies = []
    for b in range(rows):
        pick = ones_where(iota((half, 1), 0) + b * half == rope_target)
        rope_b = dot(pick, tail_ref[...])
        rope_b = jnp.concatenate([rope_b, pltpu.roll(rope_b, TAIL - rope_w, 1)], axis=0)
        lane = iota(rope_b.shape, 1)
        bias = bias_ref[b * per_row : (b + 1) * per_row]
        rope_b = jnp.where(lane < rope_w, rope_b, jnp.where(lane == rope_w, bias, 0.0))
        key_ref[b, :, lat_w:] = rope_b.astype(jnp.bfloat16)
        pick = ones_where(iota((per_row, 1), 0) + b * per_row == target)
        key_ref[b, :, :lat_w] = dot(pick, lat_ref[...]).astype(jnp.bfloat16)
        copy = pltpu.make_async_copy(key_ref.at[b], key_hbm.at[b], out_sem.at[b])
        copy.start()
        copies.append(copy)
    for copy in copies:
        copy.wait()


def attend(scale, key, query, lat_w):
    scores = dot(key, query)
    high = jnp.max(scores, axis=0, keepdims=True)
    weights = jnp.exp2((scores - high) * (scale * LOG2E))
    total = jnp.sum(weights, axis=0, keepdims=True)
    return high, total, dot(key[:, :lat_w].T, weights.astype(jnp.bfloat16))


def ask(q_refs, b):
    left = iota(q_refs[0].shape, 1) < q_refs[0].shape[1] // 2
    tiles = []
    for k in range(0, len(q_refs), 2):
        one, two = q_refs[k][...].astype(jnp.float32), q_refs[k + 1][...].astype(jnp.float32)
        first, second = (one, two) if b == 0 else (two, one)
        tiles.append(jnp.where(left, first, second).astype(jnp.bfloat16))
    return jnp.concatenate(tiles, axis=1)


def own_kernel(scale, key_ref, *refs):
    q_refs, (part_ref, stat_ref) = refs[:-2], refs[-2:]
    for b in range(key_ref.shape[0]):
        high, total, part = attend(scale, key_ref[b], ask(q_refs, b), part_ref.shape[1])
        part_ref[b] = part
        stat_ref[b] = jnp.where(iota(stat_ref.shape[1:], 0) == 0, high, total)


def both_kernel(scale, key_ref, own_ref, stat_ref, *refs):
    count = len(refs) // 2
    q_refs, out_refs = refs[:count], refs[count:]
    lat_w = own_ref.shape[1]
    queries = q_refs[0].shape[1]
    parts = []
    for b in range(key_ref.shape[0]):
        high, total, part = attend(scale, key_ref[b], ask(q_refs, b), lat_w)
        high_own, total_own = stat_ref[b, 0:1], stat_ref[b, 1:2]
        top = jnp.maximum(high, high_own)
        keep = jnp.exp2((high - top) * (scale * LOG2E))
        keep_own = jnp.exp2((high_own - top) * (scale * LOG2E))
        total = total * keep + total_own * keep_own
        inverse = 1.0 / total
        part = part * (keep * inverse) + own_ref[b] * (keep_own * inverse)
        hi, mid, low = split3(top * scale + jnp.log(total))
        mark = iota((INFO, part.shape[1]), 0)
        info = jnp.where(mark == 0, hi, jnp.where(mark == 1, mid, jnp.where(mark == 2, low, 0.0)))
        parts.append(jnp.concatenate([part, info], axis=0))
    left = iota((lat_w + INFO, queries), 1) < queries // 2
    for k in range(0, count, 2):
        lanes = slice(k * queries // 2, (k + 2) * queries // 2)
        one, two = parts[0][:, lanes], parts[1][:, lanes]
        out_refs[k][...] = jnp.where(left, one, two).astype(jnp.bfloat16)
        out_refs[k + 1][...] = jnp.where(left, two, one).astype(jnp.bfloat16)


def merge_kernel(rows_dev, fresh_ref, fresh_lse_ref, w_ref, *refs):
    part_refs, out_ref, lat_ref = refs[:-2], refs[-2], refs[-1]
    heads, lat_w, value_w = w_ref.shape
    width = out_ref.shape[1]
    steps = width // rows_dev
    half = fresh_ref.shape[1] // 2
    lses = [fresh_lse_ref[...]]
    for k, part_ref in enumerate(part_refs):
        info = jnp.sum(part_ref[lat_w:, :].astype(jnp.float32), axis=0, keepdims=True)
        info = jnp.broadcast_to(info, lses[0].shape)
        lses.append(pltpu.roll(info, half, 1) if k % 2 else info)
    high = functools.reduce(jnp.maximum, lses)
    shares = [jnp.exp(lse - high) for lse in lses]
    inverse = 1.0 / functools.reduce(jnp.add, shares)
    total = fresh_ref[...] * (shares[0] * inverse)[:1]
    swapped = 0.0
    for k, part_ref in enumerate(part_refs):
        share = shares[k + 1] * inverse
        part = part_ref[:lat_w, :].astype(jnp.float32)
        if k % 2:
            swapped = swapped + part * pltpu.roll(share, half, 1)[:1]
        else:
            total = total + part * share[:1]
    total = total + pltpu.roll(swapped, half, 1)
    shape = (heads * width, heads * width)
    to, at = iota(shape, 0), iota(shape, 1)
    wanted = (to % rows_dev * heads + to // width) * steps + to % width // rows_dev
    lat_ref[...] = dot_t(ones_where(at == wanted), total.astype(jnp.bfloat16))
    for head in range(heads):
        rows = lat_ref[head * width : (head + 1) * width, :].astype(jnp.bfloat16)
        value = dot(rows, w_ref[head]).astype(jnp.bfloat16)
        for copy in range(out_ref.shape[0]):
            out_ref[copy, :, head * value_w : (head + 1) * value_w] = value


def stage_kernel(own_hbm, near_hbm, out_ref, sem_ref):
    copies = [
        pltpu.make_async_copy(own_hbm, out_ref.at[0], sem_ref.at[0]),
        pltpu.make_async_copy(near_hbm, out_ref.at[1], sem_ref.at[1]),
    ]
    for copy in copies:
        copy.start()
    for copy in copies:
        copy.wait()


def project_kernel(width, x_ref, w_ref, far_hbm, opposite_hbm, out_ref, late_ref, sem_ref):
    copies = [
        pltpu.make_async_copy(far_hbm, late_ref.at[0], sem_ref.at[0]),
        pltpu.make_async_copy(opposite_hbm, late_ref.at[1], sem_ref.at[1]),
    ]
    for copy in copies:
        copy.start()
    here = lax.axis_index("row") // NZ

    def put(k, block):
        owner = (here + k) % NX
        for z in range(NZ):
            rows = block[z * width : (z + 1) * width]
            out_ref[z * NX + owner] = rows.astype(out_ref.dtype)

    put(0, dot_t(x_ref[...], w_ref[0]))
    put(NX - 1, dot_t(x_ref[...], w_ref[1]))
    for i, copy in enumerate(copies):
        copy.wait()
        put(1 + i, dot_t(x_ref[...], late_ref[i]))


def sum_kernel(in_ref, keep_ref, send_ref):
    core = lax.axis_index("head") % 2
    per_core = keep_ref.shape[0]
    for i in range(per_core):
        for ref, half in ((keep_ref, core), (send_ref, 1 - core)):
            first = (half * per_core + i) * NX
            parts = [in_ref[first + y].astype(jnp.float32) for y in range(NX)]
            ref[i] = functools.reduce(jnp.add, parts)


def final_kernel(keep_ref, got_ref, out_ref):
    value = [keep_ref[i] + got_ref[i] for i in range(keep_ref.shape[0])]
    value = jnp.concatenate(value, axis=1)
    rows = out_ref.shape[1]
    for step in range(out_ref.shape[0]):
        out_ref[step] = value[step * rows : (step + 1) * rows].astype(out_ref.dtype)


def shift_y(x, n_head, k):
    cores = n_head // NX
    if k % NX == 0:
        return x
    return lax.ppermute(x, "head", [(h, (h + k * cores) % n_head) for h in range(n_head)])


def shift_x(x, k):
    return lax.ppermute(
        x,
        "row",
        [(a * NZ + b, (a + k) % NX * NZ + b) for a in range(NX) for b in range(NZ)],
    )


def on_device(
    q_nope,
    q_rope,
    new_latent,
    new_rope,
    latent_pages,
    rope_pages,
    dest_rows,
    dest_slots,
    page_table,
    lengths,
    w_uk,
    w_uv,
    w_o,
):
    bf16, f32 = jnp.bfloat16, jnp.float32
    n_row = lax.axis_size("row")
    n_head = lax.axis_size("head")
    row, head = lax.axis_index("row"), lax.axis_index("head")
    rows_dev, pages_row = page_table.shape
    pages, page_len, lat_w = latent_pages.shape
    rope_w = new_rope.shape[-1]
    steps, _, heads, nope_w = q_nope.shape
    value_w = w_uv.shape[-1]
    piece = page_len // n_head
    per_pair = 2 * (pages // n_row) + min(pages % n_row, 1)
    scale = 1.0 / (nope_w + rope_w) ** 0.5
    width = steps * rows_dev
    queries = heads * width
    tokens = pages * piece
    slots = n_row * per_pair * piece

    lat_rows = per_pair * piece * lat_w // TAIL
    rope_rows = per_pair * piece * rope_w // TAIL
    block = lat_rows + (rope_rows + 8) // 8 * 8
    send = call(
        functools.partial(pack_kernel, rows_dev, pages_row, per_pair),
        jax.ShapeDtypeStruct((n_row, block, TAIL), bf16),
        [dest_rows[None, :], dest_slots[None, :], latent_pages, rope_pages],
        scratch=[
            pltpu.VMEM((1, pages), jnp.int32),
            pltpu.VMEM((1, pages), jnp.int32),
            pltpu.VMEM((tokens, lat_w), bf16),
            pltpu.VMEM((pages, 2 * piece, lat_w), bf16),
            pltpu.VMEM((pages, piece * rope_w), bf16),
            pltpu.VMEM((n_row, block, TAIL), bf16),
            pltpu.SemaphoreType.DMA((7,)),
            pltpu.SemaphoreType.DMA((4,)),
        ],
        flops=2 * slots * tokens * lat_w,
        nbytes=2 * (slots + 2 * tokens) * lat_w,
        mem=60,
        out_spec=HBM,
        in_hbm=(0, 1, 2, 3),
    )
    got = lax.all_to_all(send, "row", split_axis=0, concat_axis=0, tiled=True)

    qn = jnp.transpose(q_nope, (2, 1, 0, 3)).reshape(heads, width, nope_w)
    qr = q_rope.reshape(steps, rows_dev, heads, rope_w)
    qr = jnp.transpose(qr, (1, 2, 0, 3)).reshape(queries, rope_w)
    one_lane = jnp.arange(TAIL - rope_w, dtype=jnp.int32)[None, :] == 0
    q_tail = jnp.concatenate(
        [qr, jnp.broadcast_to(one_lane, (queries, TAIL - rope_w)).astype(bf16)], axis=1
    )
    fresh = jnp.concatenate(
        [
            new_latent.reshape(width, lat_w),
            new_rope.reshape(width, rope_w),
            jnp.zeros((width, TAIL - rope_w), bf16),
        ],
        axis=1,
    )
    fresh = jnp.concatenate([fresh, jnp.zeros((-width % 16, lat_w + TAIL), bf16)], axis=0)
    query, swapped, fresh_part, fresh_lse = call(
        functools.partial(query_kernel, scale, rows_dev),
        (
            jax.ShapeDtypeStruct((lat_w + TAIL, queries), bf16),
            jax.ShapeDtypeStruct((lat_w + TAIL, queries), bf16),
            jax.ShapeDtypeStruct((lat_w, queries), f32),
            jax.ShapeDtypeStruct((8, queries), f32),
        ),
        [qn, q_tail, w_uk, fresh, fresh[:, :lat_w].T],
        scratch=[pltpu.VMEM((queries, lat_w), f32)],
        flops=2 * queries * nope_w * lat_w,
        nbytes=2 * heads * nope_w * lat_w,
    )
    all_queries = [shift_y((query, swapped)[k % 2], n_head, k) for k in range(NX)]

    w_t = w_o.T
    w_near, w_far = shift_x(w_t, 1), shift_x(w_t, -1)

    slot_ids = jnp.arange(pages_row, dtype=jnp.int32)
    holds = (page_table[:, :, None] == slot_ids[None, None, :]).astype(jnp.int32)
    logical = jnp.sum(holds * slot_ids[None, :, None], axis=1)
    limit = lengths[:, None] - logical * page_len - head * piece
    within = jnp.arange(piece, dtype=jnp.int32).reshape(piece // 2, 2).T
    usable = within[None, :, None, :] < limit[:, None, :, None]
    bias = jnp.where(usable, 0.0, NEG).astype(f32).reshape(rows_dev * pages_row * piece, 1)

    got, w_near, all_queries = lax.optimization_barrier((got, w_near, all_queries))
    key = call(
        functools.partial(gather_kernel, piece, per_pair, rope_w, pages_row),
        jax.ShapeDtypeStruct((rows_dev, pages_row * piece, lat_w + TAIL), bf16),
        [got, bias],
        scratch=[
            pltpu.VMEM(got.shape, bf16),
            pltpu.VMEM((slots, lat_w), bf16),
            pltpu.VMEM((n_row * (block - lat_rows), TAIL), bf16),
            pltpu.VMEM((rows_dev, pages_row * piece, lat_w + TAIL), bf16),
            pltpu.SemaphoreType.DMA((4,)),
            pltpu.SemaphoreType.DMA((rows_dev,)),
        ],
        flops=2 * slots * tokens * lat_w,
        nbytes=2 * slots * lat_w,
        out_spec=HBM,
        in_hbm=(0,),
    )
    other = lax.ppermute(key, "head", [(h, h ^ 1) for h in range(n_head)])
    asked = NX * queries // rows_dev
    own_part, own_stat = call(
        functools.partial(own_kernel, scale),
        (
            jax.ShapeDtypeStruct((rows_dev, lat_w, asked), f32),
            jax.ShapeDtypeStruct((rows_dev, 8, asked), f32),
        ),
        [key] + all_queries,
        flops=2 * tokens * asked * (2 * lat_w + TAIL),
        nbytes=2 * tokens * lat_w,
    )
    w_opposite = shift_x(w_near, 1)
    parts = call(
        functools.partial(both_kernel, scale),
        tuple(jax.ShapeDtypeStruct((lat_w + INFO, queries), bf16) for _ in range(NX)),
        [other, own_part, own_stat] + all_queries,
        flops=2 * tokens * asked * (2 * lat_w + TAIL),
        nbytes=2 * tokens * lat_w,
    )
    parts = [shift_y(part, n_head, -k) for k, part in enumerate(parts)]
    head_out = call(
        functools.partial(merge_kernel, rows_dev),
        jax.ShapeDtypeStruct((NZ, width, heads * value_w), bf16),
        [fresh_part, fresh_lse, w_uv] + parts,
        scratch=[pltpu.VMEM((queries, lat_w), f32)],
        flops=2 * queries * lat_w * value_w,
        nbytes=2 * heads * lat_w * value_w,
    )

    rings = [[a * NZ + b for b in range(NZ)] for a in range(NX)]
    ring = lax.all_to_all(
        head_out, "row", split_axis=0, concat_axis=0, axis_index_groups=rings, tiled=True
    )
    cols = w_o.shape[1]
    cores = n_head // NX
    w_ring = call(
        stage_kernel,
        jax.ShapeDtypeStruct((2,) + w_t.shape, bf16),
        [w_t, w_near],
        scratch=[pltpu.SemaphoreType.DMA((2,))],
        nbytes=8 * w_o.size,
        in_hbm=(0, 1),
    )
    sums = call(
        functools.partial(project_kernel, width),
        jax.ShapeDtypeStruct((NZ * NX, width, cols), bf16),
        [ring.reshape(NZ * width, heads * value_w), w_ring, w_far, w_opposite],
        scratch=[pltpu.VMEM((2,) + w_t.shape, bf16), pltpu.SemaphoreType.DMA((2,))],
        flops=2 * NX * NZ * width * w_o.size,
        nbytes=2 * NX * w_o.size,
        in_hbm=(2, 3),
    )
    planes = [
        [(x * NZ + z) * n_head + y * cores + core for z in range(NZ) for y in range(NX)]
        for x in range(NX)
        for core in range(cores)
    ]
    sums = lax.all_to_all(
        sums,
        ("row", "head"),
        split_axis=0,
        concat_axis=0,
        axis_index_groups=planes,
        tiled=True,
    )
    half = jax.ShapeDtypeStruct((NZ // cores, width, cols), f32)
    keep, give = call(sum_kernel, (half, half), [sums])
    taken = lax.ppermute(give, "head", [(h, h ^ 1) for h in range(n_head)])
    return call(
        final_kernel,
        jax.ShapeDtypeStruct((steps, rows_dev, NZ // cores * cols), bf16),
        [keep, taken],
    )


def solution(mesh):
    placed = (
        P(None, "row", "head", None),
        P(None, "row", "head"),
        P(None, "row", None),
        P(None, "row", None),
        P("row", None, None),
        P("row", None),
        P("row"),
        P("row"),
        P("row", None),
        P("row"),
        P("head", None, None),
        P("head", None, None),
        P("head", "row"),
    )
    return jax.shard_map(
        on_device, mesh=mesh, in_specs=placed, out_specs=P(None, "row", "head"), check_vma=False
    )
```

```python
import functools

import jax
import jax.numpy as jnp
from jax import lax
from jax.experimental import pallas as pl
from jax.experimental.pallas import tpu as pltpu
from jax.sharding import PartitionSpec as P

NX = 4
NZ = 8
TAIL = 128
INFO = 16
NEG = -1e30
LOG2E = 1.4426950408889634
LN2 = 0.6931471805599453

VMEM = pl.BlockSpec(memory_space=pltpu.VMEM)
SMEM = pl.BlockSpec(memory_space=pltpu.SMEM)
HBM = pl.BlockSpec(memory_space=pltpu.HBM)


def call(
    body, out_shape, ins, scratch=(), flops=0, nbytes=0, mem=24, out_spec=VMEM, in_hbm=()
):
    return pl.pallas_call(
        body,
        out_shape=out_shape,
        in_specs=[
            HBM if i in in_hbm else SMEM if a.dtype == jnp.int32 and a.ndim == 1 else VMEM
            for i, a in enumerate(ins)
        ],
        out_specs=out_spec
        if isinstance(out_spec, tuple)
        else jax.tree.map(lambda _: out_spec, out_shape),
        scratch_shapes=list(scratch),
        compiler_params=pltpu.CompilerParams(vmem_limit_bytes=mem * 2**20),
        cost_estimate=pl.CostEstimate(flops=flops, bytes_accessed=nbytes, transcendentals=0),
    )(*ins)


def dot(a, b):
    return lax.dot_general(a, b, (((1,), (0,)), ((), ())), preferred_element_type=jnp.float32)


def dot_t(a, b):
    return lax.dot_general(a, b, (((1,), (1,)), ((), ())), preferred_element_type=jnp.float32)


def iota(shape, dim):
    return lax.broadcasted_iota(jnp.int32, shape, dim)


def ones_where(mask):
    return jnp.where(mask, 1.0, 0.0).astype(jnp.bfloat16)


def pack_kernel(
    rows_dev,
    pages_row,
    per_pair,
    rows_hbm,
    slots_hbm,
    lat_hbm,
    rope_hbm,
    out_hbm,
    rows_ref,
    slots_ref,
    lat_ref,
    lat_buf,
    rope_buf,
    buf_ref,
    in_sem,
    out_sem,
):
    pages, both, lat_w = lat_buf.shape
    piece = both // 2
    count, block, _ = buf_ref.shape
    chunks = out_sem.shape[0]
    cuts = lat_w // TAIL
    rope_rows = rope_buf.shape[1] // TAIL
    lat_rows = per_pair * cuts * piece
    head = lax.axis_index("head")
    lists = [
        pltpu.make_async_copy(rows_hbm, rows_ref, in_sem.at[0]),
        pltpu.make_async_copy(slots_hbm, slots_ref, in_sem.at[1]),
    ]
    for copy in lists:
        copy.start()
    lane0 = pl.multiple_of(head * rope_buf.shape[1], rope_buf.shape[1])
    rope_copy = pltpu.make_async_copy(
        rope_hbm.at[:, pl.ds(lane0, rope_buf.shape[1])], rope_buf, in_sem.at[2]
    )
    rope_copy.start()
    first = pl.multiple_of(head // 2 * both, both)
    cut = pages // chunks
    lat_copies = []
    for i in range(chunks):
        here = pl.ds(i * cut, cut)
        copy = pltpu.make_async_copy(
            lat_hbm.at[here, pl.ds(first, both), :], lat_buf.at[here], in_sem.at[3 + i]
        )
        copy.start()
        lat_copies.append(copy)
    def unpack(i):
        lat_copies[i].wait()
        lat = lat_buf[i * cut : (i + 1) * cut].astype(jnp.float32).reshape(cut, 2, piece, lat_w)
        lat = jnp.where(head % 2 == 1, lat[:, 1], lat[:, 0]).reshape(cut * piece, lat_w)
        lat_ref[i * cut * piece : (i + 1) * cut * piece, :] = lat.astype(jnp.bfloat16)

    for copy in lists:
        copy.wait()
    for i in range(chunks // 2):
        unpack(i)

    dest = rows_ref[...] // rows_dev
    label = (rows_ref[...] % rows_dev * pages_row + slots_ref[...] + 1).astype(jnp.float32)
    owned = jnp.where(iota((count, pages), 0) == dest, 1.0, 0.0)
    before = ones_where(iota((pages, pages), 0) < iota((pages, pages), 1))
    rank = jnp.sum(owned * dot(owned.astype(jnp.bfloat16), before), axis=0, keepdims=True)
    rank = rank.astype(jnp.int32)
    at_slot = (dest * per_pair + rank).astype(jnp.float32).astype(jnp.bfloat16)
    spread = ones_where(iota((pages, pages * piece), 0) == iota((pages, pages * piece), 1) // piece)
    at_slot = dot(jnp.broadcast_to(at_slot, (8, pages)), spread)[:1].astype(jnp.int32)
    place = at_slot * piece + iota((1, pages * piece), 1) % piece

    label_lane = iota((TAIL, pages), 0)
    named = ones_where((label_lane // piece == rank) & (label_lane < per_pair * piece))
    labels = dot_t((owned * label).astype(jnp.bfloat16), named).astype(jnp.bfloat16)
    rest = block - lat_rows
    row = iota((count * rest, 1), 0)
    tail = dot(
        ones_where(row == iota((1, count), 1) * rest + per_pair * rope_rows), labels
    )
    rope_copy.wait()
    for j in range(rope_rows):
        pick = ones_where(row == dest * rest + rank * rope_rows + j)
        tail = tail + dot(pick, rope_buf[:, j * TAIL : (j + 1) * TAIL])
    tail = tail.reshape(count, rest, TAIL)

    for i in range(chunks // 2, chunks):
        unpack(i)
    lat = lat_ref[...]
    step = count // chunks
    copies = []
    for i in range(chunks):
        rows = step * per_pair * piece
        value = dot(ones_where(iota((rows, 1), 0) + i * rows == place), lat)
        value = [
            value[:, c * TAIL : (c + 1) * TAIL].reshape(step * per_pair, 1, piece, TAIL)
            for c in range(cuts)
        ]
        value = jnp.concatenate(value, axis=1).reshape(step, lat_rows, TAIL)
        here = pl.ds(i * step, step)
        value = jnp.concatenate([tail[i * step : (i + 1) * step], value], axis=1)
        buf_ref[here] = value.astype(jnp.bfloat16)
        copy = pltpu.make_async_copy(buf_ref.at[here], out_hbm.at[here], out_sem.at[i])
        copy.start()
        copies.append(copy)
    for copy in copies:
        copy.wait()


def split3(x):
    hi = x.astype(jnp.bfloat16)
    rest = x - hi.astype(jnp.float32)
    mid = rest.astype(jnp.bfloat16)
    low = (rest - mid.astype(jnp.float32)).astype(jnp.bfloat16)
    return hi.astype(jnp.float32), mid.astype(jnp.float32), low.astype(jnp.float32)


def query_kernel(
    scale, rows, qn_ref, qtail_ref, w_ref, fresh_ref, fresh_t_ref, q_ref, swap_ref, part_ref, lse_ref, acc_ref
):
    heads, width, _ = qn_ref.shape
    lat_w = w_ref.shape[2]
    steps = width // rows
    for head in range(heads):
        absorbed = dot(qn_ref[head], w_ref[head])
        for row in range(rows):
            at = (row * heads + head) * steps
            acc_ref[at : at + steps, :] = absorbed[row * steps : (row + 1) * steps]
    half = rows * heads * steps // 2
    absorbed = acc_ref[...].T
    tail = qtail_ref[...].astype(jnp.float32).T
    q_ref[:lat_w, :] = absorbed.astype(jnp.bfloat16)
    q_ref[lat_w:, :] = tail.astype(jnp.bfloat16)
    swap_ref[:lat_w, :] = pltpu.roll(absorbed, half, 1).astype(jnp.bfloat16)
    swap_ref[lat_w:, :] = pltpu.roll(tail, half, 1).astype(jnp.bfloat16)
    scores = dot(fresh_ref[...], q_ref[...]) * scale
    shape = scores.shape
    token = iota(shape, 0)
    query = iota(shape, 1)
    allowed = (query // (heads * steps) == token % rows) & (token // rows <= query % steps)
    scores = jnp.where(allowed, scores, NEG)
    high = jnp.max(scores, axis=0, keepdims=True)
    weights = jnp.exp(scores - high)
    total = jnp.sum(weights, axis=0, keepdims=True)
    part_ref[...] = dot(fresh_t_ref[...], weights.astype(jnp.bfloat16)) * (1.0 / total)
    lse_ref[...] = jnp.broadcast_to(high + jnp.log(total), lse_ref.shape)


def gather_kernel(
    piece,
    per_pair,
    rope_w,
    pages_row,
    block_hbm,
    bias_ref,
    key_hbm,
    block_ref,
    early_ref,
    lat_ref,
    key_ref,
    in_sem,
    out_sem,
):
    rows, per_row, key_w = key_ref.shape
    count, block, _ = block_ref.shape
    cuts = (key_w - TAIL) // TAIL
    lat_w = cuts * TAIL
    pair_tokens = per_pair * piece
    lat_rows = pair_tokens * cuts
    rest = block - lat_rows
    rope_rows = piece * rope_w // TAIL
    half = per_row // 2

    chunks = in_sem.shape[0] - 1
    step = count // chunks
    copies = []
    early = pltpu.make_async_copy(
        block_hbm.at[:, pl.ds(0, early_ref.shape[1]), :], early_ref, in_sem.at[chunks]
    )
    early.start()
    for i in range(chunks):
        here = pl.ds(i * step, step)
        copy = pltpu.make_async_copy(block_hbm.at[here], block_ref.at[here], in_sem.at[i])
        copy.start()
        copies.append(copy)

    def spread_over(columns, group, lane):
        own = iota((count, columns), 0) == iota((1, columns), 1) // group
        return ones_where(iota((TAIL, columns), 0) == lane), jnp.where(own, 1.0, 0.0)

    lat_columns = count * pair_tokens
    lat_inner = iota((1, lat_columns), 1) % pair_tokens
    lat_spread = spread_over(lat_columns, pair_tokens, lat_inner)
    rope_columns = count * rest
    rope_inner = iota((1, rope_columns), 1) % rest
    lane = jnp.where(rope_inner < per_pair * rope_rows, rope_inner // rope_rows * piece, TAIL)
    rope_spread = spread_over(rope_columns, rest, lane)

    early.wait()
    tail = early_ref[...].astype(jnp.float32)[:, :rest]
    marked = iota(tail.shape, 1) == per_pair * rope_rows
    labels = jnp.sum(jnp.where(marked, tail, 0.0), axis=1).astype(jnp.bfloat16)
    tail = tail.reshape(rope_columns, TAIL).astype(jnp.bfloat16)

    def slot_of(spread, own):
        wide = dot(labels, spread) * own
        return jnp.sum(wide, axis=0, keepdims=True).astype(jnp.int32) - 1

    slot = slot_of(*lat_spread)
    token = lat_inner % piece
    row = (slot >= pages_row).astype(jnp.int32)
    target = row * (per_row - pages_row * (piece // 2)) + token % 2 * half
    target = target + slot * (piece // 2) + token // 2
    target = jnp.where(slot >= 0, target, -1)
    slot = slot_of(*rope_spread)
    rope_target = jnp.where(slot >= 0, slot * rope_rows + rope_inner % rope_rows, -1)
    for b in range(rows):
        pick = ones_where(iota((half, 1), 0) + b * half == rope_target)
        rope_b = dot(pick, tail)
        rope_b = jnp.concatenate([rope_b, pltpu.roll(rope_b, TAIL - rope_w, 1)], axis=0)
        lane = iota(rope_b.shape, 1)
        bias = bias_ref[b * per_row : (b + 1) * per_row]
        rope_b = jnp.where(lane < rope_w, rope_b, jnp.where(lane == rope_w, bias, 0.0))
        key_ref[b, :, lat_w:] = rope_b.astype(jnp.bfloat16)
    for i, copy in enumerate(copies):
        copy.wait()
        lat = block_ref[i * step : (i + 1) * step].astype(jnp.float32)[:, rest:]
        lat = lat.reshape(step * per_pair, cuts, piece, TAIL)
        for c in range(cuts):
            lat_ref[i * step * pair_tokens : (i + 1) * step * pair_tokens, pl.ds(c * TAIL, TAIL)] = (
                lat[:, c].reshape(step * pair_tokens, TAIL).astype(jnp.bfloat16)
            )
    copies = []
    for b in range(rows):
        pick = ones_where(iota((per_row, 1), 0) + b * per_row == target)
        key_ref[b, :, :lat_w] = dot(pick, lat_ref[...]).astype(jnp.bfloat16)
        copy = pltpu.make_async_copy(key_ref.at[b], key_hbm.at[b], out_sem.at[b])
        copy.start()
        copies.append(copy)
    for copy in copies:
        copy.wait()


def attend(scale, key, query, lat_w):
    scores = dot(key, query)
    high = jnp.max(scores, axis=0, keepdims=True)
    weights = jnp.exp2((scores - high) * (scale * LOG2E))
    total = jnp.sum(weights, axis=0, keepdims=True)
    return high, total, dot(key[:, :lat_w].T, weights.astype(jnp.bfloat16))


def ask(q_refs, b):
    left = iota(q_refs[0].shape, 1) < q_refs[0].shape[1] // 2
    tiles = []
    for k in range(0, len(q_refs), 2):
        one, two = q_refs[k][...].astype(jnp.float32), q_refs[k + 1][...].astype(jnp.float32)
        first, second = (one, two) if b == 0 else (two, one)
        tiles.append(jnp.where(left, first, second).astype(jnp.bfloat16))
    return jnp.concatenate(tiles, axis=1)


def own_kernel(scale, key_ref, *refs):
    q_refs, (part_ref, stat_ref) = refs[:-2], refs[-2:]
    for b in range(key_ref.shape[0]):
        high, total, part = attend(scale, key_ref[b], ask(q_refs, b), part_ref.shape[1])
        part_ref[b] = part
        stat_ref[b] = jnp.where(iota(stat_ref.shape[1:], 0) == 0, high, total)


def both_kernel(scale, key_ref, own_ref, stat_ref, *refs):
    q_refs, out_ref = refs[:-1], refs[-1]
    count = len(q_refs)
    lat_w = own_ref.shape[1]
    queries = q_refs[0].shape[1]
    here = lax.axis_index("head") // 2
    parts = []
    for b in range(key_ref.shape[0]):
        high, total, part = attend(scale, key_ref[b], ask(q_refs, b), lat_w)
        high_own, total_own = stat_ref[b, 0:1], stat_ref[b, 1:2]
        top = jnp.maximum(high, high_own)
        keep = jnp.exp2((high - top) * (scale * LOG2E))
        keep_own = jnp.exp2((high_own - top) * (scale * LOG2E))
        total = total * keep + total_own * keep_own
        inverse = 1.0 / total
        part = part * (keep * inverse) + own_ref[b] * (keep_own * inverse)
        hi, mid, low = split3(top * scale + jnp.log(total))
        mark = iota((INFO, part.shape[1]), 0)
        info = jnp.where(mark == 0, hi, jnp.where(mark == 1, mid, jnp.where(mark == 2, low, 0.0)))
        parts.append(jnp.concatenate([part, info], axis=0))
    left = iota((lat_w + INFO, queries), 1) < queries // 2
    for k in range(0, count, 2):
        lanes = slice(k * queries // 2, (k + 2) * queries // 2)
        one, two = parts[0][:, lanes], parts[1][:, lanes]
        out_ref[(here - k + count) % count] = jnp.where(left, one, two).astype(jnp.bfloat16)
        out_ref[(here - k - 1 + count) % count] = jnp.where(left, two, one).astype(jnp.bfloat16)


def merge_kernel(rows_dev, fresh_ref, fresh_lse_ref, w_ref, in_ref, out_ref, lat_ref):
    here = lax.axis_index("head") // 2
    part_refs = [in_ref.at[(here + k) % NX] for k in range(NX)]
    heads, lat_w, value_w = w_ref.shape
    width = out_ref.shape[1]
    steps = width // rows_dev
    half = fresh_ref.shape[1] // 2
    lses = [fresh_lse_ref[...]]
    for k, part_ref in enumerate(part_refs):
        info = jnp.sum(part_ref[lat_w:, :].astype(jnp.float32), axis=0, keepdims=True)
        info = jnp.broadcast_to(info, lses[0].shape)
        lses.append(pltpu.roll(info, half, 1) if k % 2 else info)
    high = functools.reduce(jnp.maximum, lses)
    shares = [jnp.exp(lse - high) for lse in lses]
    inverse = 1.0 / functools.reduce(jnp.add, shares)
    total = fresh_ref[...] * (shares[0] * inverse)[:1]
    swapped = 0.0
    for k, part_ref in enumerate(part_refs):
        share = shares[k + 1] * inverse
        part = part_ref[:lat_w, :].astype(jnp.float32)
        if k % 2:
            swapped = swapped + part * pltpu.roll(share, half, 1)[:1]
        else:
            total = total + part * share[:1]
    total = total + pltpu.roll(swapped, half, 1)
    shape = (heads * width, heads * width)
    to, at = iota(shape, 0), iota(shape, 1)
    wanted = (to % rows_dev * heads + to // width) * steps + to % width // rows_dev
    lat_ref[...] = dot_t(ones_where(at == wanted), total.astype(jnp.bfloat16))
    for head in range(heads):
        rows = lat_ref[head * width : (head + 1) * width, :].astype(jnp.bfloat16)
        value = dot(rows, w_ref[head]).astype(jnp.bfloat16)
        for copy in range(out_ref.shape[0]):
            out_ref[copy, :, head * value_w : (head + 1) * value_w] = value


def stage_kernel(own_hbm, near_hbm, far_hbm, out_ref, sem_ref):
    copies = [
        pltpu.make_async_copy(ref, out_ref.at[i], sem_ref.at[i])
        for i, ref in enumerate((own_hbm, near_hbm, far_hbm))
    ]
    for copy in copies:
        copy.start()
    for copy in copies:
        copy.wait()


def project_kernel(width, x_ref, w_ref, opp_a_hbm, opp_b_hbm, out_ref, opp_ref, sem_ref):
    size = opp_a_hbm.shape[0]
    copies = [
        pltpu.make_async_copy(opp_a_hbm, opp_ref.at[pl.ds(0, size)], sem_ref.at[0]),
        pltpu.make_async_copy(opp_b_hbm, opp_ref.at[pl.ds(size, size)], sem_ref.at[1]),
    ]
    for copy in copies:
        copy.start()
    here = lax.axis_index("row") // NZ

    def put(k, block):
        owner = (here + k) % NX
        for z in range(NZ):
            rows = block[z * width : (z + 1) * width]
            out_ref[z * NX + owner] = rows.astype(out_ref.dtype)

    for i, k in enumerate((0, NX - 1, 1)):
        put(k, dot_t(x_ref[...], w_ref[i]))
    for copy in copies:
        copy.wait()
    put(2, dot_t(x_ref[...], opp_ref[...]))


def sum_kernel(in_ref, keep_ref, send_ref):
    core = lax.axis_index("head") % 2
    per_core = keep_ref.shape[0]
    for i in range(per_core):
        for ref, half in ((keep_ref, core), (send_ref, 1 - core)):
            first = (half * per_core + i) * NX
            parts = [in_ref[first + y].astype(jnp.float32) for y in range(NX)]
            ref[i] = functools.reduce(jnp.add, parts)


def final_kernel(keep_ref, got_ref, out_ref):
    value = [keep_ref[i] + got_ref[i] for i in range(keep_ref.shape[0])]
    value = jnp.concatenate(value, axis=1)
    rows = out_ref.shape[1]
    for step in range(out_ref.shape[0]):
        out_ref[step] = value[step * rows : (step + 1) * rows].astype(out_ref.dtype)


def shift_y(x, n_head, k):
    cores = n_head // NX
    if k % NX == 0:
        return x
    return lax.ppermute(x, "head", [(h, (h + k * cores) % n_head) for h in range(n_head)])


def shift_x(x, k):
    return lax.ppermute(
        x,
        "row",
        [(a * NZ + b, (a + k) % NX * NZ + b) for a in range(NX) for b in range(NZ)],
    )


def on_device(
    q_nope,
    q_rope,
    new_latent,
    new_rope,
    latent_pages,
    rope_pages,
    dest_rows,
    dest_slots,
    page_table,
    lengths,
    w_uk,
    w_uv,
    w_o,
):
    bf16, f32 = jnp.bfloat16, jnp.float32
    n_row = lax.axis_size("row")
    n_head = lax.axis_size("head")
    row, head = lax.axis_index("row"), lax.axis_index("head")
    rows_dev, pages_row = page_table.shape
    pages, page_len, lat_w = latent_pages.shape
    rope_w = new_rope.shape[-1]
    steps, _, heads, nope_w = q_nope.shape
    value_w = w_uv.shape[-1]
    piece = page_len // n_head
    per_pair = 2 * (pages // n_row) + min(pages % n_row, 1)
    scale = 1.0 / (nope_w + rope_w) ** 0.5
    width = steps * rows_dev
    queries = heads * width
    tokens = pages * piece
    slots = n_row * per_pair * piece

    lat_rows = per_pair * piece * lat_w // TAIL
    rope_rows = per_pair * piece * rope_w // TAIL
    block = lat_rows + (rope_rows + 8) // 8 * 8
    send = call(
        functools.partial(pack_kernel, rows_dev, pages_row, per_pair),
        jax.ShapeDtypeStruct((n_row, block, TAIL), bf16),
        [dest_rows[None, :], dest_slots[None, :], latent_pages, rope_pages],
        scratch=[
            pltpu.VMEM((1, pages), jnp.int32),
            pltpu.VMEM((1, pages), jnp.int32),
            pltpu.VMEM((tokens, lat_w), bf16),
            pltpu.VMEM((pages, 2 * piece, lat_w), bf16),
            pltpu.VMEM((pages, piece * rope_w), bf16),
            pltpu.VMEM((n_row, block, TAIL), bf16),
            pltpu.SemaphoreType.DMA((7,)),
            pltpu.SemaphoreType.DMA((4,)),
        ],
        flops=2 * slots * tokens * lat_w,
        nbytes=2 * (slots + 2 * tokens) * lat_w,
        mem=60,
        out_spec=HBM,
        in_hbm=(0, 1, 2, 3),
    )
    got = lax.all_to_all(send, "row", split_axis=0, concat_axis=0, tiled=True)

    qn = jnp.transpose(q_nope, (2, 1, 0, 3)).reshape(heads, width, nope_w)
    qr = q_rope.reshape(steps, rows_dev, heads, rope_w)
    qr = jnp.transpose(qr, (1, 2, 0, 3)).reshape(queries, rope_w)
    one_lane = jnp.arange(TAIL - rope_w, dtype=jnp.int32)[None, :] == 0
    q_tail = jnp.concatenate(
        [qr, jnp.broadcast_to(one_lane, (queries, TAIL - rope_w)).astype(bf16)], axis=1
    )
    fresh = jnp.concatenate(
        [
            new_latent.reshape(width, lat_w),
            new_rope.reshape(width, rope_w),
            jnp.zeros((width, TAIL - rope_w), bf16),
        ],
        axis=1,
    )
    fresh = jnp.concatenate([fresh, jnp.zeros((-width % 16, lat_w + TAIL), bf16)], axis=0)
    query, swapped, fresh_part, fresh_lse = call(
        functools.partial(query_kernel, scale, rows_dev),
        (
            jax.ShapeDtypeStruct((lat_w + TAIL, queries), bf16),
            jax.ShapeDtypeStruct((lat_w + TAIL, queries), bf16),
            jax.ShapeDtypeStruct((lat_w, queries), f32),
            jax.ShapeDtypeStruct((8, queries), f32),
        ),
        [qn, q_tail, w_uk, fresh, fresh[:, :lat_w].T],
        scratch=[pltpu.VMEM((queries, lat_w), f32)],
        flops=2 * queries * nope_w * lat_w,
        nbytes=2 * heads * nope_w * lat_w,
    )
    all_queries = [shift_y((query, swapped)[k % 2], n_head, k) for k in range(NX)]

    w_t = w_o.T
    w_near, w_far = shift_x(w_t, 1), shift_x(w_t, -1)

    slot_ids = jnp.arange(pages_row, dtype=jnp.int32)
    holds = (page_table[:, :, None] == slot_ids[None, None, :]).astype(jnp.int32)
    logical = jnp.sum(holds * slot_ids[None, :, None], axis=1)
    limit = lengths[:, None] - logical * page_len - head * piece
    within = jnp.arange(piece, dtype=jnp.int32).reshape(piece // 2, 2).T
    usable = within[None, :, None, :] < limit[:, None, :, None]
    bias = jnp.where(usable, 0.0, NEG).astype(f32).reshape(rows_dev * pages_row * piece, 1)

    got, w_near, w_far, all_queries = lax.optimization_barrier((got, w_near, w_far, all_queries))
    key = call(
        functools.partial(gather_kernel, piece, per_pair, rope_w, pages_row),
        jax.ShapeDtypeStruct((rows_dev, pages_row * piece, lat_w + TAIL), bf16),
        [got, bias],
        scratch=[
            pltpu.VMEM(got.shape, bf16),
            pltpu.VMEM((n_row, 32, TAIL), bf16),
            pltpu.VMEM((slots, lat_w), bf16),
            pltpu.VMEM((rows_dev, pages_row * piece, lat_w + TAIL), bf16),
            pltpu.SemaphoreType.DMA((5,)),
            pltpu.SemaphoreType.DMA((rows_dev,)),
        ],
        flops=2 * slots * tokens * lat_w,
        nbytes=2 * slots * lat_w,
        out_spec=HBM,
        in_hbm=(0,),
    )
    other = lax.ppermute(key, "head", [(h, h ^ 1) for h in range(n_head)])
    asked = NX * queries // rows_dev
    own_part, own_stat = call(
        functools.partial(own_kernel, scale),
        (
            jax.ShapeDtypeStruct((rows_dev, lat_w, asked), f32),
            jax.ShapeDtypeStruct((rows_dev, 8, asked), f32),
        ),
        [key] + all_queries,
        flops=2 * tokens * asked * (2 * lat_w + TAIL),
        nbytes=2 * tokens * lat_w,
    )
    size = w_t.shape[0] // 2
    opposite = [shift_x(w_near[:size], 1), shift_x(w_far[size:], -1)]
    parts = call(
        functools.partial(both_kernel, scale),
        jax.ShapeDtypeStruct((NX, lat_w + INFO, queries), bf16),
        [other, own_part, own_stat] + all_queries,
        flops=2 * tokens * asked * (2 * lat_w + TAIL),
        nbytes=2 * tokens * lat_w,
    )
    kinds = [list(range(core, n_head, 2)) for core in range(2)]
    parts = lax.all_to_all(
        parts, "head", split_axis=0, concat_axis=0, axis_index_groups=kinds, tiled=True
    )
    head_out = call(
        functools.partial(merge_kernel, rows_dev),
        jax.ShapeDtypeStruct((NZ, width, heads * value_w), bf16),
        [fresh_part, fresh_lse, w_uv, parts],
        scratch=[pltpu.VMEM((queries, lat_w), f32)],
        flops=2 * queries * lat_w * value_w,
        nbytes=2 * heads * lat_w * value_w,
    )

    rings = [[a * NZ + b for b in range(NZ)] for a in range(NX)]
    ring = lax.all_to_all(
        head_out, "row", split_axis=0, concat_axis=0, axis_index_groups=rings, tiled=True
    )
    cols = w_o.shape[1]
    cores = n_head // NX
    w_ring = call(
        stage_kernel,
        jax.ShapeDtypeStruct((3,) + w_t.shape, bf16),
        [w_t, w_near, w_far],
        scratch=[pltpu.SemaphoreType.DMA((3,))],
        nbytes=12 * w_o.size,
        in_hbm=(0, 1, 2),
    )
    sums = call(
        functools.partial(project_kernel, width),
        jax.ShapeDtypeStruct((NZ * NX, width, cols), bf16),
        [ring.reshape(NZ * width, heads * value_w), w_ring] + opposite,
        scratch=[pltpu.VMEM(w_t.shape, bf16), pltpu.SemaphoreType.DMA((2,))],
        flops=2 * NX * NZ * width * w_o.size,
        nbytes=2 * NX * w_o.size,
        in_hbm=(2, 3),
    )
    planes = [
        [(x * NZ + z) * n_head + y * cores + core for z in range(NZ) for y in range(NX)]
        for x in range(NX)
        for core in range(cores)
    ]
    sums = lax.all_to_all(
        sums,
        ("row", "head"),
        split_axis=0,
        concat_axis=0,
        axis_index_groups=planes,
        tiled=True,
    )
    half = jax.ShapeDtypeStruct((NZ // cores, width, cols), f32)
    keep, give = call(sum_kernel, (half, half), [sums])
    taken = lax.ppermute(give, "head", [(h, h ^ 1) for h in range(n_head)])
    return call(
        final_kernel,
        jax.ShapeDtypeStruct((steps, rows_dev, NZ // cores * cols), bf16),
        [keep, taken],
    )


def solution(mesh):
    placed = (
        P(None, "row", "head", None),
        P(None, "row", "head"),
        P(None, "row", None),
        P(None, "row", None),
        P("row", None, None),
        P("row", None),
        P("row"),
        P("row"),
        P("row", None),
        P("row"),
        P("head", None, None),
        P("head", None, None),
        P("head", "row"),
    )
    return jax.shard_map(
        on_device, mesh=mesh, in_specs=placed, out_specs=P(None, "row", "head"), check_vma=False
    )
```

```python
import functools

import jax
import jax.numpy as jnp
from jax import lax
from jax.experimental import pallas as pl
from jax.experimental.pallas import tpu as pltpu
from jax.sharding import PartitionSpec as P

NX = 4
NZ = 8
TAIL = 128
INFO = 16
NEG = -1e30
LOG2E = 1.4426950408889634
LN2 = 0.6931471805599453

VMEM = pl.BlockSpec(memory_space=pltpu.VMEM)
SMEM = pl.BlockSpec(memory_space=pltpu.SMEM)
HBM = pl.BlockSpec(memory_space=pltpu.HBM)


def call(
    body, out_shape, ins, scratch=(), flops=0, nbytes=0, mem=24, out_spec=VMEM, in_hbm=()
):
    return pl.pallas_call(
        body,
        out_shape=out_shape,
        in_specs=[
            HBM if i in in_hbm else SMEM if a.dtype == jnp.int32 and a.ndim == 1 else VMEM
            for i, a in enumerate(ins)
        ],
        out_specs=out_spec
        if isinstance(out_spec, tuple)
        else jax.tree.map(lambda _: out_spec, out_shape),
        scratch_shapes=list(scratch),
        compiler_params=pltpu.CompilerParams(vmem_limit_bytes=mem * 2**20),
        cost_estimate=pl.CostEstimate(flops=flops, bytes_accessed=nbytes, transcendentals=0),
    )(*ins)


def dot(a, b):
    return lax.dot_general(a, b, (((1,), (0,)), ((), ())), preferred_element_type=jnp.float32)


def dot_t(a, b):
    return lax.dot_general(a, b, (((1,), (1,)), ((), ())), preferred_element_type=jnp.float32)


def iota(shape, dim):
    return lax.broadcasted_iota(jnp.int32, shape, dim)


def ones_where(mask):
    return jnp.where(mask, 1.0, 0.0).astype(jnp.bfloat16)


def pack_kernel(
    rows_dev,
    pages_row,
    per_pair,
    rows_hbm,
    slots_hbm,
    lat_hbm,
    rope_hbm,
    out_hbm,
    rows_ref,
    slots_ref,
    lat_ref,
    lat_buf,
    rope_buf,
    buf_ref,
    in_sem,
    out_sem,
):
    pages, both, lat_w = lat_buf.shape
    piece = both // 2
    count, block, _ = buf_ref.shape
    chunks = out_sem.shape[0]
    cuts = lat_w // TAIL
    rope_rows = rope_buf.shape[1] // TAIL
    lat_rows = per_pair * cuts * piece
    head = lax.axis_index("head")
    lists = [
        pltpu.make_async_copy(rows_hbm, rows_ref, in_sem.at[0]),
        pltpu.make_async_copy(slots_hbm, slots_ref, in_sem.at[1]),
    ]
    for copy in lists:
        copy.start()
    lane0 = pl.multiple_of(head * rope_buf.shape[1], rope_buf.shape[1])
    rope_copy = pltpu.make_async_copy(
        rope_hbm.at[:, pl.ds(lane0, rope_buf.shape[1])], rope_buf, in_sem.at[2]
    )
    rope_copy.start()
    first = pl.multiple_of(head // 2 * both, both)
    cut = pages // chunks
    lat_copies = []
    for i in range(chunks):
        here = pl.ds(i * cut, cut)
        copy = pltpu.make_async_copy(
            lat_hbm.at[here, pl.ds(first, both), :], lat_buf.at[here], in_sem.at[3 + i]
        )
        copy.start()
        lat_copies.append(copy)
    for copy in lists:
        copy.wait()

    dest = rows_ref[...] // rows_dev
    label = (rows_ref[...] % rows_dev * pages_row + slots_ref[...] + 1).astype(jnp.float32)
    owned = jnp.where(iota((count, pages), 0) == dest, 1.0, 0.0)
    before = ones_where(iota((pages, pages), 0) < iota((pages, pages), 1))
    rank = jnp.sum(owned * dot(owned.astype(jnp.bfloat16), before), axis=0, keepdims=True)
    rank = rank.astype(jnp.int32)
    at_slot = (dest * per_pair + rank).astype(jnp.float32).astype(jnp.bfloat16)
    spread = ones_where(iota((pages, pages * piece), 0) == iota((pages, pages * piece), 1) // piece)
    at_slot = dot(jnp.broadcast_to(at_slot, (8, pages)), spread)[:1].astype(jnp.int32)
    place = at_slot * piece + iota((1, pages * piece), 1) % piece

    label_lane = iota((TAIL, pages), 0)
    named = ones_where((label_lane // piece == rank) & (label_lane < per_pair * piece))
    labels = dot_t((owned * label).astype(jnp.bfloat16), named).astype(jnp.bfloat16)
    rest = block - lat_rows
    row = iota((count * rest, 1), 0)
    tail = dot(
        ones_where(row == iota((1, count), 1) * rest + per_pair * rope_rows), labels
    )
    rope_copy.wait()
    for j in range(rope_rows):
        pick = ones_where(row == dest * rest + rank * rope_rows + j)
        tail = tail + dot(pick, rope_buf[:, j * TAIL : (j + 1) * TAIL])
    buf_ref[:, lat_rows:, :] = tail.reshape(count, rest, TAIL).astype(jnp.bfloat16)

    for i, copy in enumerate(lat_copies):
        copy.wait()
        lat = lat_buf[i * cut : (i + 1) * cut].astype(jnp.float32).reshape(cut, 2, piece, lat_w)
        lat = jnp.where(head % 2 == 1, lat[:, 1], lat[:, 0]).reshape(cut * piece, lat_w)
        lat_ref[i * cut * piece : (i + 1) * cut * piece, :] = lat.astype(jnp.bfloat16)
    lat = lat_ref[...]
    step = count // chunks
    copies = []
    for i in range(chunks):
        rows = step * per_pair * piece
        value = dot(ones_where(iota((rows, 1), 0) + i * rows == place), lat)
        value = [
            value[:, c * TAIL : (c + 1) * TAIL].reshape(step * per_pair, 1, piece, TAIL)
            for c in range(cuts)
        ]
        value = jnp.concatenate(value, axis=1).reshape(step, lat_rows, TAIL)
        here = pl.ds(i * step, step)
        buf_ref[here, :lat_rows, :] = value.astype(jnp.bfloat16)
        copy = pltpu.make_async_copy(buf_ref.at[here], out_hbm.at[here], out_sem.at[i])
        copy.start()
        copies.append(copy)
    for copy in copies:
        copy.wait()


def split3(x):
    hi = x.astype(jnp.bfloat16)
    rest = x - hi.astype(jnp.float32)
    mid = rest.astype(jnp.bfloat16)
    low = (rest - mid.astype(jnp.float32)).astype(jnp.bfloat16)
    return hi.astype(jnp.float32), mid.astype(jnp.float32), low.astype(jnp.float32)


def query_kernel(
    scale, rows, qn_ref, qtail_ref, w_ref, fresh_ref, fresh_t_ref, q_ref, swap_ref, part_ref, lse_ref, acc_ref
):
    heads, width, _ = qn_ref.shape
    lat_w = w_ref.shape[2]
    steps = width // rows
    for head in range(heads):
        absorbed = dot(qn_ref[head], w_ref[head])
        for row in range(rows):
            at = (row * heads + head) * steps
            acc_ref[at : at + steps, :] = absorbed[row * steps : (row + 1) * steps]
    half = rows * heads * steps // 2
    absorbed = acc_ref[...].T
    tail = qtail_ref[...].astype(jnp.float32).T
    q_ref[:lat_w, :] = absorbed.astype(jnp.bfloat16)
    q_ref[lat_w:, :] = tail.astype(jnp.bfloat16)
    swap_ref[:lat_w, :] = pltpu.roll(absorbed, half, 1).astype(jnp.bfloat16)
    swap_ref[lat_w:, :] = pltpu.roll(tail, half, 1).astype(jnp.bfloat16)
    scores = dot(fresh_ref[...], q_ref[...]) * scale
    shape = scores.shape
    token = iota(shape, 0)
    query = iota(shape, 1)
    allowed = (query // (heads * steps) == token % rows) & (token // rows <= query % steps)
    scores = jnp.where(allowed, scores, NEG)
    high = jnp.max(scores, axis=0, keepdims=True)
    weights = jnp.exp(scores - high)
    total = jnp.sum(weights, axis=0, keepdims=True)
    part_ref[...] = dot(fresh_t_ref[...], weights.astype(jnp.bfloat16)) * (1.0 / total)
    lse_ref[...] = jnp.broadcast_to(high + jnp.log(total), lse_ref.shape)


def gather_kernel(
    piece,
    per_pair,
    rope_w,
    pages_row,
    block_hbm,
    bias_ref,
    key_hbm,
    block_ref,
    lat_ref,
    tail_ref,
    key_ref,
    in_sem,
    out_sem,
):
    rows, per_row, key_w = key_ref.shape
    count, block, _ = block_ref.shape
    cuts = (key_w - TAIL) // TAIL
    lat_w = cuts * TAIL
    pair_tokens = per_pair * piece
    lat_rows = pair_tokens * cuts
    rest = block - lat_rows
    rope_rows = piece * rope_w // TAIL
    half = per_row // 2

    chunks = in_sem.shape[0]
    step = count // chunks
    copies = []
    for i in range(chunks):
        here = pl.ds(i * step, step)
        copy = pltpu.make_async_copy(block_hbm.at[here], block_ref.at[here], in_sem.at[i])
        copy.start()
        copies.append(copy)

    def spread_over(columns, group, lane):
        own = iota((count, columns), 0) == iota((1, columns), 1) // group
        return ones_where(iota((TAIL, columns), 0) == lane), jnp.where(own, 1.0, 0.0)

    lat_columns = count * pair_tokens
    lat_inner = iota((1, lat_columns), 1) % pair_tokens
    lat_spread = spread_over(lat_columns, pair_tokens, lat_inner)
    rope_columns = count * rest
    rope_inner = iota((1, rope_columns), 1) % rest
    lane = jnp.where(rope_inner < per_pair * rope_rows, rope_inner // rope_rows * piece, TAIL)
    rope_spread = spread_over(rope_columns, rest, lane)

    labels = []
    for i, copy in enumerate(copies):
        copy.wait()
        here = slice(i * step, (i + 1) * step)
        tail = block_ref[here, lat_rows:, :].astype(jnp.float32)
        marked = iota(tail.shape, 1) == per_pair * rope_rows
        labels.append(jnp.sum(jnp.where(marked, tail, 0.0), axis=1))
        tail_ref[i * step * rest : (i + 1) * step * rest, :] = tail.reshape(
            step * rest, TAIL
        ).astype(jnp.bfloat16)
        lat = block_ref[here, :lat_rows, :].astype(jnp.float32)
        lat = lat.reshape(step * per_pair, cuts, piece, TAIL)
        for c in range(cuts):
            lat_ref[i * step * pair_tokens : (i + 1) * step * pair_tokens, pl.ds(c * TAIL, TAIL)] = (
                lat[:, c].reshape(step * pair_tokens, TAIL).astype(jnp.bfloat16)
            )
    labels = jnp.concatenate(labels, axis=0).astype(jnp.bfloat16)

    def slot_of(spread, own):
        wide = dot(labels, spread) * own
        return jnp.sum(wide, axis=0, keepdims=True).astype(jnp.int32) - 1

    slot = slot_of(*lat_spread)
    token = lat_inner % piece
    row = (slot >= pages_row).astype(jnp.int32)
    target = row * (per_row - pages_row * (piece // 2)) + token % 2 * half
    target = target + slot * (piece // 2) + token // 2
    target = jnp.where(slot >= 0, target, -1)
    slot = slot_of(*rope_spread)
    rope_target = jnp.where(slot >= 0, slot * rope_rows + rope_inner % rope_rows, -1)
    copies = []
    for b in range(rows):
        pick = ones_where(iota((half, 1), 0) + b * half == rope_target)
        rope_b = dot(pick, tail_ref[...])
        rope_b = jnp.concatenate([rope_b, pltpu.roll(rope_b, TAIL - rope_w, 1)], axis=0)
        lane = iota(rope_b.shape, 1)
        bias = bias_ref[b * per_row : (b + 1) * per_row]
        rope_b = jnp.where(lane < rope_w, rope_b, jnp.where(lane == rope_w, bias, 0.0))
        key_ref[b, :, lat_w:] = rope_b.astype(jnp.bfloat16)
        pick = ones_where(iota((per_row, 1), 0) + b * per_row == target)
        key_ref[b, :, :lat_w] = dot(pick, lat_ref[...]).astype(jnp.bfloat16)
        copy = pltpu.make_async_copy(key_ref.at[b], key_hbm.at[b], out_sem.at[b])
        copy.start()
        copies.append(copy)
    for copy in copies:
        copy.wait()


def attend(scale, key, query, lat_w):
    scores = dot(key, query)
    high = jnp.max(scores, axis=0, keepdims=True)
    weights = jnp.exp2((scores - high) * (scale * LOG2E))
    total = jnp.sum(weights, axis=0, keepdims=True)
    return high, total, dot(key[:, :lat_w].T, weights.astype(jnp.bfloat16))


def ask(q_refs, b):
    left = iota(q_refs[0].shape, 1) < q_refs[0].shape[1] // 2
    tiles = []
    for k in range(0, len(q_refs), 2):
        one, two = q_refs[k][...].astype(jnp.float32), q_refs[k + 1][...].astype(jnp.float32)
        first, second = (one, two) if b == 0 else (two, one)
        tiles.append(jnp.where(left, first, second).astype(jnp.bfloat16))
    return jnp.concatenate(tiles, axis=1)


def own_kernel(scale, key_ref, *refs):
    q_refs, (part_ref, stat_ref) = refs[:-2], refs[-2:]
    for b in range(key_ref.shape[0]):
        high, total, part = attend(scale, key_ref[b], ask(q_refs, b), part_ref.shape[1])
        part_ref[b] = part
        stat_ref[b] = jnp.where(iota(stat_ref.shape[1:], 0) == 0, high, total)


def both_kernel(scale, key_ref, own_ref, stat_ref, *refs):
    count = len(refs) // 2
    q_refs, out_refs = refs[:count], refs[count:]
    lat_w = own_ref.shape[1]
    queries = q_refs[0].shape[1]
    parts = []
    for b in range(key_ref.shape[0]):
        high, total, part = attend(scale, key_ref[b], ask(q_refs, b), lat_w)
        high_own, total_own = stat_ref[b, 0:1], stat_ref[b, 1:2]
        top = jnp.maximum(high, high_own)
        keep = jnp.exp2((high - top) * (scale * LOG2E))
        keep_own = jnp.exp2((high_own - top) * (scale * LOG2E))
        total = total * keep + total_own * keep_own
        inverse = 1.0 / total
        part = part * (keep * inverse) + own_ref[b] * (keep_own * inverse)
        hi, mid, low = split3(top * scale + jnp.log(total))
        mark = iota((INFO, part.shape[1]), 0)
        info = jnp.where(mark == 0, hi, jnp.where(mark == 1, mid, jnp.where(mark == 2, low, 0.0)))
        parts.append(jnp.concatenate([part, info], axis=0))
    left = iota((lat_w + INFO, queries), 1) < queries // 2
    for k in range(0, count, 2):
        lanes = slice(k * queries // 2, (k + 2) * queries // 2)
        one, two = parts[0][:, lanes], parts[1][:, lanes]
        out_refs[k][...] = jnp.where(left, one, two).astype(jnp.bfloat16)
        out_refs[k + 1][...] = jnp.where(left, two, one).astype(jnp.bfloat16)


def merge_kernel(rows_dev, fresh_ref, fresh_lse_ref, w_ref, *refs):
    part_refs, out_ref, lat_ref = refs[:-2], refs[-2], refs[-1]
    heads, lat_w, value_w = w_ref.shape
    width = out_ref.shape[1]
    steps = width // rows_dev
    half = fresh_ref.shape[1] // 2
    lses = [fresh_lse_ref[...]]
    for k, part_ref in enumerate(part_refs):
        info = jnp.sum(part_ref[lat_w:, :].astype(jnp.float32), axis=0, keepdims=True)
        info = jnp.broadcast_to(info, lses[0].shape)
        lses.append(pltpu.roll(info, half, 1) if k % 2 else info)
    high = functools.reduce(jnp.maximum, lses)
    shares = [jnp.exp(lse - high) for lse in lses]
    inverse = 1.0 / functools.reduce(jnp.add, shares)
    total = fresh_ref[...] * (shares[0] * inverse)[:1]
    swapped = 0.0
    for k, part_ref in enumerate(part_refs):
        share = shares[k + 1] * inverse
        part = part_ref[:lat_w, :].astype(jnp.float32)
        if k % 2:
            swapped = swapped + part * pltpu.roll(share, half, 1)[:1]
        else:
            total = total + part * share[:1]
    total = total + pltpu.roll(swapped, half, 1)
    shape = (heads * width, heads * width)
    to, at = iota(shape, 0), iota(shape, 1)
    wanted = (to % rows_dev * heads + to // width) * steps + to % width // rows_dev
    lat_ref[...] = dot_t(ones_where(at == wanted), total.astype(jnp.bfloat16))
    for head in range(heads):
        rows = lat_ref[head * width : (head + 1) * width, :].astype(jnp.bfloat16)
        value = dot(rows, w_ref[head]).astype(jnp.bfloat16)
        for copy in range(out_ref.shape[0]):
            out_ref[copy, :, head * value_w : (head + 1) * value_w] = value


def stage_kernel(own_hbm, near_hbm, far_hbm, out_ref, sem_ref):
    copies = [
        pltpu.make_async_copy(ref, out_ref.at[i], sem_ref.at[i])
        for i, ref in enumerate((own_hbm, near_hbm, far_hbm))
    ]
    for copy in copies:
        copy.start()
    for copy in copies:
        copy.wait()


def project_kernel(width, x_ref, w_ref, opposite_hbm, out_ref, opposite_ref, sem_ref):
    copy = pltpu.make_async_copy(opposite_hbm, opposite_ref, sem_ref.at[0])
    copy.start()
    here = lax.axis_index("row") // NZ

    def put(k, block):
        owner = (here + k) % NX
        for z in range(NZ):
            rows = block[z * width : (z + 1) * width]
            out_ref[z * NX + owner] = rows.astype(out_ref.dtype)

    for i, k in enumerate((0, NX - 1, 1)):
        put(k, dot_t(x_ref[...], w_ref[i]))
    copy.wait()
    put(2, dot_t(x_ref[...], opposite_ref[...]))


def sum_kernel(in_ref, keep_ref, send_ref):
    core = lax.axis_index("head") % 2
    per_core = keep_ref.shape[0]
    for i in range(per_core):
        for ref, half in ((keep_ref, core), (send_ref, 1 - core)):
            first = (half * per_core + i) * NX
            parts = [in_ref[first + y].astype(jnp.float32) for y in range(NX)]
            ref[i] = functools.reduce(jnp.add, parts)


def final_kernel(keep_ref, got_ref, out_ref):
    value = [keep_ref[i] + got_ref[i] for i in range(keep_ref.shape[0])]
    value = jnp.concatenate(value, axis=1)
    rows = out_ref.shape[1]
    for step in range(out_ref.shape[0]):
        out_ref[step] = value[step * rows : (step + 1) * rows].astype(out_ref.dtype)


def shift_y(x, n_head, k):
    cores = n_head // NX
    if k % NX == 0:
        return x
    return lax.ppermute(x, "head", [(h, (h + k * cores) % n_head) for h in range(n_head)])


def shift_x(x, k):
    return lax.ppermute(
        x,
        "row",
        [(a * NZ + b, (a + k) % NX * NZ + b) for a in range(NX) for b in range(NZ)],
    )


def on_device(
    q_nope,
    q_rope,
    new_latent,
    new_rope,
    latent_pages,
    rope_pages,
    dest_rows,
    dest_slots,
    page_table,
    lengths,
    w_uk,
    w_uv,
    w_o,
):
    bf16, f32 = jnp.bfloat16, jnp.float32
    n_row = lax.axis_size("row")
    n_head = lax.axis_size("head")
    row, head = lax.axis_index("row"), lax.axis_index("head")
    rows_dev, pages_row = page_table.shape
    pages, page_len, lat_w = latent_pages.shape
    rope_w = new_rope.shape[-1]
    steps, _, heads, nope_w = q_nope.shape
    value_w = w_uv.shape[-1]
    piece = page_len // n_head
    per_pair = 2 * (pages // n_row) + min(pages % n_row, 1)
    scale = 1.0 / (nope_w + rope_w) ** 0.5
    width = steps * rows_dev
    queries = heads * width
    tokens = pages * piece
    slots = n_row * per_pair * piece

    lat_rows = per_pair * piece * lat_w // TAIL
    rope_rows = per_pair * piece * rope_w // TAIL
    block = lat_rows + (rope_rows + 8) // 8 * 8
    send = call(
        functools.partial(pack_kernel, rows_dev, pages_row, per_pair),
        jax.ShapeDtypeStruct((n_row, block, TAIL), bf16),
        [dest_rows[None, :], dest_slots[None, :], latent_pages, rope_pages],
        scratch=[
            pltpu.VMEM((1, pages), jnp.int32),
            pltpu.VMEM((1, pages), jnp.int32),
            pltpu.VMEM((tokens, lat_w), bf16),
            pltpu.VMEM((pages, 2 * piece, lat_w), bf16),
            pltpu.VMEM((pages, piece * rope_w), bf16),
            pltpu.VMEM((n_row, block, TAIL), bf16),
            pltpu.SemaphoreType.DMA((7,)),
            pltpu.SemaphoreType.DMA((4,)),
        ],
        flops=2 * slots * tokens * lat_w,
        nbytes=2 * (slots + 2 * tokens) * lat_w,
        mem=60,
        out_spec=HBM,
        in_hbm=(0, 1, 2, 3),
    )
    got = lax.all_to_all(send, "row", split_axis=0, concat_axis=0, tiled=True)

    qn = jnp.transpose(q_nope, (2, 1, 0, 3)).reshape(heads, width, nope_w)
    qr = q_rope.reshape(steps, rows_dev, heads, rope_w)
    qr = jnp.transpose(qr, (1, 2, 0, 3)).reshape(queries, rope_w)
    one_lane = jnp.arange(TAIL - rope_w, dtype=jnp.int32)[None, :] == 0
    q_tail = jnp.concatenate(
        [qr, jnp.broadcast_to(one_lane, (queries, TAIL - rope_w)).astype(bf16)], axis=1
    )
    fresh = jnp.concatenate(
        [
            new_latent.reshape(width, lat_w),
            new_rope.reshape(width, rope_w),
            jnp.zeros((width, TAIL - rope_w), bf16),
        ],
        axis=1,
    )
    fresh = jnp.concatenate([fresh, jnp.zeros((-width % 16, lat_w + TAIL), bf16)], axis=0)
    query, swapped, fresh_part, fresh_lse = call(
        functools.partial(query_kernel, scale, rows_dev),
        (
            jax.ShapeDtypeStruct((lat_w + TAIL, queries), bf16),
            jax.ShapeDtypeStruct((lat_w + TAIL, queries), bf16),
            jax.ShapeDtypeStruct((lat_w, queries), f32),
            jax.ShapeDtypeStruct((8, queries), f32),
        ),
        [qn, q_tail, w_uk, fresh, fresh[:, :lat_w].T],
        scratch=[pltpu.VMEM((queries, lat_w), f32)],
        flops=2 * queries * nope_w * lat_w,
        nbytes=2 * heads * nope_w * lat_w,
    )
    all_queries = [shift_y((query, swapped)[k % 2], n_head, k) for k in range(NX)]

    w_t = w_o.T
    w_near, w_far, w_opposite = shift_x(w_t, 1), shift_x(w_t, -1), shift_x(w_t, 2)

    slot_ids = jnp.arange(pages_row, dtype=jnp.int32)
    holds = (page_table[:, :, None] == slot_ids[None, None, :]).astype(jnp.int32)
    logical = jnp.sum(holds * slot_ids[None, :, None], axis=1)
    limit = lengths[:, None] - logical * page_len - head * piece
    within = jnp.arange(piece, dtype=jnp.int32).reshape(piece // 2, 2).T
    usable = within[None, :, None, :] < limit[:, None, :, None]
    bias = jnp.where(usable, 0.0, NEG).astype(f32).reshape(rows_dev * pages_row * piece, 1)

    got, w_near, w_far, all_queries = lax.optimization_barrier((got, w_near, w_far, all_queries))
    key = call(
        functools.partial(gather_kernel, piece, per_pair, rope_w, pages_row),
        jax.ShapeDtypeStruct((rows_dev, pages_row * piece, lat_w + TAIL), bf16),
        [got, bias],
        scratch=[
            pltpu.VMEM(got.shape, bf16),
            pltpu.VMEM((slots, lat_w), bf16),
            pltpu.VMEM((n_row * (block - lat_rows), TAIL), bf16),
            pltpu.VMEM((rows_dev, pages_row * piece, lat_w + TAIL), bf16),
            pltpu.SemaphoreType.DMA((4,)),
            pltpu.SemaphoreType.DMA((rows_dev,)),
        ],
        flops=2 * slots * tokens * lat_w,
        nbytes=2 * slots * lat_w,
        out_spec=HBM,
        in_hbm=(0,),
    )
    other = lax.ppermute(key, "head", [(h, h ^ 1) for h in range(n_head)])
    asked = NX * queries // rows_dev
    own_part, own_stat = call(
        functools.partial(own_kernel, scale),
        (
            jax.ShapeDtypeStruct((rows_dev, lat_w, asked), f32),
            jax.ShapeDtypeStruct((rows_dev, 8, asked), f32),
        ),
        [key] + all_queries,
        flops=2 * tokens * asked * (2 * lat_w + TAIL),
        nbytes=2 * tokens * lat_w,
    )
    parts = call(
        functools.partial(both_kernel, scale),
        tuple(jax.ShapeDtypeStruct((lat_w + INFO, queries), bf16) for _ in range(NX)),
        [other, own_part, own_stat] + all_queries,
        flops=2 * tokens * asked * (2 * lat_w + TAIL),
        nbytes=2 * tokens * lat_w,
    )
    parts = [shift_y(part, n_head, -k) for k, part in enumerate(parts)]
    head_out = call(
        functools.partial(merge_kernel, rows_dev),
        jax.ShapeDtypeStruct((NZ, width, heads * value_w), bf16),
        [fresh_part, fresh_lse, w_uv] + parts,
        scratch=[pltpu.VMEM((queries, lat_w), f32)],
        flops=2 * queries * lat_w * value_w,
        nbytes=2 * heads * lat_w * value_w,
    )

    rings = [[a * NZ + b for b in range(NZ)] for a in range(NX)]
    ring = lax.all_to_all(
        head_out, "row", split_axis=0, concat_axis=0, axis_index_groups=rings, tiled=True
    )
    cols = w_o.shape[1]
    cores = n_head // NX
    w_ring = call(
        stage_kernel,
        jax.ShapeDtypeStruct((3,) + w_t.shape, bf16),
        [w_t, w_near, w_far],
        scratch=[pltpu.SemaphoreType.DMA((3,))],
        nbytes=12 * w_o.size,
        in_hbm=(0, 1, 2),
    )
    sums = call(
        functools.partial(project_kernel, width),
        jax.ShapeDtypeStruct((NZ * NX, width, cols), bf16),
        [ring.reshape(NZ * width, heads * value_w), w_ring, w_opposite],
        scratch=[pltpu.VMEM(w_t.shape, bf16), pltpu.SemaphoreType.DMA((1,))],
        flops=2 * NX * NZ * width * w_o.size,
        nbytes=2 * NX * w_o.size,
        in_hbm=(2,),
    )
    planes = [
        [(x * NZ + z) * n_head + y * cores + core for z in range(NZ) for y in range(NX)]
        for x in range(NX)
        for core in range(cores)
    ]
    sums = lax.all_to_all(
        sums,
        ("row", "head"),
        split_axis=0,
        concat_axis=0,
        axis_index_groups=planes,
        tiled=True,
    )
    half = jax.ShapeDtypeStruct((NZ // cores, width, cols), f32)
    keep, give = call(sum_kernel, (half, half), [sums])
    taken = lax.ppermute(give, "head", [(h, h ^ 1) for h in range(n_head)])
    return call(
        final_kernel,
        jax.ShapeDtypeStruct((steps, rows_dev, NZ // cores * cols), bf16),
        [keep, taken],
    )


def solution(mesh):
    placed = (
        P(None, "row", "head", None),
        P(None, "row", "head"),
        P(None, "row", None),
        P(None, "row", None),
        P("row", None, None),
        P("row", None),
        P("row"),
        P("row"),
        P("row", None),
        P("row"),
        P("head", None, None),
        P("head", None, None),
        P("head", "row"),
    )
    return jax.shard_map(
        on_device, mesh=mesh, in_specs=placed, out_specs=P(None, "row", "head"), check_vma=False
    )
```

```python
import functools

import jax
import jax.numpy as jnp
from jax import lax
from jax.experimental import pallas as pl
from jax.experimental.pallas import tpu as pltpu
from jax.sharding import PartitionSpec as P

NX = 4
NZ = 8
TAIL = 128
INFO = 16
NEG = -1e30
LOG2E = 1.4426950408889634
LN2 = 0.6931471805599453

VMEM = pl.BlockSpec(memory_space=pltpu.VMEM)
SMEM = pl.BlockSpec(memory_space=pltpu.SMEM)
HBM = pl.BlockSpec(memory_space=pltpu.HBM)


def call(
    body, out_shape, ins, scratch=(), flops=0, nbytes=0, mem=24, out_spec=VMEM, in_hbm=()
):
    return pl.pallas_call(
        body,
        out_shape=out_shape,
        in_specs=[
            HBM if i in in_hbm else SMEM if a.dtype == jnp.int32 and a.ndim == 1 else VMEM
            for i, a in enumerate(ins)
        ],
        out_specs=out_spec
        if isinstance(out_spec, tuple)
        else jax.tree.map(lambda _: out_spec, out_shape),
        scratch_shapes=list(scratch),
        compiler_params=pltpu.CompilerParams(vmem_limit_bytes=mem * 2**20),
        cost_estimate=pl.CostEstimate(flops=flops, bytes_accessed=nbytes, transcendentals=0),
    )(*ins)


def dot(a, b):
    return lax.dot_general(a, b, (((1,), (0,)), ((), ())), preferred_element_type=jnp.float32)


def dot_t(a, b):
    return lax.dot_general(a, b, (((1,), (1,)), ((), ())), preferred_element_type=jnp.float32)


def iota(shape, dim):
    return lax.broadcasted_iota(jnp.int32, shape, dim)


def ones_where(mask):
    return jnp.where(mask, 1.0, 0.0).astype(jnp.bfloat16)


def pack_kernel(
    rows_dev,
    pages_row,
    per_pair,
    rows_hbm,
    slots_hbm,
    lat_hbm,
    rope_hbm,
    out_hbm,
    rows_ref,
    slots_ref,
    lat_ref,
    lat_buf,
    rope_buf,
    buf_ref,
    in_sem,
    out_sem,
):
    pages, both, lat_w = lat_buf.shape
    piece = both // 2
    count, block, _ = buf_ref.shape
    chunks = out_sem.shape[0]
    cuts = lat_w // TAIL
    rope_rows = rope_buf.shape[1] // TAIL
    lat_rows = per_pair * cuts * piece
    head = lax.axis_index("head")
    lists = [
        pltpu.make_async_copy(rows_hbm, rows_ref, in_sem.at[0]),
        pltpu.make_async_copy(slots_hbm, slots_ref, in_sem.at[1]),
    ]
    for copy in lists:
        copy.start()
    lane0 = pl.multiple_of(head * rope_buf.shape[1], rope_buf.shape[1])
    rope_copy = pltpu.make_async_copy(
        rope_hbm.at[:, pl.ds(lane0, rope_buf.shape[1])], rope_buf, in_sem.at[2]
    )
    rope_copy.start()
    first = pl.multiple_of(head // 2 * both, both)
    cut = pages // chunks
    lat_copies = []
    for i in range(chunks):
        here = pl.ds(i * cut, cut)
        copy = pltpu.make_async_copy(
            lat_hbm.at[here, pl.ds(first, both), :], lat_buf.at[here], in_sem.at[3 + i]
        )
        copy.start()
        lat_copies.append(copy)
    for copy in lists:
        copy.wait()

    dest = rows_ref[...] // rows_dev
    label = (rows_ref[...] % rows_dev * pages_row + slots_ref[...] + 1).astype(jnp.float32)
    owned = jnp.where(iota((count, pages), 0) == dest, 1.0, 0.0)
    before = ones_where(iota((pages, pages), 0) < iota((pages, pages), 1))
    rank = jnp.sum(owned * dot(owned.astype(jnp.bfloat16), before), axis=0, keepdims=True)
    rank = rank.astype(jnp.int32)
    at_slot = (dest * per_pair + rank).astype(jnp.float32).astype(jnp.bfloat16)
    spread = ones_where(iota((pages, pages * piece), 0) == iota((pages, pages * piece), 1) // piece)
    at_slot = dot(jnp.broadcast_to(at_slot, (8, pages)), spread)[:1].astype(jnp.int32)
    place = at_slot * piece + iota((1, pages * piece), 1) % piece

    label_lane = iota((TAIL, pages), 0)
    named = ones_where((label_lane // piece == rank) & (label_lane < per_pair * piece))
    labels = dot_t((owned * label).astype(jnp.bfloat16), named).astype(jnp.bfloat16)
    rest = block - lat_rows
    row = iota((count * rest, 1), 0)
    tail = dot(
        ones_where(row == iota((1, count), 1) * rest + per_pair * rope_rows), labels
    )
    rope_copy.wait()
    for j in range(rope_rows):
        pick = ones_where(row == dest * rest + rank * rope_rows + j)
        tail = tail + dot(pick, rope_buf[:, j * TAIL : (j + 1) * TAIL])
    buf_ref[:, lat_rows:, :] = tail.reshape(count, rest, TAIL).astype(jnp.bfloat16)

    for i, copy in enumerate(lat_copies):
        copy.wait()
        lat = lat_buf[i * cut : (i + 1) * cut].astype(jnp.float32).reshape(cut, 2, piece, lat_w)
        lat = jnp.where(head % 2 == 1, lat[:, 1], lat[:, 0]).reshape(cut * piece, lat_w)
        lat_ref[i * cut * piece : (i + 1) * cut * piece, :] = lat.astype(jnp.bfloat16)
    lat = lat_ref[...]
    step = count // chunks
    copies = []
    for i in range(chunks):
        rows = step * per_pair * piece
        value = dot(ones_where(iota((rows, 1), 0) + i * rows == place), lat)
        value = [
            value[:, c * TAIL : (c + 1) * TAIL].reshape(step * per_pair, 1, piece, TAIL)
            for c in range(cuts)
        ]
        value = jnp.concatenate(value, axis=1).reshape(step, lat_rows, TAIL)
        here = pl.ds(i * step, step)
        buf_ref[here, :lat_rows, :] = value.astype(jnp.bfloat16)
        copy = pltpu.make_async_copy(buf_ref.at[here], out_hbm.at[here], out_sem.at[i])
        copy.start()
        copies.append(copy)
    for copy in copies:
        copy.wait()


def split3(x):
    hi = x.astype(jnp.bfloat16)
    rest = x - hi.astype(jnp.float32)
    mid = rest.astype(jnp.bfloat16)
    low = (rest - mid.astype(jnp.float32)).astype(jnp.bfloat16)
    return hi.astype(jnp.float32), mid.astype(jnp.float32), low.astype(jnp.float32)


def query_kernel(
    scale, rows, qn_ref, qtail_ref, w_ref, fresh_ref, fresh_t_ref, q_ref, swap_ref, part_ref, lse_ref, acc_ref
):
    heads, width, _ = qn_ref.shape
    lat_w = w_ref.shape[2]
    steps = width // rows
    for head in range(heads):
        absorbed = dot(qn_ref[head], w_ref[head])
        for row in range(rows):
            at = (row * heads + head) * steps
            acc_ref[at : at + steps, :] = absorbed[row * steps : (row + 1) * steps]
    half = rows * heads * steps // 2
    absorbed = acc_ref[...].T
    tail = qtail_ref[...].astype(jnp.float32).T
    q_ref[:lat_w, :] = absorbed.astype(jnp.bfloat16)
    q_ref[lat_w:, :] = tail.astype(jnp.bfloat16)
    swap_ref[:lat_w, :] = pltpu.roll(absorbed, half, 1).astype(jnp.bfloat16)
    swap_ref[lat_w:, :] = pltpu.roll(tail, half, 1).astype(jnp.bfloat16)
    scores = dot(fresh_ref[...], q_ref[...]) * scale
    shape = scores.shape
    token = iota(shape, 0)
    query = iota(shape, 1)
    allowed = (query // (heads * steps) == token % rows) & (token // rows <= query % steps)
    scores = jnp.where(allowed, scores, NEG)
    high = jnp.max(scores, axis=0, keepdims=True)
    weights = jnp.exp(scores - high)
    total = jnp.sum(weights, axis=0, keepdims=True)
    part_ref[...] = dot(fresh_t_ref[...], weights.astype(jnp.bfloat16)) * (1.0 / total)
    lse_ref[...] = jnp.broadcast_to(high + jnp.log(total), lse_ref.shape)


def gather_kernel(
    piece,
    per_pair,
    rope_w,
    pages_row,
    block_ref,
    bias_ref,
    key_hbm,
    key_ref,
    out_sem,
):
    rows, per_row, key_w = key_ref.shape
    count, block, _ = block_ref.shape
    cuts = (key_w - TAIL) // TAIL
    lat_w = cuts * TAIL
    pair_tokens = per_pair * piece
    lat_rows = pair_tokens * cuts
    rest = block - lat_rows
    rope_rows = piece * rope_w // TAIL
    half = per_row // 2

    def spread_over(columns, group, lane):
        own = iota((count, columns), 0) == iota((1, columns), 1) // group
        return ones_where(iota((TAIL, columns), 0) == lane), jnp.where(own, 1.0, 0.0)

    lat_columns = count * pair_tokens
    lat_inner = iota((1, lat_columns), 1) % pair_tokens
    lat_spread = spread_over(lat_columns, pair_tokens, lat_inner)
    rope_columns = count * rest
    rope_inner = iota((1, rope_columns), 1) % rest
    lane = jnp.where(rope_inner < per_pair * rope_rows, rope_inner // rope_rows * piece, TAIL)
    rope_spread = spread_over(rope_columns, rest, lane)

    tail = block_ref[:, lat_rows:, :].astype(jnp.float32)
    marked = iota(tail.shape, 1) == per_pair * rope_rows
    labels = jnp.sum(jnp.where(marked, tail, 0.0), axis=1).astype(jnp.bfloat16)
    tail = tail.reshape(rope_columns, TAIL).astype(jnp.bfloat16)
    lat = block_ref[:, :lat_rows, :].astype(jnp.float32)
    lat = lat.reshape(count * per_pair, cuts, piece, TAIL)
    lat = [lat[:, c].reshape(lat_columns, TAIL).astype(jnp.bfloat16) for c in range(cuts)]
    lat = jnp.concatenate(lat, axis=1)
    bias_all = bias_ref[...].T

    def slot_of(spread, own):
        wide = dot(labels, spread) * own
        return jnp.sum(wide, axis=0, keepdims=True).astype(jnp.int32) - 1

    slot = slot_of(*lat_spread)
    token = lat_inner % piece
    row = (slot >= pages_row).astype(jnp.int32)
    target = row * (per_row - pages_row * (piece // 2)) + token % 2 * half
    target = target + slot * (piece // 2) + token // 2
    target = jnp.where(slot >= 0, target, -1)
    slot = slot_of(*rope_spread)
    rope_target = jnp.where(slot >= 0, slot * rope_rows + rope_inner % rope_rows, -1)
    copies = []
    for b in range(rows):
        pick = ones_where(iota((half, 1), 0) + b * half == rope_target)
        rope_b = dot(pick, tail)
        rope_b = jnp.concatenate([rope_b, pltpu.roll(rope_b, TAIL - rope_w, 1)], axis=0)
        lane = iota(rope_b.shape, 1)
        bias = bias_all[b * per_row : (b + 1) * per_row, :1]
        rope_b = jnp.where(lane < rope_w, rope_b, jnp.where(lane == rope_w, bias, 0.0))
        key_ref[b, :, lat_w:] = rope_b.astype(jnp.bfloat16)
        pick = ones_where(iota((per_row, 1), 0) + b * per_row == target)
        key_ref[b, :, :lat_w] = dot(pick, lat).astype(jnp.bfloat16)
        copy = pltpu.make_async_copy(key_ref.at[b], key_hbm.at[b], out_sem.at[b])
        copy.start()
        copies.append(copy)
    for copy in copies:
        copy.wait()


def attend(scale, key, query, lat_w):
    scores = dot(key, query)
    high = jnp.max(scores, axis=0, keepdims=True)
    weights = jnp.exp2((scores - high) * (scale * LOG2E))
    total = jnp.sum(weights, axis=0, keepdims=True)
    return high, total, dot(key[:, :lat_w].T, weights.astype(jnp.bfloat16))


def ask(q_refs, b):
    left = iota(q_refs[0].shape, 1) < q_refs[0].shape[1] // 2
    tiles = []
    for k in range(0, len(q_refs), 2):
        one, two = q_refs[k][...].astype(jnp.float32), q_refs[k + 1][...].astype(jnp.float32)
        first, second = (one, two) if b == 0 else (two, one)
        tiles.append(jnp.where(left, first, second).astype(jnp.bfloat16))
    return jnp.concatenate(tiles, axis=1)


def own_kernel(scale, key_ref, *refs):
    q_refs, (part_ref, stat_ref) = refs[:-2], refs[-2:]
    for b in range(key_ref.shape[0]):
        high, total, part = attend(scale, key_ref[b], ask(q_refs, b), part_ref.shape[1])
        part_ref[b] = part
        stat_ref[b] = jnp.where(iota(stat_ref.shape[1:], 0) == 0, high, total)


def both_kernel(scale, key_ref, own_ref, stat_ref, *refs):
    count = len(refs) // 2
    q_refs, out_refs = refs[:count], refs[count:]
    lat_w = own_ref.shape[1]
    queries = q_refs[0].shape[1]
    parts = []
    for b in range(key_ref.shape[0]):
        high, total, part = attend(scale, key_ref[b], ask(q_refs, b), lat_w)
        high_own, total_own = stat_ref[b, 0:1], stat_ref[b, 1:2]
        top = jnp.maximum(high, high_own)
        keep = jnp.exp2((high - top) * (scale * LOG2E))
        keep_own = jnp.exp2((high_own - top) * (scale * LOG2E))
        total = total * keep + total_own * keep_own
        inverse = 1.0 / total
        part = part * (keep * inverse) + own_ref[b] * (keep_own * inverse)
        hi, mid, low = split3(top * scale + jnp.log(total))
        mark = iota((INFO, part.shape[1]), 0)
        info = jnp.where(mark == 0, hi, jnp.where(mark == 1, mid, jnp.where(mark == 2, low, 0.0)))
        parts.append(jnp.concatenate([part, info], axis=0))
    left = iota((lat_w + INFO, queries), 1) < queries // 2
    for k in range(0, count, 2):
        lanes = slice(k * queries // 2, (k + 2) * queries // 2)
        one, two = parts[0][:, lanes], parts[1][:, lanes]
        out_refs[k][...] = jnp.where(left, one, two).astype(jnp.bfloat16)
        out_refs[k + 1][...] = jnp.where(left, two, one).astype(jnp.bfloat16)


def merge_kernel(rows_dev, fresh_ref, fresh_lse_ref, w_ref, *refs):
    part_refs, out_ref, lat_ref = refs[:-2], refs[-2], refs[-1]
    heads, lat_w, value_w = w_ref.shape
    width = out_ref.shape[1]
    steps = width // rows_dev
    half = fresh_ref.shape[1] // 2
    lses = [fresh_lse_ref[...]]
    for k, part_ref in enumerate(part_refs):
        info = jnp.sum(part_ref[lat_w:, :].astype(jnp.float32), axis=0, keepdims=True)
        info = jnp.broadcast_to(info, lses[0].shape)
        lses.append(pltpu.roll(info, half, 1) if k % 2 else info)
    high = functools.reduce(jnp.maximum, lses)
    shares = [jnp.exp(lse - high) for lse in lses]
    inverse = 1.0 / functools.reduce(jnp.add, shares)
    total = fresh_ref[...] * (shares[0] * inverse)[:1]
    swapped = 0.0
    for k, part_ref in enumerate(part_refs):
        share = shares[k + 1] * inverse
        part = part_ref[:lat_w, :].astype(jnp.float32)
        if k % 2:
            swapped = swapped + part * pltpu.roll(share, half, 1)[:1]
        else:
            total = total + part * share[:1]
    total = total + pltpu.roll(swapped, half, 1)
    shape = (heads * width, heads * width)
    to, at = iota(shape, 0), iota(shape, 1)
    wanted = (to % rows_dev * heads + to // width) * steps + to % width // rows_dev
    lat_ref[...] = dot_t(ones_where(at == wanted), total.astype(jnp.bfloat16))
    for head in range(heads):
        rows = lat_ref[head * width : (head + 1) * width, :].astype(jnp.bfloat16)
        value = dot(rows, w_ref[head]).astype(jnp.bfloat16)
        for copy in range(out_ref.shape[0]):
            out_ref[copy, :, head * value_w : (head + 1) * value_w] = value


def stage_kernel(own_hbm, near_hbm, far_hbm, out_ref, sem_ref):
    copies = [
        pltpu.make_async_copy(ref, out_ref.at[i], sem_ref.at[i])
        for i, ref in enumerate((own_hbm, near_hbm, far_hbm))
    ]
    for copy in copies:
        copy.start()
    for copy in copies:
        copy.wait()


def project_kernel(width, x_ref, w_ref, opp_a_hbm, opp_b_hbm, out_ref, opp_ref, sem_ref):
    size = opp_a_hbm.shape[0]
    copies = [
        pltpu.make_async_copy(opp_a_hbm, opp_ref.at[pl.ds(0, size)], sem_ref.at[0]),
        pltpu.make_async_copy(opp_b_hbm, opp_ref.at[pl.ds(size, size)], sem_ref.at[1]),
    ]
    for copy in copies:
        copy.start()
    here = lax.axis_index("row") // NZ

    def put(k, block):
        owner = (here + k) % NX
        for z in range(NZ):
            rows = block[z * width : (z + 1) * width]
            out_ref[z * NX + owner] = rows.astype(out_ref.dtype)

    for i, k in enumerate((0, NX - 1, 1)):
        put(k, dot_t(x_ref[...], w_ref[i]))
    for copy in copies:
        copy.wait()
    put(2, dot_t(x_ref[...], opp_ref[...]))


def sum_kernel(in_ref, keep_ref, send_ref):
    core = lax.axis_index("head") % 2
    per_core = keep_ref.shape[0]
    for i in range(per_core):
        for ref, half in ((keep_ref, core), (send_ref, 1 - core)):
            first = (half * per_core + i) * NX
            parts = [in_ref[first + y].astype(jnp.float32) for y in range(NX)]
            ref[i] = functools.reduce(jnp.add, parts)


def final_kernel(keep_ref, got_ref, out_ref):
    value = [keep_ref[i] + got_ref[i] for i in range(keep_ref.shape[0])]
    value = jnp.concatenate(value, axis=1)
    rows = out_ref.shape[1]
    for step in range(out_ref.shape[0]):
        out_ref[step] = value[step * rows : (step + 1) * rows].astype(out_ref.dtype)


def shift_y(x, n_head, k):
    cores = n_head // NX
    if k % NX == 0:
        return x
    return lax.ppermute(x, "head", [(h, (h + k * cores) % n_head) for h in range(n_head)])


def shift_x(x, k):
    return lax.ppermute(
        x,
        "row",
        [(a * NZ + b, (a + k) % NX * NZ + b) for a in range(NX) for b in range(NZ)],
    )


def on_device(
    q_nope,
    q_rope,
    new_latent,
    new_rope,
    latent_pages,
    rope_pages,
    dest_rows,
    dest_slots,
    page_table,
    lengths,
    w_uk,
    w_uv,
    w_o,
):
    bf16, f32 = jnp.bfloat16, jnp.float32
    n_row = lax.axis_size("row")
    n_head = lax.axis_size("head")
    row, head = lax.axis_index("row"), lax.axis_index("head")
    rows_dev, pages_row = page_table.shape
    pages, page_len, lat_w = latent_pages.shape
    rope_w = new_rope.shape[-1]
    steps, _, heads, nope_w = q_nope.shape
    value_w = w_uv.shape[-1]
    piece = page_len // n_head
    per_pair = 2 * (pages // n_row) + min(pages % n_row, 1)
    scale = 1.0 / (nope_w + rope_w) ** 0.5
    width = steps * rows_dev
    queries = heads * width
    tokens = pages * piece
    slots = n_row * per_pair * piece

    lat_rows = per_pair * piece * lat_w // TAIL
    rope_rows = per_pair * piece * rope_w // TAIL
    block = lat_rows + (rope_rows + 8) // 8 * 8
    send = call(
        functools.partial(pack_kernel, rows_dev, pages_row, per_pair),
        jax.ShapeDtypeStruct((n_row, block, TAIL), bf16),
        [dest_rows[None, :], dest_slots[None, :], latent_pages, rope_pages],
        scratch=[
            pltpu.VMEM((1, pages), jnp.int32),
            pltpu.VMEM((1, pages), jnp.int32),
            pltpu.VMEM((tokens, lat_w), bf16),
            pltpu.VMEM((pages, 2 * piece, lat_w), bf16),
            pltpu.VMEM((pages, piece * rope_w), bf16),
            pltpu.VMEM((n_row, block, TAIL), bf16),
            pltpu.SemaphoreType.DMA((7,)),
            pltpu.SemaphoreType.DMA((4,)),
        ],
        flops=2 * slots * tokens * lat_w,
        nbytes=2 * (slots + 2 * tokens) * lat_w,
        mem=60,
        out_spec=HBM,
        in_hbm=(0, 1, 2, 3),
    )
    got = lax.all_to_all(send, "row", split_axis=0, concat_axis=0, tiled=True)

    qn = jnp.transpose(q_nope, (2, 1, 0, 3)).reshape(heads, width, nope_w)
    qr = q_rope.reshape(steps, rows_dev, heads, rope_w)
    qr = jnp.transpose(qr, (1, 2, 0, 3)).reshape(queries, rope_w)
    one_lane = jnp.arange(TAIL - rope_w, dtype=jnp.int32)[None, :] == 0
    q_tail = jnp.concatenate(
        [qr, jnp.broadcast_to(one_lane, (queries, TAIL - rope_w)).astype(bf16)], axis=1
    )
    fresh = jnp.concatenate(
        [
            new_latent.reshape(width, lat_w),
            new_rope.reshape(width, rope_w),
            jnp.zeros((width, TAIL - rope_w), bf16),
        ],
        axis=1,
    )
    fresh = jnp.concatenate([fresh, jnp.zeros((-width % 16, lat_w + TAIL), bf16)], axis=0)
    query, swapped, fresh_part, fresh_lse = call(
        functools.partial(query_kernel, scale, rows_dev),
        (
            jax.ShapeDtypeStruct((lat_w + TAIL, queries), bf16),
            jax.ShapeDtypeStruct((lat_w + TAIL, queries), bf16),
            jax.ShapeDtypeStruct((lat_w, queries), f32),
            jax.ShapeDtypeStruct((8, queries), f32),
        ),
        [qn, q_tail, w_uk, fresh, fresh[:, :lat_w].T],
        scratch=[pltpu.VMEM((queries, lat_w), f32)],
        flops=2 * queries * nope_w * lat_w,
        nbytes=2 * heads * nope_w * lat_w,
    )
    all_queries = [shift_y((query, swapped)[k % 2], n_head, k) for k in range(NX)]

    w_t = w_o.T
    w_near, w_far = shift_x(w_t, 1), shift_x(w_t, -1)

    slot_ids = jnp.arange(pages_row, dtype=jnp.int32)
    holds = (page_table[:, :, None] == slot_ids[None, None, :]).astype(jnp.int32)
    logical = jnp.sum(holds * slot_ids[None, :, None], axis=1)
    limit = lengths[:, None] - logical * page_len - head * piece
    within = jnp.arange(piece, dtype=jnp.int32).reshape(piece // 2, 2).T
    usable = within[None, :, None, :] < limit[:, None, :, None]
    bias = jnp.where(usable, 0.0, NEG).astype(f32).reshape(1, rows_dev * pages_row * piece)
    bias = jnp.broadcast_to(bias, (8, bias.shape[1]))

    got, w_near, w_far, all_queries = lax.optimization_barrier((got, w_near, w_far, all_queries))
    key = call(
        functools.partial(gather_kernel, piece, per_pair, rope_w, pages_row),
        jax.ShapeDtypeStruct((rows_dev, pages_row * piece, lat_w + TAIL), bf16),
        [got, bias],
        scratch=[
            pltpu.VMEM((rows_dev, pages_row * piece, lat_w + TAIL), bf16),
            pltpu.SemaphoreType.DMA((rows_dev,)),
        ],
        flops=2 * slots * tokens * lat_w,
        nbytes=2 * slots * lat_w,
        out_spec=HBM,
    )
    other = lax.ppermute(key, "head", [(h, h ^ 1) for h in range(n_head)])
    asked = NX * queries // rows_dev
    own_part, own_stat = call(
        functools.partial(own_kernel, scale),
        (
            jax.ShapeDtypeStruct((rows_dev, lat_w, asked), f32),
            jax.ShapeDtypeStruct((rows_dev, 8, asked), f32),
        ),
        [key] + all_queries,
        flops=2 * tokens * asked * (2 * lat_w + TAIL),
        nbytes=2 * tokens * lat_w,
    )
    size = w_t.shape[0] // 2
    opposite = [shift_x(w_near[:size], 1), shift_x(w_far[size:], -1)]
    parts = call(
        functools.partial(both_kernel, scale),
        tuple(jax.ShapeDtypeStruct((lat_w + INFO, queries), bf16) for _ in range(NX)),
        [other, own_part, own_stat] + all_queries,
        flops=2 * tokens * asked * (2 * lat_w + TAIL),
        nbytes=2 * tokens * lat_w,
    )
    parts = [shift_y(part, n_head, -k) for k, part in enumerate(parts)]
    head_out = call(
        functools.partial(merge_kernel, rows_dev),
        jax.ShapeDtypeStruct((NZ, width, heads * value_w), bf16),
        [fresh_part, fresh_lse, w_uv] + parts,
        scratch=[pltpu.VMEM((queries, lat_w), f32)],
        flops=2 * queries * lat_w * value_w,
        nbytes=2 * heads * lat_w * value_w,
    )

    rings = [[a * NZ + b for b in range(NZ)] for a in range(NX)]
    ring = lax.all_to_all(
        head_out, "row", split_axis=0, concat_axis=0, axis_index_groups=rings, tiled=True
    )
    cols = w_o.shape[1]
    cores = n_head // NX
    w_ring = call(
        stage_kernel,
        jax.ShapeDtypeStruct((3,) + w_t.shape, bf16),
        [w_t, w_near, w_far],
        scratch=[pltpu.SemaphoreType.DMA((3,))],
        nbytes=12 * w_o.size,
        in_hbm=(0, 1, 2),
    )
    sums = call(
        functools.partial(project_kernel, width),
        jax.ShapeDtypeStruct((NZ * NX, width, cols), bf16),
        [ring.reshape(NZ * width, heads * value_w), w_ring] + opposite,
        scratch=[pltpu.VMEM(w_t.shape, bf16), pltpu.SemaphoreType.DMA((2,))],
        flops=2 * NX * NZ * width * w_o.size,
        nbytes=2 * NX * w_o.size,
        in_hbm=(2, 3),
    )
    planes = [
        [(x * NZ + z) * n_head + y * cores + core for z in range(NZ) for y in range(NX)]
        for x in range(NX)
        for core in range(cores)
    ]
    sums = lax.all_to_all(
        sums,
        ("row", "head"),
        split_axis=0,
        concat_axis=0,
        axis_index_groups=planes,
        tiled=True,
    )
    half = jax.ShapeDtypeStruct((NZ // cores, width, cols), f32)
    keep, give = call(sum_kernel, (half, half), [sums])
    taken = lax.ppermute(give, "head", [(h, h ^ 1) for h in range(n_head)])
    return call(
        final_kernel,
        jax.ShapeDtypeStruct((steps, rows_dev, NZ // cores * cols), bf16),
        [keep, taken],
    )


def solution(mesh):
    placed = (
        P(None, "row", "head", None),
        P(None, "row", "head"),
        P(None, "row", None),
        P(None, "row", None),
        P("row", None, None),
        P("row", None),
        P("row"),
        P("row"),
        P("row", None),
        P("row"),
        P("head", None, None),
        P("head", None, None),
        P("head", "row"),
    )
    return jax.shard_map(
        on_device, mesh=mesh, in_specs=placed, out_specs=P(None, "row", "head"), check_vma=False
    )
```
